32 devices in a mesh: dp: 8 (over z, y), row: 2 (over x), col: 2 (over core).
Axes of the slice: x: 2, y: 2, z: 4, core: 2. Of those that a mesh axis runs over, the one named last changes fastest.
Arguments:
- block_in: bfloat16 [12288, 1600], P(('dp', 'col'), 'row'), may hold values from -6 to 6
- out_grad: bfloat16 [12288, 1600], P(('dp', 'col'), 'row'), may hold values from -6 to 6
- seq_lengths: int32 [8, 5], P('dp'), may hold values from 1 to 768, 1536 in all within a row
- ln1_gain: bfloat16 [1600], P('row'), may hold values from 0.5 to 1.5
- ln1_bias: bfloat16 [1600], P('row'), may hold values from -3 to 3
- qkv_weight: bfloat16 [3, 1600, 1600], P(None, 'row', 'col'), may hold values from -1 to 1
- qv_bias: bfloat16 [2, 1600], P(None, 'col'), may hold values from -3 to 3
- out_weight: bfloat16 [1600, 1600], P('col', 'row'), may hold values from -1.25 to 1.25
- out_bias: bfloat16 [1600], P('row'), may hold values from -3 to 3
- ln2_gain: bfloat16 [1600], P('row'), may hold values from 0.5 to 1.5
- ln2_bias: bfloat16 [1600], P('row'), may hold values from -3 to 3
- fc_weight: bfloat16 [1600, 6400], P('row', 'col'), may hold values from -1 to 1
- fc_bias: bfloat16 [6400], P('col'), may hold values from -3 to 3
- proj_weight: bfloat16 [6400, 1600], P('col', 'row'), may hold values from -0.078125 to 0.078125
- proj_bias: bfloat16 [1600], P('row'), may hold values from -3 to 3
Outputs:
- block_out: bfloat16 [12288, 1600], P(('dp', 'col'), 'row')
- x_grad: float32 [12288, 1600], P(('dp', 'col'), 'row')
- ln1_gain_grad: float32 [1600], P('row')
- ln1_bias_grad: float32 [1600], P('row')
- qkv_weight_grad: float32 [3, 1600, 1600], P(None, 'row', 'col')
- qv_bias_grad: float32 [2, 1600], P(None, 'col')
- out_weight_grad: float32 [1600, 1600], P('col', 'row')
- out_bias_grad: float32 [1600], P('row')
- ln2_gain_grad: float32 [1600], P('row')
- ln2_bias_grad: float32 [1600], P('row')
- fc_weight_grad: float32 [1600, 6400], P('row', 'col')
- fc_bias_grad: float32 [6400], P('col')
- proj_weight_grad: float32 [6400, 1600], P('col', 'row')
- proj_bias_grad: float32 [1600], P('row')
The draws below stay inside these ranges and needn't reach their ends.
Inputs may be any that keep to these rules, and one draw needn't show every extreme that they name: `seq_lengths`: row g gives the lengths of the 5 sequences of data shard g, in the order in which their tokens lie among that shard's 1536 tokens; each row sums to 1536, and the longest sequence of each row has exactly 768 tokens.
All inputs are finite; a program needn't handle non-finite values.
Results may differ from the reference program's by a relative error of at most 0.015.
Values may be sent and summed in bfloat16 or wider, within the bound.
No kernel may reach another device: no remote copies, remote signals or barrier semaphores. Data moves between devices by JAX's collectives and lax.ppermute only.
A program may use at most 256 MiB of HBM per device.

```python
import math
import jax
import jax.numpy as jnp
import numpy as np
from jax import lax

D = 1600
HEADS = 25
HEAD_DIM = 64
FF = 6400
TOK_DEV = 384
TOK_GRP = 1536
TOKENS = 12288
MAXLEN = 768
REACH = 2
SEQS = 5
N_DP = 8
N_ROW = 2
N_COL = 2


def draw_qkv_weight(key, part):
    key = jax.random.fold_in(key, 11)
    noise_key, common_key = jax.random.split(key)
    noise = jax.random.truncated_normal(noise_key, -3.0, 3.0, (3, D, D), jnp.float32)
    common = jax.random.truncated_normal(common_key, -3.0, 3.0, (3, 1, D), jnp.float32)
    return ((noise + 0.5 * common) * D ** (-0.5)).astype(jnp.bfloat16)


def draw_fc_weight(key, part):
    key = jax.random.fold_in(key, 12)
    noise_key, common_key = jax.random.split(key)
    noise = jax.random.truncated_normal(noise_key, -3.0, 3.0, (D, FF), jnp.float32)
    common = jax.random.truncated_normal(common_key, -3.0, 3.0, (1, FF), jnp.float32)
    return ((noise + 0.5 * common) * D ** (-0.5)).astype(jnp.bfloat16)


def block_scale(rng, extent, shards, smallest, high):
    gain = 1.0
    for axis_at, parts in shards:
        steps = jax.random.uniform(jax.random.fold_in(jax.random.fold_in(rng, 6), axis_at), (parts,), jnp.float32, smallest / len(shards), high / len(shards))
        gain = gain * jnp.repeat(jnp.exp(steps), extent[axis_at] // parts).reshape((-1,) + (1,) * (len(extent) - 1 - axis_at))
    return gain


def profile(amount, total, bound, slope):
    weights = [(1 << 20) // math.isqrt(rank ** slope) + 1 for rank in range(2, amount + 1)]
    rest, counts = total - bound - (amount - 1), [1] * (amount - 1)
    while rest > 0:
        movable = [i for i in range(amount - 1) if counts[i] < bound]
        whole, left = sum([weights[i] for i in movable]), rest
        for i in movable:
            extra = min(bound - counts[i], max(1, left * weights[i] // whole), rest)
            counts[i] = counts[i] + extra
            rest = rest - extra
    return np.array([bound] + counts)


def ragged(own_key, number_of, total, most, lean):
    if number_of == 2:
        one = jax.random.randint(own_key, (), max(1, total - most), min(most, total - 1) + 1)
        return jnp.stack([one, total - one])
    lengths = jnp.asarray(profile(number_of, total, most, lean), jnp.int32)
    pairs = (number_of - 1) // 2
    source_of, sink = lengths[1:1 + 2 * pairs:2], lengths[2:2 + 2 * pairs:2]
    margin = jnp.minimum(source_of - 1, most - sink)
    passed = jax.random.randint(jax.random.fold_in(own_key, 1), (pairs,), 0, 1 << 20) % (margin + 1)
    lengths = lengths.at[1:1 + 2 * pairs:2].set(source_of - passed).at[2:2 + 2 * pairs:2].set(sink + passed)
    return lengths[jax.random.permutation(jax.random.fold_in(own_key, 2), number_of)]


def gaussian(stream_key, extent, scale, reach, cuts=(), kind=jnp.bfloat16):
    result = scale * jax.random.normal(stream_key, extent, jnp.float32)
    if cuts:
        result = result * block_scale(stream_key, extent, cuts, -0.22, 0.18)
    return jnp.clip(result, -reach, reach).astype(kind)


def setup_inputs(seed: int = 0) -> dict:
    streams_of = jax.random.split(jax.random.key(seed), 16)
    block_in = gaussian(streams_of[0], (TOKENS, D), 1.0, 6.0, ((0, 16), (1, 2)))
    out_grad = gaussian(streams_of[1], (TOKENS, D), 1.0, 6.0, ((0, 16), (1, 2)))
    seq_lengths = jax.vmap(lambda own: ragged(own, SEQS, TOK_GRP, MAXLEN, 2))(jax.random.split(streams_of[2], N_DP)).reshape((N_DP, SEQS)).astype(jnp.int32)
    ln1_gain = jnp.clip(1.0 + 0.1 * jax.random.normal(streams_of[3], (D,), jnp.float32), 0.5, 1.5).astype(jnp.bfloat16)
    ln1_bias = gaussian(streams_of[4], (D,), 0.5, 3.0, ((0, 2),))
    qkv_weight = draw_qkv_weight(jax.random.fold_in(streams_of[15], 71), 0)
    qv_bias = gaussian(streams_of[6], (2, D), 0.5, 3.0, ((1, 2),))
    out_weight = gaussian(streams_of[7], (D, D), HEADS ** -0.5, 1.25, ((0, 2), (1, 2)))
    out_bias = gaussian(streams_of[8], (D,), 0.5, 3.0, ((0, 2),))
    ln2_gain = jnp.clip(1.0 + 0.1 * jax.random.normal(streams_of[9], (D,), jnp.float32), 0.5, 1.5).astype(jnp.bfloat16)
    ln2_bias = gaussian(streams_of[10], (D,), 0.5, 3.0, ((0, 2),))
    fc_weight = draw_fc_weight(jax.random.fold_in(streams_of[15], 71), 0)
    fc_bias = gaussian(streams_of[12], (FF,), 0.5, 3.0, ((0, 2),))
    proj_weight = gaussian(streams_of[13], (FF, D), FF ** -0.5, 0.078125, ((0, 2), (1, 2)))
    proj_bias = gaussian(streams_of[14], (D,), 0.5, 3.0, ((0, 2),))
    return dict(block_in=block_in, out_grad=out_grad, seq_lengths=seq_lengths, ln1_gain=ln1_gain, ln1_bias=ln1_bias, qkv_weight=qkv_weight, qv_bias=qv_bias, out_weight=out_weight, out_bias=out_bias, ln2_gain=ln2_gain, ln2_bias=ln2_bias, fc_weight=fc_weight, fc_bias=fc_bias, proj_weight=proj_weight, proj_bias=proj_bias)


@jax.custom_vjp
def low(v):
    return lax.optimization_barrier(v.astype(jnp.bfloat16)).astype(jnp.float32)

@jax.custom_vjp
def low_back(v):
    return v

def low_keep(v):
    return (low(v), None)

def low_pass(kept, grad):
    return (grad,)

def back_keep(v):
    return (v, None)

def back_low(kept, grad):
    return (low(grad),)
low.defvjp(low_keep, low_pass)
low_back.defvjp(back_keep, back_low)
gelu_root = math.sqrt(2.0 / math.pi)
gelu_cubic = 0.044715

def gelu_tanh(values):
    return 0.5 * values * (1.0 + jnp.tanh(gelu_root * (values + gelu_cubic * values * values * values)))

def layer_norm(values, norm_gain, norm_bias):
    center = lax.optimization_barrier(jnp.mean(values, axis=-1, keepdims=True))
    spread = lax.optimization_barrier(jnp.mean((values - center) * (values - center), axis=-1, keepdims=True))
    return (values - center) * lax.rsqrt(spread + 1e-05) * norm_gain + norm_bias

def seq_starts(seq_lengths):
    seq_ends = jnp.cumsum(seq_lengths, axis=1, dtype=jnp.int32)
    places = jnp.arange(TOK_GRP, dtype=jnp.int32)
    starts = lax.optimization_barrier(jnp.sum(jnp.where(seq_ends[:, None, :] <= places[None, :, None], seq_lengths[:, None, :], 0), axis=2, dtype=jnp.int32))
    return starts.reshape(TOKENS).astype(jnp.int32)

def attention(projected, starts):
    window = (REACH + 1) * TOK_DEV
    group_blocks = N_ROW * N_COL
    scale = HEAD_DIM ** (-0.5)
    queries_all = projected[:, 0, :]
    padded = jnp.concatenate([jnp.zeros((REACH * TOK_DEV, 2, D), jnp.float32), projected[:, 1:, :]], axis=0)

    def one_block(block_number):
        first_row = block_number * TOK_DEV
        query_rows = lax.dynamic_slice_in_dim(queries_all, first_row, TOK_DEV, 0).reshape(TOK_DEV, HEADS, HEAD_DIM)
        key_values = lax.dynamic_slice_in_dim(padded, first_row, window, 0)
        key_rows = key_values[:, 0, :].reshape(window, HEADS, HEAD_DIM)
        value_rows = key_values[:, 1, :].reshape(window, HEADS, HEAD_DIM)
        local_block = block_number % group_blocks
        places = local_block * TOK_DEV + jnp.arange(TOK_DEV, dtype=jnp.int32)
        key_places = (local_block - REACH) * TOK_DEV + jnp.arange(window, dtype=jnp.int32)
        first_places = lax.dynamic_slice_in_dim(starts, first_row, TOK_DEV, 0)
        allowed = (key_places[None, :] >= first_places[:, None]) & (key_places[None, :] <= places[:, None])
        scores = scale * jnp.einsum('qhe,khe->hqk', query_rows, key_rows, precision=lax.Precision.HIGHEST)
        scores = low_back(jnp.where(allowed[None], scores, -1e+30))
        highest = lax.optimization_barrier(jnp.max(scores, axis=2, keepdims=True))
        weights = jnp.exp(scores - highest)
        probs_low = low(weights / lax.optimization_barrier(jnp.sum(weights, axis=2, keepdims=True)))
        mixed_out = jnp.einsum('hqk,khe->qhe', probs_low, value_rows, precision=lax.Precision.HIGHEST)
        return mixed_out.reshape(TOK_DEV, D)
    blocks = lax.map(jax.checkpoint(one_block), jnp.arange(TOKENS // TOK_DEV, dtype=jnp.int32))
    return blocks.reshape(TOKENS, D)

def reference(block_in, out_grad, seq_lengths, ln1_gain, ln1_bias, qkv_weight, qv_bias, out_weight, out_bias, ln2_gain, ln2_bias, fc_weight, fc_bias, proj_weight, proj_bias):
    starts = seq_starts(seq_lengths)

    def forward(x_float, gain_one, bias_one, qkv_w, qv_b, out_w, out_b, gain_two, bias_two, fc_w, fc_b, proj_w, proj_b):
        h_one = low(layer_norm(x_float, gain_one, bias_one))
        bias_three = jnp.stack([qv_b[0], jnp.zeros_like(qv_b[0]), qv_b[1]])
        projected = jnp.einsum('td,kde->tke', h_one, qkv_w, precision=lax.Precision.HIGHEST) + bias_three[None]
        projected = low_back(low(projected))
        attended = low_back(low(attention(projected, starts)))
        branch = low_back(jnp.dot(attended, out_w, precision=lax.Precision.HIGHEST) + out_b)
        x_mid = x_float + branch
        h_two = low(layer_norm(x_mid, gain_two, bias_two))
        pre_act = low_back(jnp.dot(h_two, fc_w, precision=lax.Precision.HIGHEST) + fc_b)
        activated = low(gelu_tanh(pre_act))
        return x_mid + jnp.dot(activated, proj_w, precision=lax.Precision.HIGHEST) + proj_b
    out_value, pullback = jax.vjp(forward, block_in.astype(jnp.float32), ln1_gain.astype(jnp.float32), ln1_bias.astype(jnp.float32), qkv_weight.astype(jnp.float32), qv_bias.astype(jnp.float32), out_weight.astype(jnp.float32), out_bias.astype(jnp.float32), ln2_gain.astype(jnp.float32), ln2_bias.astype(jnp.float32), fc_weight.astype(jnp.float32), fc_bias.astype(jnp.float32), proj_weight.astype(jnp.float32), proj_bias.astype(jnp.float32))
    gradients = pullback(out_grad.astype(jnp.float32))
    return (out_value.astype(jnp.bfloat16), gradients[0], gradients[1], gradients[2], gradients[3], gradients[4], gradients[5], gradients[6], gradients[7], gradients[8], gradients[9], gradients[10], gradients[11], gradients[12])
```

```python
import functools
import math

import jax
import jax.numpy as jnp
from jax import lax
from jax.experimental import pallas as pl
from jax.experimental.pallas import tpu as pltpu
from jax.sharding import PartitionSpec as P

HEAD_DIM = 64
BLK=256
NEG=-1e30

def nt(a,b):
    return lax.dot_general(a,b,(((1,),(1,)),((),())),preferred_element_type=jnp.float32)
def nn(a,b):
    return lax.dot_general(a,b,(((1,),(0,)),((),())),preferred_element_type=jnp.float32)

def lane_masked(x, h):
    lanes = lax.broadcasted_iota(jnp.int32, x.shape, 1)
    return jnp.where((lanes // HEAD_DIM) == h, x, jnp.zeros_like(x))

def allowed_tile(i, j, first):
    keys = j * BLK + lax.broadcasted_iota(jnp.int32, (BLK, BLK), 0)
    queries = i * BLK + lax.broadcasted_iota(jnp.int32, (BLK, BLK), 1)
    return (keys >= first) & (keys <= queries)

def attend_kernel(heads, blocks, info_ref, q_ref, k_ref, v_ref, first_ref, o_ref, lse_ref, vt_ref):
    pair = pl.program_id(0)
    shift = info_ref[0]
    vt_ref[...] = jnp.transpose(v_ref[...].astype(jnp.float32)).astype(jnp.bfloat16)
    def place(b):
        return pl.multiple_of(lax.rem(b + shift, blocks) * BLK, BLK)
    def one_block(i, members):
        rows = pl.ds(place(i), BLK)
        query = q_ref[rows, :] * jnp.bfloat16(HEAD_DIM ** -0.5)
        queries = [lane_masked(query, h) for h in members]
        first = first_ref[pl.ds(i, 1), :]
        def step(j, carry):
            cols = pl.ds(place(j), BLK)
            keys = k_ref[cols, :]
            ok = allowed_tile(i, j, first)
            out = []
            for h in members:
                top, total, acc = carry[h]
                scores = jnp.where(ok, nt(keys, queries[h]), NEG)
                new_top = jnp.maximum(top, jnp.max(scores, axis=0, keepdims=True))
                probs = jnp.exp(scores - new_top)
                shrink = jnp.exp(top - new_top)
                total = total * shrink + jnp.sum(probs, axis=0, keepdims=True)
                acc = acc * shrink + nn(vt_ref[h * HEAD_DIM:(h + 1) * HEAD_DIM, cols], probs.astype(jnp.bfloat16))
                out.append((new_top, total, acc))
            return tuple(out)
        start = tuple((jnp.full((1, BLK), NEG, jnp.float32), jnp.zeros((1, BLK), jnp.float32),
                       jnp.zeros((HEAD_DIM, BLK), jnp.float32)) for h in members)
        done = lax.fori_loop(info_ref[1 + i], i + 1, step, start)
        parts = []
        for h in range(2):
            if h < len(members):
                top, total, acc = done[h]
                parts.append(acc / total)
                lse_ref[0, h:h + 1, pl.ds(i * BLK, BLK)] = top + jnp.log(total)
            else:
                parts.append(jnp.zeros((HEAD_DIM, BLK), jnp.float32))
                lse_ref[0, h:h + 1, pl.ds(i * BLK, BLK)] = jnp.zeros((1, BLK), jnp.float32)
        o_ref[rows, :] = jnp.transpose(jnp.concatenate(parts, axis=0)).astype(jnp.bfloat16)
    full = heads // 2
    @pl.when(pair < full)
    def _():
        for i in range(blocks):
            one_block(i, (0, 1))
    if heads % 2:
        @pl.when(pair == full)
        def _():
            for i in range(blocks):
                one_block(i, (0,))

def attend(info, proj, first, heads):
    tokens, width = proj.shape[0], proj.shape[1] // 3
    pairs = width // 128
    blocks = tokens // BLK
    spec = lambda at: pl.BlockSpec((tokens, 128), lambda p, s, at=at: (0, at * pairs + p))
    return pl.pallas_call(
        functools.partial(attend_kernel, heads, blocks),
        grid_spec=pltpu.PrefetchScalarGridSpec(
            num_scalar_prefetch=1, grid=(pairs,),
            in_specs=[spec(0), spec(1), spec(2), pl.BlockSpec((blocks, BLK), lambda p, s: (0, 0))],
            out_specs=[pl.BlockSpec((tokens, 128), lambda p, s: (0, p)),
                       pl.BlockSpec((1, 2, tokens), lambda p, s: (p, 0, 0))],
            scratch_shapes=[pltpu.VMEM((128, tokens), jnp.bfloat16)]),
        out_shape=[jax.ShapeDtypeStruct((tokens, width), jnp.bfloat16),
                   jax.ShapeDtypeStruct((pairs, 2, tokens), jnp.float32)],
        compiler_params=pltpu.CompilerParams(vmem_limit_bytes=48 * 2 ** 20),
        cost_estimate=pl.CostEstimate(flops=7 * 12 * 4 * 65536 * 64 * 8, bytes_accessed=8 * tokens * width, transcendentals=0),
        name="attend",
    )(info, proj, proj, proj, first)

def attend_back_kernel(heads, blocks, info_ref, q_ref, k_ref, v_ref, o_ref, g_ref, lse_ref, first_ref,
                       dq_ref, dk_ref, dv_ref, kt_ref, dk_acc, dv_acc):
    pair = pl.program_id(0)
    shift = info_ref[0]
    kt_ref[...] = jnp.transpose(k_ref[...].astype(jnp.float32)).astype(jnp.bfloat16)
    dk_acc[...] = jnp.zeros_like(dk_acc)
    dv_acc[...] = jnp.zeros_like(dv_acc)
    scale = jnp.bfloat16(HEAD_DIM ** -0.5)
    def place(b):
        return pl.multiple_of(lax.rem(b + shift, blocks) * BLK, BLK)
    def one_block(i, members):
        rows = pl.ds(place(i), BLK)
        query = q_ref[rows, :] * scale
        grad = g_ref[rows, :]
        queries = [lane_masked(query, h) for h in members]
        grads = [lane_masked(grad, h) for h in members]
        spread = jnp.transpose(grad.astype(jnp.float32) * o_ref[rows, :].astype(jnp.float32))
        centre = [jnp.sum(spread[h * HEAD_DIM:(h + 1) * HEAD_DIM], axis=0, keepdims=True) for h in members]
        lse = [lse_ref[0, h:h + 1, pl.ds(i * BLK, BLK)] for h in members]
        first = first_ref[pl.ds(i, 1), :]
        def step(j, carry):
            cols = pl.ds(place(j), BLK)
            keys = k_ref[cols, :]
            values = v_ref[cols, :]
            ok = allowed_tile(i, j, first)
            out = []
            dk = dv = None
            for h in members:
                scores = jnp.where(ok, nt(keys, queries[h]), NEG)
                probs = jnp.exp(scores - lse[h])
                prob_grad = nt(values, grads[h])
                score_grad = (probs * (prob_grad - centre[h])).astype(jnp.bfloat16)
                dv_h = nn(probs.astype(jnp.bfloat16), grads[h])
                dk_h = nn(score_grad, queries[h])
                dk, dv = (dk_h, dv_h) if dk is None else (dk + dk_h, dv + dv_h)
                out.append(carry[h] + nn(kt_ref[h * HEAD_DIM:(h + 1) * HEAD_DIM, cols], score_grad))
            dk_acc[cols, :] += dk
            dv_acc[cols, :] += dv
            return tuple(out)
        start = tuple(jnp.zeros((HEAD_DIM, BLK), jnp.float32) for h in members)
        done = list(lax.fori_loop(info_ref[1 + i], i + 1, step, start))
        if len(done) < 2:
            done.append(jnp.zeros((HEAD_DIM, BLK), jnp.float32))
        dq = jnp.transpose(jnp.concatenate(done, axis=0)) * (HEAD_DIM ** -0.5)
        dq_ref[rows, :] = dq.astype(jnp.bfloat16)
    full = heads // 2
    @pl.when(pair < full)
    def _():
        for i in range(blocks):
            one_block(i, (0, 1))
    if heads % 2:
        @pl.when(pair == full)
        def _():
            for i in range(blocks):
                one_block(i, (0,))
    dk_ref[...] = dk_acc[...].astype(jnp.bfloat16)
    dv_ref[...] = dv_acc[...].astype(jnp.bfloat16)

def attend_back(info, proj, att, grad, lse, first, heads):
    tokens, width = att.shape
    pairs = width // 128
    blocks = tokens // BLK
    spec = lambda at: pl.BlockSpec((tokens, 128), lambda p, s, at=at: (0, at * pairs + p))
    out = jax.ShapeDtypeStruct((tokens, width), jnp.bfloat16)
    return pl.pallas_call(
        functools.partial(attend_back_kernel, heads, blocks),
        grid_spec=pltpu.PrefetchScalarGridSpec(
            num_scalar_prefetch=1, grid=(pairs,),
            in_specs=[spec(0), spec(1), spec(2), spec(0), spec(0),
                      pl.BlockSpec((1, 2, tokens), lambda p, s: (p, 0, 0)),
                      pl.BlockSpec((blocks, BLK), lambda p, s: (0, 0))],
            out_specs=[spec(0), spec(0), spec(0)],
            scratch_shapes=[pltpu.VMEM((128, tokens), jnp.bfloat16), pltpu.VMEM((tokens, 128), jnp.float32),
                            pltpu.VMEM((tokens, 128), jnp.float32)]),
        out_shape=[out, out, out],
        compiler_params=pltpu.CompilerParams(vmem_limit_bytes=48 * 2 ** 20),
        cost_estimate=pl.CostEstimate(flops=7 * 12 * 10 * 65536 * 64 * 8, bytes_accessed=16 * tokens * width, transcendentals=0),
        name="attend_back",
    )(info, proj, proj, proj, att, grad, lse, first)


D = 1600
SWAP = ((0, 1), (1, 0))
gelu_root = math.sqrt(2.0 / math.pi)
gelu_cubic = 0.044715
f32 = jnp.float32
bf16 = jnp.bfloat16


def tn(a, b):
    return lax.dot_general(a, b, (((0,), (0,)), ((), ())), preferred_element_type=f32)


def row_swap(value):
    return lax.ppermute(value, "row", SWAP)


def col_swap(value):
    return lax.ppermute(value, "col", SWAP)


def dp_xor(value, mask):
    return lax.ppermute(value, "dp", [(i, i ^ mask) for i in range(lax.axis_size("dp"))])


def ordered(at, first, second, axis):
    return jnp.where(
        at == 0,
        jnp.concatenate([first, second], axis=axis),
        jnp.concatenate([second, first], axis=axis),
    )


def half_of(at, value, axis):
    size = value.shape[axis] // 2
    return jnp.where(
        at == 0,
        lax.slice_in_dim(value, 0, size, axis=axis),
        lax.slice_in_dim(value, size, 2 * size, axis=axis),
    )


def pad_to(value, size, axis):
    widths = [(0, 0)] * value.ndim
    widths[axis] = (0, size - value.shape[axis])
    return jnp.pad(value, widths)


def head_slots(c, value, axis, most, spare):
    cut = lambda low, high: lax.slice_in_dim(value, low, high, axis=axis)
    size = value.shape[axis]
    tail = col_swap(cut(0, spare))
    less = most - HEAD_DIM
    first = jnp.where(c == 0, cut(0, most), pad_to(cut(spare, spare + less), most, axis))
    second = jnp.where(
        c == 0,
        pad_to(jnp.concatenate([cut(most, size), tail], axis=axis), most, axis),
        pad_to(cut(spare + less, size), most, axis),
    )
    return first, second


def from_slots(c, first, second, axis, spare):
    cut = lambda value, low, high: lax.slice_in_dim(value, low, high, axis=axis)
    most = first.shape[axis]
    less = most - HEAD_DIM
    tail = col_swap(cut(second, less - spare, less))
    return jnp.where(
        c == 0,
        jnp.concatenate([first, cut(second, 0, less - spare)], axis=axis),
        jnp.concatenate([tail, cut(first, 0, less), cut(second, 0, less)], axis=axis),
    )


def put(buffer, piece, places):
    start = [jnp.int32(p) for p in places] + [jnp.int32(0)] * (buffer.ndim - len(places))
    return lax.dynamic_update_slice(buffer, piece, start)


def gather_quarters(other, k):
    rows, width = other.shape
    if lax.axis_size("dp") % 4:
        return row_swap(other)
    at = k % 4
    quarters = other.reshape(4, rows // 4, width)
    got = {0: row_swap(lax.dynamic_index_in_dim(quarters, at, 0, keepdims=False))}
    got[2] = dp_xor(got[0], 2)
    got[1] = dp_xor(got[0], 1)
    got[3] = dp_xor(got[2], 1)
    buffer = jnp.zeros_like(quarters)
    for d in range(4):
        buffer = put(buffer, got[d][None], (at ^ d,))
    return buffer.reshape(rows, width)


def scattered(grad, y, z):
    send = lax.dynamic_index_in_dim(grad, 1 - y, 0, keepdims=False)
    keep = lax.dynamic_index_in_dim(grad, y, 0, keepdims=False)
    part = (keep.astype(f32) + dp_xor(send, 1).astype(f32)).astype(bf16)
    total = lax.dynamic_index_in_dim(part, z, 0, keepdims=False).astype(f32)
    for d in (1, 2, 3):
        piece = lax.dynamic_index_in_dim(part, z ^ d, 0, keepdims=False)
        total = total + dp_xor(piece, 2 * d).astype(f32)
    return total.astype(bf16)


def gathered(piece, y, z):
    own = [piece] + [dp_xor(piece, 2 * d) for d in (1, 2, 3)]
    buffer = jnp.zeros((4,) + piece.shape, piece.dtype)
    for d in range(4):
        buffer = put(buffer, own[d][None], (z ^ d,))
    return buffer, dp_xor(buffer, 1)


def reduce_rows(grad, r, k):
    rows, width = grad.shape
    if lax.axis_size("dp") != 8:
        halves = grad.reshape(2, rows // 2, width)
        keep = lax.dynamic_index_in_dim(halves, r, 0, keepdims=False)
        got = row_swap(lax.dynamic_index_in_dim(halves, 1 - r, 0, keepdims=False))
        both = lax.psum(jnp.where(r == 0, jnp.stack([keep, got]), jnp.stack([got, keep])), "dp")
        return both[0], both[1]
    y, z = k % 2, k // 2
    piece = scattered(grad.reshape(2, 4, rows // 8, width), y, z)
    cross = [
        (2 * i + j, 2 * (i ^ 1) + (j ^ 1))
        for i in range(lax.axis_size("dp"))
        for j in range(2)
        if i % 2 != j
    ]
    piece = jnp.where(y == r, piece, lax.ppermute(piece, ("dp", "row"), cross))
    mine, other = gathered(piece, y, z)
    mine, other = mine.reshape(rows // 2, width), other.reshape(rows // 2, width)
    return jnp.where(y == 0, mine, other), jnp.where(y == 0, other, mine)


def reduce_cols(grad, r, k):
    rows, width = grad.shape
    if lax.axis_size("dp") != 8:
        keep, send = half_of(r, grad, 1), half_of(1 - r, grad, 1)
        got = row_swap(send)
        both = lax.psum(jnp.where(r == 0, jnp.stack([keep, got]), jnp.stack([got, keep])), "dp")
        return both[0], both[1]
    y, z = k % 2, k // 2
    piece = scattered(grad.reshape(2, 4, rows // 8, width), y, z)
    keep, got = half_of(r, piece, 1), row_swap(half_of(1 - r, piece, 1))
    piece = jnp.where(r == 0, jnp.stack([keep, got]), jnp.stack([got, keep]))
    mine, other = gathered(piece, y, z)
    both = jnp.where(y == 0, jnp.stack([mine, other]), jnp.stack([other, mine]))
    both = both.transpose(2, 0, 1, 3, 4).reshape(2, rows, width // 2)
    return both[0], both[1]


def norm(values):
    center = jnp.mean(values, axis=1, keepdims=True)
    shifted = values - center
    inverse = lax.rsqrt(jnp.mean(shifted * shifted, axis=1, keepdims=True) + 1e-05)
    return shifted * inverse, inverse


def core_sum(left, product, rows):
    other = product(left[rows:]).astype(bf16)
    return product(left[:rows]) + col_swap(other).astype(f32)


def full_sum(left, product, rows):
    low = core_sum(left, product, rows).astype(bf16)
    return low.astype(f32) + row_swap(low).astype(f32)


def half_sum(left, product, rows, r):
    part = core_sum(left, product, rows)
    return half_of(r, part, 1) + row_swap(half_of(1 - r, part, 1).astype(bf16)).astype(f32)


def per_device(
    block_in,
    out_grad,
    seq_lengths,
    ln1_gain,
    ln1_bias,
    qkv_weight,
    qv_bias,
    out_weight,
    out_bias,
    ln2_gain,
    ln2_bias,
    fc_weight,
    fc_bias,
    proj_weight,
    proj_bias,
):
    n_dp = lax.axis_size("dp")
    r, c, k = lax.axis_index("row"), lax.axis_index("col"), lax.axis_index("dp")
    tokens, half = block_in.shape
    heads = 7
    most = heads * HEAD_DIM
    wide = 8 * HEAD_DIM
    spare = 32

    qkv_first, qkv_second = head_slots(c, qkv_weight, 2, most, spare)
    qkv_mine = jnp.where(r == 0, qkv_first, qkv_second)
    qkv_other = jnp.where(r == 0, qkv_second, qkv_first)
    y = k % 2
    parts = qkv_other.reshape(3, 2, half // 2, most)
    got_one = row_swap(lax.dynamic_index_in_dim(parts, y, 1, keepdims=False))
    x_peer = row_swap(block_in)
    got_two = dp_xor(got_one, 1)
    buffer = jnp.zeros((3, 4, half // 2, wide), bf16)
    buffer = put(buffer, pad_to(qkv_mine.reshape(3, 2, half // 2, most), wide, 3), (0, 2 * r))
    buffer = put(buffer, pad_to(got_one, wide, 2)[:, None], (0, 2 * (1 - r) + y))
    buffer = put(buffer, pad_to(got_two, wide, 2)[:, None], (0, 2 * (1 - r) + 1 - y))
    qkv_full = buffer.reshape(3, 2 * half, wide)

    vectors = jnp.stack([ln1_gain, ln1_bias, out_bias, ln2_gain, ln2_bias, proj_bias])
    vectors = ordered(r, vectors, row_swap(vectors), 1).astype(f32)
    gain_one, bias_one, bias_out, gain_two, bias_two = [vectors[i][None] for i in range(5)]

    bias_first, bias_second = head_slots(c, qv_bias, 1, most, spare)
    bias_mine = pad_to(jnp.where(r == 0, bias_first, bias_second).astype(f32), wide, 1)

    out_first, out_second = head_slots(c, out_weight, 0, most, spare)
    out_mine = jnp.where(r == 0, out_first, out_second)
    out_got = row_swap(jnp.where(r == 0, out_second, out_first))
    out_full = pad_to(ordered(r, out_mine, out_got, 1), wide, 0)

    fc_mine, fc_other = half_of(r, fc_weight, 1), half_of(1 - r, fc_weight, 1)
    fc_full = ordered(r, fc_mine, gather_quarters(fc_other, k), 0)
    proj_halves = proj_weight.reshape(2, proj_weight.shape[0] // 2, half)
    proj_mine = lax.dynamic_index_in_dim(proj_halves, r, 0, keepdims=False)
    proj_other = lax.dynamic_index_in_dim(proj_halves, 1 - r, 0, keepdims=False)
    proj_full = ordered(r, proj_mine, gather_quarters(proj_other, k), 1)
    fc_bias_mine = half_of(r, fc_bias, 0).astype(f32)[None]

    lengths = seq_lengths[0]
    group = 2 * tokens
    places = jnp.arange(group, dtype=jnp.int32)
    ends = jnp.cumsum(lengths, dtype=jnp.int32)
    first = jnp.sum(
        jnp.where(ends[None, :] <= places[:, None], lengths[None, :], 0), axis=1, dtype=jnp.int32
    ).reshape(group // BLK, BLK)
    info = jnp.concatenate([(c * (tokens // BLK))[None].astype(jnp.int32), first[:, 0] // BLK])

    x_full = ordered(r, block_in, x_peer, 1).astype(f32)
    normed_one, inverse_one = norm(x_full)
    h_one = (normed_one * gain_one + bias_one).astype(bf16)
    h_one_all = jnp.concatenate([h_one, col_swap(h_one)], axis=0)
    zero_bias = jnp.zeros((1, wide), f32)
    projected = jnp.concatenate(
        [
            (nn(h_one_all, qkv_full[i]) + bias).astype(bf16)
            for i, bias in enumerate((bias_mine[:1], zero_bias, bias_mine[1:]))
        ],
        axis=1,
    )
    attended, log_totals = attend(info, projected, first, heads)
    x_mid = x_full + full_sum(attended, lambda rows: nn(rows, out_full), tokens) + bias_out
    normed_two, inverse_two = norm(x_mid)
    h_two = (normed_two * gain_two + bias_two).astype(bf16)
    h_two_all = jnp.concatenate([h_two, col_swap(h_two)], axis=0)
    pre_act = nn(h_two_all, fc_full) + fc_bias_mine
    cube = pre_act * pre_act
    bend = jnp.tanh(gelu_root * (pre_act + gelu_cubic * cube * pre_act))
    activated = (0.5 * pre_act * (1.0 + bend)).astype(bf16)
    slope = 0.5 * (1.0 + bend) + 0.5 * pre_act * (1.0 - bend * bend) * gelu_root * (
        1.0 + 3.0 * gelu_cubic * cube
    )

    out_grad_full = ordered(r, out_grad, row_swap(out_grad), 1)
    out_grad_all = jnp.concatenate([out_grad_full, col_swap(out_grad_full)], axis=0)
    proj_first, proj_second = reduce_cols(tn(activated, out_grad_all).astype(bf16), r, k)
    pre_grad = (nt(out_grad_all, proj_full) * slope).astype(bf16)
    fc_first, fc_second = reduce_rows(tn(h_two_all, pre_grad).astype(bf16), r, k)
    proj_part = half_sum(activated, lambda rows: nn(rows, proj_full), tokens, r)
    block_out = (half_of(r, x_mid, 1) + proj_part + proj_bias.astype(f32)).astype(bf16)

    h_two_grad = full_sum(pre_grad, lambda rows: nt(rows, fc_full), tokens)
    scaled = h_two_grad * gain_two
    mid_grad = out_grad_full.astype(f32) + inverse_two * (
        scaled
        - jnp.mean(scaled, axis=1, keepdims=True)
        - normed_two * jnp.mean(scaled * normed_two, axis=1, keepdims=True)
    )
    branch_grad = mid_grad.astype(bf16)
    branch_all = jnp.concatenate([branch_grad, col_swap(branch_grad)], axis=0)
    out_first, out_second = reduce_cols(tn(attended, branch_all).astype(bf16)[:most], r, k)

    attended_grad = nt(branch_all, out_full).astype(bf16)
    parts_grad = attend_back(info, projected, attended, attended_grad, log_totals, first, heads)
    qkv_parts = [reduce_rows(tn(h_one_all, part).astype(bf16)[:, :most], r, k) for part in parts_grad]

    def h_one_product(rows):
        return sum(nt(part, qkv_full[i]) for i, part in enumerate(rows))

    other = h_one_product([part[tokens:] for part in parts_grad]).astype(bf16)
    mine = h_one_product([part[:tokens] for part in parts_grad]) + col_swap(other).astype(f32)
    h_one_grad = half_of(r, mine, 1) + row_swap(half_of(1 - r, mine, 1).astype(bf16)).astype(f32)
    normed_half = half_of(r, normed_one, 1)
    scaled = h_one_grad * ln1_gain.astype(f32)[None]
    sums = jnp.stack([jnp.sum(scaled, axis=1), jnp.sum(scaled * normed_half, axis=1)])
    sums = (sums + row_swap(sums)) / D
    x_grad = half_of(r, mid_grad, 1) + inverse_one * (
        scaled - sums[0][:, None] - normed_half * sums[1][:, None]
    )

    h_two_half = half_of(r, h_two_grad, 1)
    own = jnp.stack(
        [
            jnp.sum(h_one_grad * normed_half, axis=0),
            jnp.sum(h_one_grad, axis=0),
            jnp.sum(h_two_half * half_of(r, normed_two, 1), axis=0),
            jnp.sum(h_two_half, axis=0),
            jnp.sum(half_of(r, branch_grad, 1).astype(f32), axis=0),
            jnp.sum(out_grad.astype(f32), axis=0),
        ]
    )
    own = own + col_swap(own)
    fc_bias_grad = jnp.sum(pre_grad.astype(f32), axis=0)
    qv = jnp.stack([jnp.sum(parts_grad[i].astype(f32), axis=0)[:most] for i in (0, 2)])
    pack = jnp.concatenate([own.reshape(-1), fc_bias_grad, qv.reshape(-1)])
    pack = pad_to(pack, -(-pack.shape[0] // 1024) * 1024, 0).reshape(-1, 128)
    if n_dp & (n_dp - 1):
        pack = lax.psum(pack, "dp")
    else:
        mask = 1
        while mask < n_dp:
            pack = pack + dp_xor(pack, mask)
            mask *= 2
    peer = row_swap(pack).reshape(-1)
    pack = pack.reshape(-1)
    own = pack[: 6 * half].reshape(6, half)
    low, high = 6 * half, 6 * half + fc_bias_grad.shape[0]
    fc_bias_grad = ordered(r, pack[low:high], peer[low:high], 0)
    qv_mine, qv_peer = [v[high : high + 2 * most].reshape(2, most) for v in (pack, peer)]
    qv_bias_grad = from_slots(
        c, jnp.where(r == 0, qv_mine, qv_peer), jnp.where(r == 0, qv_peer, qv_mine), 1, spare
    )

    qkv_weight_grad = jnp.stack([from_slots(c, a, b, 1, spare).astype(f32) for a, b in qkv_parts])
    out_weight_grad = from_slots(c, out_first, out_second, 0, spare).astype(f32)
    fc_weight_grad = jnp.concatenate([fc_first, fc_second], axis=1).astype(f32)
    proj_weight_grad = jnp.concatenate([proj_first, proj_second], axis=0).astype(f32)
    return (
        block_out,
        x_grad,
        own[0],
        own[1],
        qkv_weight_grad,
        qv_bias_grad,
        out_weight_grad,
        own[4],
        own[2],
        own[3],
        fc_weight_grad,
        fc_bias_grad,
        proj_weight_grad,
        own[5],
    )


def solution(mesh):
    placed = (
        P(("dp", "col"), "row"),
        P(("dp", "col"), "row"),
        P("dp", None),
        P("row"),
        P("row"),
        P(None, "row", "col"),
        P(None, "col"),
        P("col", "row"),
        P("row"),
        P("row"),
        P("row"),
        P("row", "col"),
        P("col"),
        P("col", "row"),
        P("row"),
    )
    return jax.shard_map(
        per_device,
        mesh=mesh,
        in_specs=placed,
        out_specs=(
            P(("dp", "col"), "row"),
            P(("dp", "col"), "row"),
            P("row"),
            P("row"),
            P(None, "row", "col"),
            P(None, "col"),
            P("col", "row"),
            P("row"),
            P("row"),
            P("row"),
            P("row", "col"),
            P("col"),
            P("col", "row"),
            P("row"),
        ),
        check_vma=False,
    )
```

```python
import functools
import math

import jax
import jax.numpy as jnp
from jax import lax
from jax.experimental import pallas as pl
from jax.experimental.pallas import tpu as pltpu
from jax.sharding import PartitionSpec as P

HEAD_DIM = 64
gelu_root = math.sqrt(2.0 / math.pi)
gelu_cubic = 0.044715
BLK = 256
NEG = -1e30
KERNEL_VMEM = 40 * 2**20


def dot_over(dims, a, b):
    return lax.dot_general(a, b, (dims, ((), ())), preferred_element_type=jnp.float32)


def nn(a, b):
    return dot_over(((1,), (0,)), a, b)


def nt(a, b):
    return dot_over(((1,), (1,)), a, b)


def tn(a, b):
    return dot_over(((0,), (0,)), a, b)


def head_rows(h):
    return slice(h * HEAD_DIM, (h + 1) * HEAD_DIM)


def allowed_tile(i, j, first):
    keys = j * BLK + lax.broadcasted_iota(jnp.int32, (BLK, BLK), 0)
    queries = i * BLK + lax.broadcasted_iota(jnp.int32, (BLK, BLK), 1)
    return (keys >= first) & (keys <= queries)


def turned(x):
    return jnp.transpose(x.astype(jnp.float32)).astype(jnp.bfloat16)


def attend_kernel(heads, blocks, info_ref, q_ref, k_ref, v_ref, first_ref, o_ref, lse_ref, keys_ref):
    i = pl.program_id(0)
    shift = info_ref[0]

    @pl.when(i == 0)
    def _():
        for h in range(heads):
            keys_ref[h] = turned(k_ref[head_rows(h), :])

    first = first_ref[pl.ds(i, 1), :]
    scale = jnp.bfloat16(HEAD_DIM**-0.5)

    def step(j, carry):
        place = pl.ds(pl.multiple_of(lax.rem(j + shift, blocks) * BLK, BLK), BLK)
        allowed = allowed_tile(i, j, first)
        out = []
        for h in range(heads):
            top, total, acc = carry[h]
            scores = nn(keys_ref[h, place, :], q_ref[head_rows(h), :] * scale)
            scores = jnp.where(allowed, scores, NEG)
            new_top = jnp.maximum(top, jnp.max(scores, axis=0, keepdims=True))
            probs = jnp.exp(scores - new_top)
            shrink = jnp.exp(top - new_top)
            total = total * shrink + jnp.sum(probs, axis=0, keepdims=True)
            acc = acc * shrink + nn(v_ref[head_rows(h), place], probs.astype(jnp.bfloat16))
            out.append((new_top, total, acc))
        return tuple(out)

    row = lambda value: jnp.full((1, BLK), value, jnp.float32)
    start = tuple((row(NEG), row(0.0), jnp.zeros((HEAD_DIM, BLK), jnp.float32)) for h in range(heads))
    done = lax.fori_loop(info_ref[1 + i], i + 1, step, start)
    for h, (top, total, acc) in enumerate(done):
        o_ref[head_rows(h), :] = (acc / total).astype(jnp.bfloat16)
        lse_ref[h : h + 1, :] = top + jnp.log(total)


def attend(info, projected, first, heads):
    tokens = projected.shape[1]
    wide, blocks = heads * HEAD_DIM, tokens // BLK
    at = lambda i, s: lax.rem(i + s[0], blocks)
    return pl.pallas_call(
        functools.partial(attend_kernel, heads, blocks),
        grid_spec=pltpu.PrefetchScalarGridSpec(
            num_scalar_prefetch=1,
            grid=(blocks,),
            in_specs=[
                pl.BlockSpec((wide, BLK), lambda i, s: (0, at(i, s))),
                pl.BlockSpec((wide, tokens), lambda i, s: (1, 0)),
                pl.BlockSpec((wide, tokens), lambda i, s: (2, 0)),
                pl.BlockSpec((blocks, BLK), lambda i, s: (0, 0)),
            ],
            out_specs=[
                pl.BlockSpec((wide, BLK), lambda i, s: (0, at(i, s))),
                pl.BlockSpec((8, BLK), lambda i, s: (0, i)),
            ],
            scratch_shapes=[pltpu.VMEM((heads, tokens, HEAD_DIM), jnp.bfloat16)],
        ),
        out_shape=[
            jax.ShapeDtypeStruct((wide, tokens), jnp.bfloat16),
            jax.ShapeDtypeStruct((8, tokens), jnp.float32),
        ],
        compiler_params=pltpu.CompilerParams(vmem_limit_bytes=KERNEL_VMEM),
        cost_estimate=pl.CostEstimate(flops=0, bytes_accessed=2 * tokens * wide, transcendentals=0),
        name="attend",
    )(info, projected, projected, projected, first)


def attend_back_kernel(
    heads, blocks, info_ref, q_ref, k_ref, v_ref, o_ref, g_ref, lse_ref, first_ref,
    d_ref, keys_ref, values_ref, dk_acc, dv_acc,
):
    i = pl.program_id(0)
    shift = info_ref[0]

    @pl.when(i == 0)
    def _():
        for h in range(heads):
            keys_ref[h] = turned(k_ref[head_rows(h), :])
            values_ref[h] = turned(v_ref[head_rows(h), :])
        dk_acc[...] = jnp.zeros_like(dk_acc)
        dv_acc[...] = jnp.zeros_like(dv_acc)

    first = first_ref[pl.ds(i, 1), :]
    scale = jnp.bfloat16(HEAD_DIM**-0.5)
    centre = [
        jnp.sum(
            g_ref[head_rows(h), :].astype(jnp.float32) * o_ref[head_rows(h), :].astype(jnp.float32),
            axis=0,
            keepdims=True,
        )
        for h in range(heads)
    ]

    def step(j, carry):
        place = pl.ds(pl.multiple_of(lax.rem(j + shift, blocks) * BLK, BLK), BLK)
        allowed = allowed_tile(i, j, first)
        out = []
        for h in range(heads):
            rows = head_rows(h)
            query = q_ref[rows, :] * scale
            grad = g_ref[rows, :]
            scores = jnp.where(allowed, nn(keys_ref[h, place, :], query), NEG)
            probs = jnp.exp(scores - lse_ref[h : h + 1, :])
            prob_grad = nn(values_ref[h, place, :], grad)
            score_grad = (probs * (prob_grad - centre[h])).astype(jnp.bfloat16)
            dv_acc[rows, place] += nt(grad, probs.astype(jnp.bfloat16))
            dk_acc[rows, place] += nt(query, score_grad)
            out.append(carry[h] + nn(k_ref[rows, place], score_grad))
        return tuple(out)

    start = tuple(jnp.zeros((HEAD_DIM, BLK), jnp.float32) for h in range(heads))
    done = lax.fori_loop(info_ref[1 + i], i + 1, step, start)
    mine = pl.ds(pl.multiple_of(lax.rem(i + shift, blocks) * BLK, BLK), BLK)
    for h in range(heads):
        d_ref[head_rows(2 * heads + h), mine] = (done[h] * HEAD_DIM**-0.5).astype(jnp.bfloat16)

    @pl.when(i == blocks - 1)
    def _():
        d_ref[: heads * HEAD_DIM, :] = dk_acc[...].astype(jnp.bfloat16)
        d_ref[heads * HEAD_DIM : 2 * heads * HEAD_DIM, :] = dv_acc[...].astype(jnp.bfloat16)


def attend_back(info, projected, attended, grad, log_totals, first, heads):
    tokens = projected.shape[1]
    wide, blocks = heads * HEAD_DIM, tokens // BLK
    at = lambda i, s: lax.rem(i + s[0], blocks)
    block = pl.BlockSpec((wide, BLK), lambda i, s: (0, at(i, s)))
    whole = lambda part: pl.BlockSpec((wide, tokens), lambda i, s: (part, 0))
    return pl.pallas_call(
        functools.partial(attend_back_kernel, heads, blocks),
        grid_spec=pltpu.PrefetchScalarGridSpec(
            num_scalar_prefetch=1,
            grid=(blocks,),
            in_specs=[
                block,
                whole(1),
                whole(2),
                block,
                block,
                pl.BlockSpec((8, BLK), lambda i, s: (0, i)),
                pl.BlockSpec((blocks, BLK), lambda i, s: (0, 0)),
            ],
            out_specs=pl.BlockSpec((3 * wide, tokens), lambda i, s: (0, 0)),
            scratch_shapes=[
                pltpu.VMEM((heads, tokens, HEAD_DIM), jnp.bfloat16),
                pltpu.VMEM((heads, tokens, HEAD_DIM), jnp.bfloat16),
                pltpu.VMEM((wide, tokens), jnp.float32),
                pltpu.VMEM((wide, tokens), jnp.float32),
            ],
        ),
        out_shape=jax.ShapeDtypeStruct((3 * wide, tokens), jnp.bfloat16),
        compiler_params=pltpu.CompilerParams(vmem_limit_bytes=KERNEL_VMEM),
        cost_estimate=pl.CostEstimate(flops=0, bytes_accessed=2 * tokens * wide, transcendentals=0),
        name="attend_back",
    )(info, projected, projected, projected, attended, grad, log_totals, first)


def call(body, name, grid, specs, args, out_specs, out_shapes, scalars=None, scratch=()):
    return pl.pallas_call(
        body,
        grid_spec=pltpu.PrefetchScalarGridSpec(
            num_scalar_prefetch=1, grid=grid, in_specs=specs, out_specs=out_specs, scratch_shapes=scratch
        ),
        out_shape=out_shapes,
        compiler_params=pltpu.CompilerParams(vmem_limit_bytes=KERNEL_VMEM),
        cost_estimate=pl.CostEstimate(flops=0, bytes_accessed=0, transcendentals=0),
        name=name,
    )(jnp.zeros((1,), jnp.int32) if scalars is None else scalars, *args)


def shape(*dims, dtype=jnp.bfloat16):
    return jax.ShapeDtypeStruct(dims, dtype)


def whole_spec(value):
    zeros = (0,) * value.ndim
    return pl.BlockSpec(value.shape, lambda *_: zeros)


def chunks(size, step):
    return [slice(i, min(i + step, size)) for i in range(0, size, step)]


def project(weight, own, other, bias):
    parts, depth, width = weight.shape
    count = own.shape[1]

    def body(_, w_ref, own_ref, other_ref, b_ref, o_ref):
        def run(ref):
            for cols in chunks(count, 256):
                o_ref[:, cols] = (tn(w_ref[0], ref[:, cols]) + b_ref[0]).astype(jnp.bfloat16)

        pl.when(pl.program_id(0) == 0)(lambda: run(own_ref))
        pl.when(pl.program_id(0) == 1)(lambda: run(other_ref))

    return call(
        body, "project", (2, parts),
        [
            pl.BlockSpec((1, depth, width), lambda i, j, _: (j, 0, 0)),
            whole_spec(own),
            whole_spec(other),
            pl.BlockSpec((1, width, 1), lambda i, j, _: (j, 0, 0)),
        ],
        (weight, own, other, bias),
        pl.BlockSpec((width, count), lambda i, j, _: (j, i)),
        shape(parts * width, 2 * count),
    )


def hidden(weight, own, other, bias):
    depth, width = weight.shape
    count = own.shape[1]
    block = 256
    half = count // block

    def body(_, w_ref, own_ref, other_ref, b_ref, act_ref, slope_ref):
        tokens = jnp.where(pl.program_id(0) < half, own_ref[...], other_ref[...])
        for rows in chunks(width, 256):
            pre = tn(w_ref[:, rows], tokens) + b_ref[rows, :]
            square = pre * pre
            bend = jnp.tanh(pre * (gelu_root + (gelu_root * gelu_cubic) * square))
            lift = 0.5 * (1.0 + bend)
            act_ref[rows, :] = (pre * lift).astype(jnp.bfloat16)
            slope_ref[rows, :] = lift + (pre * lift) * (1.0 - bend) * (
                gelu_root + (3.0 * gelu_root * gelu_cubic) * square
            )

    tile = pl.BlockSpec((width, block), lambda i, _: (0, i))
    return call(
        body, "hidden", (2 * half,),
        [
            whole_spec(weight),
            pl.BlockSpec((depth, block), lambda i, _: (0, jnp.minimum(i, half - 1))),
            pl.BlockSpec((depth, block), lambda i, _: (0, jnp.maximum(i - half, 0))),
            whole_spec(bias),
        ],
        (weight, own, other, bias),
        [tile, tile],
        [shape(width, 2 * count), shape(width, 2 * count, dtype=jnp.float32)],
    )


def hidden_back(weight, own, other, slope):
    depth, width = weight.shape
    count = own.shape[1]
    block = 256
    half = count // block

    def body(_, w_ref, own_ref, other_ref, s_ref, o_ref, sum_ref):
        tokens = jnp.where(pl.program_id(0) < half, own_ref[...], other_ref[...])

        @pl.when(pl.program_id(0) == 0)
        def _():
            sum_ref[...] = jnp.zeros_like(sum_ref)

        for rows in chunks(width, 256):
            grad = (tn(w_ref[:, rows], tokens) * s_ref[rows, :]).astype(jnp.bfloat16)
            o_ref[rows, :] = grad
            grad = grad.astype(jnp.float32)
            sum_ref[rows, :] += grad[:, :128] + grad[:, 128:]

    tile = pl.BlockSpec((width, block), lambda i, _: (0, i))
    return call(
        body, "hidden_back", (2 * half,),
        [
            whole_spec(weight),
            pl.BlockSpec((depth, block), lambda i, _: (0, jnp.minimum(i, half - 1))),
            pl.BlockSpec((depth, block), lambda i, _: (0, jnp.maximum(i - half, 0))),
            tile,
        ],
        (weight, own, other, slope),
        [tile, pl.BlockSpec((width, 128), lambda i, _: (0, 0))],
        [shape(width, 2 * count), shape(width, 128, dtype=jnp.float32)],
    )


def mapped(weight, tokens, part, turn, received=None):
    depth, count = weight.shape[0 if turn else 1], tokens.shape[1] // 2
    rows = weight.shape[1 if turn else 0]
    block = rows if turn else 400
    step = 256 if turn else block

    def body(_, w_ref, t_ref, *refs):
        o_ref = refs[-1]
        for cut in chunks(block, step):
            part = tn(w_ref[:, cut], t_ref[...]) if turn else nn(w_ref[cut, :], t_ref[...])
            if received is not None:
                part = part + refs[0][cut, :].astype(jnp.float32)
            o_ref[cut, :] = part.astype(jnp.bfloat16)

    extra = () if received is None else (received,)
    if turn:
        cols = 256
        grid = (count // cols,)
        tile = pl.BlockSpec((rows, cols), lambda i, _: (0, i))
        specs = [
            whole_spec(weight),
            pl.BlockSpec((depth, cols), lambda i, _: (0, part * (count // cols) + i)),
        ] + [tile] * len(extra)
    else:
        grid = (rows // block,)
        tile = pl.BlockSpec((block, count), lambda i, _: (i, 0))
        specs = [
            pl.BlockSpec((block, depth), lambda i, _: (i, 0)),
            pl.BlockSpec((depth, count), lambda i, _: (0, part)),
        ] + [tile] * len(extra)
    return call(body, "mapped", grid, specs, (weight, tokens) + extra, tile, shape(rows, count))


def mapped_three(weight, parts, part, received=None):
    count = parts.shape[1] // 2
    _, rows, width = weight.shape
    block = 400

    def body(_, w_ref, p_ref, *refs):
        total = sum(nn(w_ref[(i + 1) % 3], p_ref[i * width : (i + 1) * width, :]) for i in range(3))
        if received is not None:
            total = total + refs[0][...].astype(jnp.float32)
        refs[-1][...] = total.astype(refs[-1].dtype)

    tile = pl.BlockSpec((block, count), lambda i, _: (i, 0))
    extra = () if received is None else (received,)
    return call(
        body, "mapped_three", (rows // block,),
        [
            pl.BlockSpec((3, block, width), lambda i, _: (0, i, 0)),
            pl.BlockSpec((3 * width, count), lambda i, _: (0, part)),
        ] + [tile] * len(extra),
        (weight, parts) + extra,
        tile,
        shape(rows, count, dtype=jnp.bfloat16 if received is None else jnp.float32),
    )


def attended_back(weight, own, other):
    width, depth = weight.shape
    count = own.shape[1]

    def body(_, w_ref, own_ref, other_ref, o_ref):
        def run(ref):
            for cols in chunks(count, 256):
                o_ref[:, cols] = nn(w_ref[...], ref[:, cols]).astype(jnp.bfloat16)

        pl.when(pl.program_id(0) == 0)(lambda: run(own_ref))
        pl.when(pl.program_id(0) == 1)(lambda: run(other_ref))

    return call(
        body, "attended_back", (2,),
        [whole_spec(weight), whole_spec(own), whole_spec(other)],
        (weight, own, other),
        pl.BlockSpec((width, count), lambda i, _: (0, i)),
        shape(width, 2 * count),
    )


def weight_grad(own, other, right, order, parts, part):
    rows, count = own.shape
    (place, width), size = part, rows // parts

    def body(_, own_ref, other_ref, r_ref, o_ref):
        o_ref[0] = (nt(own_ref[0], r_ref[:, :count]) + nt(other_ref[0], r_ref[:, count:])).astype(jnp.bfloat16)

    tile = pl.BlockSpec((1, size, count), lambda i, s: (s[i], 0, 0))
    return call(
        body, "weight_grad", order.shape,
        [tile, tile, pl.BlockSpec((width, 2 * count), lambda i, s: (place, 0))],
        (own.reshape(parts, size, count), other.reshape(parts, size, count), right),
        pl.BlockSpec((1, size, width), lambda i, s: (i, 0, 0)),
        shape(order.shape[0], size, width),
        scalars=order,
    )


SWAP = ((0, 1), (1, 0))
f32 = jnp.float32
bf16 = jnp.bfloat16


def row_swap(value):
    return lax.ppermute(value, "row", SWAP)


def col_swap(value):
    return lax.ppermute(value, "col", SWAP)


def dp_xor(value, mask):
    return lax.ppermute(value, "dp", [(i, i ^ mask) for i in range(lax.axis_size("dp"))])


def after(value, *marks):
    return lax.optimization_barrier((value,) + marks)[0] if marks else value


def ordered(at, first, second, axis):
    return jnp.where(
        at == 0,
        jnp.concatenate([first, second], axis=axis),
        jnp.concatenate([second, first], axis=axis),
    )


def paired(at, first, second, axis):
    return ordered(at, jnp.expand_dims(first, axis), jnp.expand_dims(second, axis), axis)


def half_of(at, value, axis):
    size = value.shape[axis] // 2
    return jnp.where(
        at == 0,
        lax.slice_in_dim(value, 0, size, axis=axis),
        lax.slice_in_dim(value, size, 2 * size, axis=axis),
    )


def pick(value, at, axis):
    return lax.dynamic_index_in_dim(value, at, axis, keepdims=False)


def plus(a, b):
    return a.astype(f32) + b.astype(f32)


def pad_to(value, size, axis):
    widths = [(0, 0)] * value.ndim
    widths[axis] = (0, size - value.shape[axis])
    return jnp.pad(value, widths)


def head_slots(c, value, tail, axis, most):
    cut = lambda low, high: lax.slice_in_dim(value, low, high, axis=axis)
    size, spare = value.shape[axis], tail.shape[axis]
    less = most - HEAD_DIM
    first = jnp.where(c == 0, cut(0, most), pad_to(cut(spare, spare + less), most, axis))
    second = jnp.where(
        c == 0,
        pad_to(jnp.concatenate([cut(most, size), tail], axis=axis), most, axis),
        pad_to(cut(spare + less, size), most, axis),
    )
    return first, second


def from_slots(c, first, second, axis, spare):
    cut = lambda value, low, high: lax.slice_in_dim(value, low, high, axis=axis)
    most = first.shape[axis]
    less = most - HEAD_DIM
    tail = col_swap(cut(second, less - spare, less))
    return jnp.where(
        c == 0,
        jnp.concatenate([first, cut(second, 0, less - spare)], axis=axis),
        jnp.concatenate([tail, cut(first, 0, less), cut(second, 0, less)], axis=axis),
    )


def pack(qkv, tail, fc, proj, c, r, at, most):
    rows, size = qkv.shape[1] // 4, qkv.shape[2]
    spare, less, wide = tail.shape[2], most - HEAD_DIM, fc.shape[1] // 2
    scalars = jnp.stack([at, c, r]).astype(jnp.int32)

    def body(s_ref, q_ref, t_ref, f_ref, p_ref, qo_ref, fo_ref, po_ref):
        core, row = s_ref[1], s_ref[2]

        @pl.when((core == 0) & (row == 1))
        def _():
            qo_ref[...] = q_ref[:, 0, :, :most]

        @pl.when((core == 0) & (row == 0))
        def _():
            qo_ref[...] = jnp.zeros_like(qo_ref)
            qo_ref[:, :, : size - most] = q_ref[:, 0, :, most:]
            qo_ref[:, :, size - most : size - most + spare] = t_ref[:, 0]

        @pl.when((core == 1) & (row == 1))
        def _():
            qo_ref[...] = jnp.zeros_like(qo_ref)
            qo_ref[:, :, :less] = q_ref[:, 0, :, spare : spare + less]

        @pl.when((core == 1) & (row == 0))
        def _():
            qo_ref[...] = jnp.zeros_like(qo_ref)
            qo_ref[:, :, :less] = q_ref[:, 0, :, spare + less :]

        @pl.when(row == 0)
        def _():
            fo_ref[...] = f_ref[0, :, wide:]
            po_ref[...] = p_ref[0, :, wide:]

        @pl.when(row == 1)
        def _():
            fo_ref[...] = f_ref[0, :, :wide]
            po_ref[...] = p_ref[0, :, :wide]

    quarter = lambda v: v.reshape(v.shape[:-2] + (4, rows, v.shape[-1]))
    return call(
        body, "pack", (1,),
        [
            pl.BlockSpec((3, 1, rows, size), lambda i, s: (0, s[0], 0, 0)),
            pl.BlockSpec((3, 1, rows, spare), lambda i, s: (0, s[0], 0, 0)),
            pl.BlockSpec((1, rows, 2 * wide), lambda i, s: (s[0], 0, 0)),
            pl.BlockSpec((1, rows, 2 * wide), lambda i, s: (s[0], 0, 0)),
        ],
        tuple(quarter(v) for v in (qkv, tail, fc, proj)),
        [pl.BlockSpec((3, rows, most), lambda i, s: (0, 0, 0))] + [pl.BlockSpec((rows, wide), lambda i, s: (0, 0))] * 2,
        [shape(3, rows, most), shape(rows, wide), shape(rows, wide)],
        scalars=scalars,
    )


class Fetch:
    def __init__(self, sent, k):
        self.y, self.z = k % 2, (k // 2) % 2
        self.got = row_swap(sent)

    def second(self, *marks):
        self.got = after(self.got, *marks)
        self.got = paired(self.z, self.got, dp_xor(self.got, 2), 1)
        return self.got

    def third(self, *marks):
        self.got = after(self.got, *marks)
        self.peer = dp_xor(self.got, 1)

    def result(self, *marks):
        both = paired(self.y, after(self.got, *marks), self.peer, 2)
        return both.reshape(both.shape[0], -1, both.shape[-1])


class Total:
    def __init__(self, own, other, right, part, r, k, y_first, *marks):
        self.rows, self.width = own.shape[0], part[1]
        self.r, self.k, self.y_first = r, k, y_first
        self.fast = lax.axis_size("dp") == 8
        right = after(right, *marks)
        if not self.fast:
            self.grad = weight_grad(own, other, right, jnp.arange(4, dtype=jnp.int32), 4, part)
            return
        self.y, self.lo, self.hi = k % 2, (k // 2) % 2, k // 4
        if y_first:
            send, parts, mask = 2 * (1 - self.y) + jnp.arange(2), 4, 1
            keep = 2 * self.y + jnp.arange(2)
        else:
            send, parts, mask = (1 - self.lo) + 2 * jnp.arange(4), 8, 2
            keep = self.lo + 2 * jnp.arange(4)
        shaped = lambda v: v.reshape(2, 2, self.rows // 8, self.width)
        sent = weight_grad(own, other, right, send.astype(jnp.int32), parts, part)
        self.got = dp_xor(shaped(sent), mask)
        self.keep = shaped(weight_grad(own, other, after(right, sent), keep.astype(jnp.int32), parts, part))

    def marks(self):
        return [self.keep] if self.fast else []

    def sum_one(self, *marks):
        if self.fast:
            part = plus(after(self.keep, *marks), self.got).astype(bf16)
            axis, at, mask = (1, self.lo, 2) if self.y_first else (0, self.y, 1)
            self.keep, self.got = pick(part, at, axis), dp_xor(pick(part, 1 - at, axis), mask)
            return [self.keep]
        return []

    def sum_two(self, *marks):
        if self.fast:
            part = plus(after(self.keep, *marks), self.got).astype(bf16)
            self.keep, self.got = pick(part, self.hi, 0), dp_xor(pick(part, 1 - self.hi, 0), 4)
            return [self.keep]
        return []

    def sum_three(self, *marks):
        if self.fast:
            cross = [
                (2 * i + j, 2 * (i ^ 1) + (j ^ 1))
                for i in range(lax.axis_size("dp"))
                for j in range(2)
                if i % 2 != j
            ]
            self.keep = plus(after(self.keep, *marks), self.got).astype(bf16)
            self.got = lax.ppermute(self.keep, ("dp", "row"), cross)
            return [self.keep]
        return []

    def spread_one(self, *marks):
        if self.fast:
            self.keep = jnp.where(self.y == self.r, after(self.keep, *marks), self.got)
            self.got = dp_xor(self.keep, 4)
            return [self.keep]
        return []

    def spread_two(self, *marks):
        if self.fast:
            self.keep = paired(self.hi, after(self.keep, *marks), self.got, 0)
            self.got = dp_xor(self.keep, 2 if self.y_first else 1)
            return [self.keep]
        return []

    def spread_three(self, *marks):
        if self.fast:
            if self.y_first:
                self.keep = paired(self.lo, after(self.keep, *marks), self.got, 1)
                self.got = dp_xor(self.keep, 1)
            else:
                self.keep = paired(self.y, after(self.keep, *marks), self.got, 0)
                self.got = dp_xor(self.keep, 2)
            return [self.keep]
        return []

    def result(self, *marks):
        if not self.fast:
            halves = self.grad.reshape(2, self.rows // 2, self.width)
            keep, got = pick(halves, self.r, 0), row_swap(pick(halves, 1 - self.r, 0))
            both = lax.psum(paired(self.r, keep, got, 0), "dp")
            return both[0], both[1]
        keep, got = after(self.keep, *marks), self.got
        if self.y_first:
            both = paired(self.y, keep, got, 0)
        else:
            both = paired(self.lo, keep, got, 2)
        both = both.reshape(2, self.rows // 2, self.width)
        return both[0], both[1]


def norm(values):
    center = jnp.mean(values, axis=0, keepdims=True)
    shifted = values - center
    inverse = lax.rsqrt(jnp.mean(shifted * shifted, axis=0, keepdims=True) + 1e-05)
    return shifted * inverse, inverse


def per_device(
    block_in,
    out_grad,
    seq_lengths,
    ln1_gain,
    ln1_bias,
    qkv_weight,
    qv_bias,
    out_weight,
    out_bias,
    ln2_gain,
    ln2_bias,
    fc_weight,
    fc_bias,
    proj_weight,
    proj_bias,
):
    n_dp = lax.axis_size("dp")
    r, c, k = lax.axis_index("row"), lax.axis_index("col"), lax.axis_index("dp")
    x_own, grad_own = block_in.T, out_grad.T
    half, tokens = x_own.shape
    heads = 7
    most = heads * HEAD_DIM
    spare = 32
    column = lambda v: v.astype(f32)[:, None]

    qkv_tail = col_swap(qkv_weight[:, :, :spare])
    proj_turned = proj_weight.T
    qkv_sent, fc_sent, proj_sent = pack(
        qkv_weight, qkv_tail, fc_weight, proj_turned, c, r, 2 * ((k // 2) % 2) + k % 2, most
    )
    qkv_fetch = Fetch(qkv_sent, k)
    x_peer = row_swap(after(x_own, qkv_sent))
    fc_fetch = Fetch(fc_sent[None], k)
    proj_fetch = Fetch(proj_sent[None], k)
    vectors = jnp.stack([ln1_gain, ln1_bias, out_bias, ln2_gain, ln2_bias])
    vectors = ordered(r, vectors, row_swap(vectors), 1).astype(f32)
    gain_one, bias_one, bias_out, gain_two, bias_two = [vectors[i][:, None] for i in range(5)]

    bias_first, bias_second = head_slots(c, qv_bias, col_swap(qv_bias[:, :spare]), 1, most)
    bias_mine = jnp.where(r == 0, bias_first, bias_second).astype(f32)
    bias_mine = jnp.stack([bias_mine[0], jnp.zeros_like(bias_mine[0]), bias_mine[1]])[:, :, None]

    out_first, out_second = head_slots(c, after(out_weight, qkv_sent), col_swap(out_weight[:spare]), 0, most)
    out_mine = jnp.where(r == 0, out_first, out_second)
    out_got = row_swap(jnp.where(r == 0, out_second, out_first))

    qkv_first, qkv_second = head_slots(c, after(qkv_weight, out_mine), qkv_tail, 2, most)
    qkv_mine = jnp.where(r == 0, qkv_first, qkv_second)
    mark = qkv_fetch.second(qkv_mine)
    qkv_fetch.third()
    fc_mine = half_of(r, after(fc_weight, mark), 1)
    proj_mine = half_of(r, after(proj_turned, mark), 1)
    fc_bias_mine = column(half_of(r, fc_bias, 0))

    lengths = seq_lengths[0]
    group = 2 * tokens
    places = jnp.arange(group, dtype=jnp.int32)
    ends = jnp.cumsum(lengths, dtype=jnp.int32)
    first = jnp.sum(
        jnp.where(ends[None, :] <= places[:, None], lengths[None, :], 0), axis=1, dtype=jnp.int32
    ).reshape(group // BLK, BLK)
    info = jnp.concatenate([(c * (tokens // BLK))[None].astype(jnp.int32), first[:, 0] // BLK])

    x_full = ordered(r, x_own, x_peer, 0).astype(f32)
    normed_one, inverse_one = norm(x_full)
    h_one = (normed_one * gain_one + bias_one).astype(bf16)
    h_one_peer = col_swap(h_one)
    mark = fc_fetch.second(h_one)
    qkv_full = ordered(r, qkv_mine, qkv_fetch.result(mark), 1)
    projected = project(qkv_full, h_one, h_one_peer, bias_mine)
    fc_fetch.third(projected)
    mark = proj_fetch.second(fc_fetch.got)
    attended, log_totals = attend(info, after(projected, mark), first, heads)
    proj_fetch.third(attended)
    out_full = ordered(r, out_mine, out_got, 1)
    other = mapped(out_full, attended, 1, True)
    low = mapped(out_full, attended, 0, True, col_swap(other))
    branch_other = row_swap(low)
    fc_full = ordered(r, after(fc_mine, low), fc_fetch.result(low)[0], 0)
    proj_full = ordered(r, after(proj_mine, fc_full), proj_fetch.result(fc_full)[0], 0)
    x_mid = after(x_full, proj_full) + plus(low, branch_other) + bias_out
    normed_two, inverse_two = norm(x_mid)
    h_two = (normed_two * gain_two + bias_two).astype(bf16)
    h_two_peer = col_swap(h_two)
    grad_full = ordered(r, after(grad_own, h_two), row_swap(after(grad_own, low)), 0)
    grad_peer = col_swap(grad_full)
    activated, slope = hidden(fc_full, h_two, h_two_peer, fc_bias_mine)

    ff = (0, activated.shape[0])
    proj_total = Total(grad_full, grad_peer, activated, ff, r, k, True)
    pre_grad, fc_bias_grad = hidden_back(proj_full, after(grad_full, *proj_total.marks()), grad_peer, slope)
    other = mapped(fc_full, pre_grad, 1, False)
    low = mapped(fc_full, pre_grad, 0, False, col_swap(other))
    h_two_grad = plus(low, row_swap(low))
    fc_total = Total(h_two, h_two_peer, pre_grad, ff, r, k, True, low)
    mark = proj_total.sum_one(*fc_total.marks())
    other = mapped(proj_full, after(activated, *mark), 1, False)
    proj_part = mapped(proj_full, activated, 0, False, col_swap(other))
    block_other = row_swap(half_of(1 - r, proj_part, 0))
    mark = proj_total.sum_two(proj_part)

    scaled = after(h_two_grad, proj_part, *mark) * gain_two
    mid_grad = grad_full.astype(f32) + inverse_two * (
        scaled
        - jnp.mean(scaled, axis=0, keepdims=True)
        - normed_two * jnp.mean(scaled * normed_two, axis=0, keepdims=True)
    )
    branch_grad = mid_grad.astype(bf16)
    branch_peer = col_swap(branch_grad)
    mark = proj_total.sum_three(branch_grad)
    mark = fc_total.sum_one(*mark)

    out_total = Total(branch_grad, branch_peer, attended, (0, most), r, k, False, *mark)
    mark = proj_total.spread_one(*out_total.marks())
    attended_grad = attended_back(out_full, after(branch_grad, *mark), branch_peer)
    parts = attend_back(info, projected, attended, attended_grad, log_totals, first, heads)
    mark = fc_total.sum_two(parts)
    mark = out_total.sum_one(*mark)
    mark = proj_total.spread_two(*mark)
    q_total = Total(h_one, h_one_peer, parts, (2, most), r, k, False, *mark)
    kv_total = Total(h_one, h_one_peer, parts, (0, 2 * most), r, k, True, *q_total.marks())
    other = mapped_three(qkv_full, after(parts, *kv_total.marks()), 1)
    mark = out_total.sum_two(other)
    mark = fc_total.sum_three(*mark)
    mine = mapped_three(qkv_full, after(parts, *mark), 0, col_swap(other))
    one_other = row_swap(half_of(1 - r, mine, 0).astype(bf16))
    mark = out_total.sum_three(mine)
    mark = proj_total.spread_three(*mark)
    mark = fc_total.spread_one(*mark)
    mark = kv_total.sum_one(*mark)
    mark = out_total.spread_one(*mark)

    normed_half = half_of(r, normed_one, 0)
    h_one_grad = after(half_of(r, mine, 0), *mark) + one_other.astype(f32)
    scaled = h_one_grad * column(ln1_gain)
    sums = jnp.stack([jnp.sum(scaled, axis=0), jnp.sum(scaled * normed_half, axis=0)])
    sums_peer = row_swap(sums)

    mark = q_total.sum_one(sums)
    mark = fc_total.spread_two(*mark)
    sums = (after(sums, *mark) + sums_peer) / (2 * half)
    x_grad = half_of(r, mid_grad, 0) + inverse_one * (
        scaled - sums[0][None] - normed_half * sums[1][None]
    )
    mark = out_total.spread_two(x_grad)
    mark = kv_total.sum_two(*mark)
    block_out = after(half_of(r, x_mid, 0), *mark) + plus(half_of(r, proj_part, 0), block_other)
    block_out = (block_out + column(proj_bias)).astype(bf16)

    h_two_half = half_of(r, h_two_grad, 0)
    own = jnp.stack(
        [
            jnp.sum(h_one_grad * normed_half, axis=1),
            jnp.sum(h_one_grad, axis=1),
            jnp.sum(h_two_half * half_of(r, normed_two, 0), axis=1),
            jnp.sum(h_two_half, axis=1),
            jnp.sum(half_of(r, branch_grad, 0).astype(f32), axis=1),
            jnp.sum(grad_own.astype(f32), axis=1),
        ]
    )
    own_peer = col_swap(own)
    fc_bias_grad = jnp.sum(fc_bias_grad, axis=1)
    qv = jnp.stack([jnp.sum(parts[i * most : (i + 1) * most].astype(f32), axis=1) for i in (2, 1)])

    proj_weight_grad = jnp.concatenate(proj_total.result(block_out), axis=1).astype(f32).T
    mark = q_total.sum_two(proj_weight_grad)
    mark = kv_total.sum_three(*mark)
    own = after(own, *mark) + own_peer
    pack_sums = jnp.concatenate([own.reshape(-1), fc_bias_grad, qv.reshape(-1)])
    pack_sums = pad_to(pack_sums, -(-pack_sums.shape[0] // 1024) * 1024, 0).reshape(-1, 128)
    steps = [
        [out_total.spread_three, q_total.sum_three],
        [kv_total.spread_one, fc_total.spread_three],
        [q_total.spread_one],
    ]
    if n_dp & (n_dp - 1):
        pack_sums = lax.psum(pack_sums, "dp")
    else:
        mask = 1
        while mask < n_dp:
            peer = dp_xor(pack_sums, mask)
            for step in steps[:1]:
                for one in step:
                    mark = one(*mark)
            steps = steps[1:]
            pack_sums = after(pack_sums, *mark) + peer
            mask *= 2
    peer = row_swap(pack_sums).reshape(-1)
    mark = kv_total.spread_two(*mark)
    mark = q_total.spread_two(*mark)
    peer = after(peer, *mark)
    pack_sums = pack_sums.reshape(-1)
    own = pack_sums[: 6 * half].reshape(6, half)
    low, high = 6 * half, 6 * half + fc_bias_grad.shape[0]
    fc_bias_grad = ordered(r, pack_sums[low:high], peer[low:high], 0)
    qv_mine, qv_peer = [v[high : high + 2 * most].reshape(2, most) for v in (pack_sums, peer)]
    qv_bias_grad = from_slots(
        c, jnp.where(r == 0, qv_mine, qv_peer), jnp.where(r == 0, qv_peer, qv_mine), 1, spare
    )
    out_weight_grad = from_slots(c, *out_total.result(*mark), 1, spare).T.astype(f32)
    fc_weight_grad = jnp.concatenate(fc_total.result(out_weight_grad), axis=1).astype(f32)
    mark = kv_total.spread_three(fc_weight_grad)
    mark = q_total.spread_three(*mark)
    q_both = q_total.result(*mark)
    kv_both = kv_total.result(q_both[0])
    pairs = [q_both] + [[v[:, i * most : (i + 1) * most] for v in kv_both] for i in range(2)]
    qkv_weight_grad = jnp.stack([from_slots(c, *pair, 1, spare).astype(f32) for pair in pairs])
    return (
        block_out.T,
        x_grad.T,
        own[0],
        own[1],
        qkv_weight_grad,
        qv_bias_grad,
        out_weight_grad,
        own[4],
        own[2],
        own[3],
        fc_weight_grad,
        fc_bias_grad,
        proj_weight_grad,
        own[5],
    )


def solution(mesh):
    placed = (
        P(("dp", "col"), "row"),
        P(("dp", "col"), "row"),
        P("dp", None),
        P("row"),
        P("row"),
        P(None, "row", "col"),
        P(None, "col"),
        P("col", "row"),
        P("row"),
        P("row"),
        P("row"),
        P("row", "col"),
        P("col"),
        P("col", "row"),
        P("row"),
    )
    return jax.shard_map(
        per_device,
        mesh=mesh,
        in_specs=placed,
        out_specs=(
            P(("dp", "col"), "row"),
            P(("dp", "col"), "row"),
            P("row"),
            P("row"),
            P(None, "row", "col"),
            P(None, "col"),
            P("col", "row"),
            P("row"),
            P("row"),
            P("row"),
            P("row", "col"),
            P("col"),
            P("col", "row"),
            P("row"),
        ),
        check_vma=False,
    )
```

```python
import functools
import math

import jax
import jax.numpy as jnp
from jax import lax
from jax.experimental import pallas as pl
from jax.experimental.pallas import tpu as pltpu
from jax.sharding import PartitionSpec as P

HEAD_DIM = 64
gelu_root = math.sqrt(2.0 / math.pi)
gelu_cubic = 0.044715
BLK = 256
NEG = -1e30
KERNEL_VMEM = 40 * 2**20
WIDE_VMEM = 58 * 2**20


def dot_over(dims, a, b):
    return lax.dot_general(a, b, (dims, ((), ())), preferred_element_type=jnp.float32)


def nn(a, b):
    return dot_over(((1,), (0,)), a, b)


def nt(a, b):
    return dot_over(((1,), (1,)), a, b)


def tn(a, b):
    return dot_over(((0,), (0,)), a, b)


def head_rows(h):
    return slice(h * HEAD_DIM, (h + 1) * HEAD_DIM)


def allowed_tile(i, j, first):
    keys = j * BLK + lax.broadcasted_iota(jnp.int32, (BLK, BLK), 0)
    queries = i * BLK + lax.broadcasted_iota(jnp.int32, (BLK, BLK), 1)
    return (keys >= first) & (keys <= queries)


def turned(x):
    return jnp.transpose(x.astype(jnp.float32)).astype(jnp.bfloat16)


def attend_kernel(heads, blocks, info_ref, q_ref, k_ref, v_ref, first_ref, o_ref, lse_ref, keys_ref):
    i = pl.program_id(0)
    shift = info_ref[0]

    @pl.when(i == 0)
    def _():
        for h in range(heads):
            keys_ref[h] = turned(k_ref[head_rows(h), :])

    first = first_ref[pl.ds(i, 1), :]
    scale = jnp.bfloat16(HEAD_DIM**-0.5)

    def step(j, carry):
        place = pl.ds(pl.multiple_of(lax.rem(j + shift, blocks) * BLK, BLK), BLK)
        allowed = allowed_tile(i, j, first)
        out = []
        for h in range(heads):
            top, total, acc = carry[h]
            scores = nn(keys_ref[h, place, :], q_ref[head_rows(h), :] * scale)
            scores = jnp.where(allowed, scores, NEG)
            new_top = jnp.maximum(top, jnp.max(scores, axis=0, keepdims=True))
            probs = jnp.exp(scores - new_top)
            shrink = jnp.exp(top - new_top)
            total = total * shrink + jnp.sum(probs, axis=0, keepdims=True)
            acc = acc * shrink + nn(v_ref[head_rows(h), place], probs.astype(jnp.bfloat16))
            out.append((new_top, total, acc))
        return tuple(out)

    row = lambda value: jnp.full((1, BLK), value, jnp.float32)
    start = tuple((row(NEG), row(0.0), jnp.zeros((HEAD_DIM, BLK), jnp.float32)) for h in range(heads))
    done = lax.fori_loop(info_ref[1 + i], i + 1, step, start)
    for h, (top, total, acc) in enumerate(done):
        o_ref[head_rows(h), :] = (acc / total).astype(jnp.bfloat16)
        lse_ref[h : h + 1, :] = top + jnp.log(total)


def attend(info, projected, first, heads):
    tokens = projected.shape[1]
    wide, blocks = heads * HEAD_DIM, tokens // BLK
    at = lambda i, s: lax.rem(i + s[0], blocks)
    return pl.pallas_call(
        functools.partial(attend_kernel, heads, blocks),
        grid_spec=pltpu.PrefetchScalarGridSpec(
            num_scalar_prefetch=1,
            grid=(blocks,),
            in_specs=[
                pl.BlockSpec((wide, BLK), lambda i, s: (0, at(i, s))),
                pl.BlockSpec((wide, tokens), lambda i, s: (1, 0)),
                pl.BlockSpec((wide, tokens), lambda i, s: (2, 0)),
                pl.BlockSpec((blocks, BLK), lambda i, s: (0, 0)),
            ],
            out_specs=[
                pl.BlockSpec((wide, BLK), lambda i, s: (0, at(i, s))),
                pl.BlockSpec((8, BLK), lambda i, s: (0, i)),
            ],
            scratch_shapes=[pltpu.VMEM((heads, tokens, HEAD_DIM), jnp.bfloat16)],
        ),
        out_shape=[
            jax.ShapeDtypeStruct((wide, tokens), jnp.bfloat16),
            jax.ShapeDtypeStruct((8, tokens), jnp.float32),
        ],
        compiler_params=pltpu.CompilerParams(vmem_limit_bytes=KERNEL_VMEM),
        cost_estimate=pl.CostEstimate(flops=0, bytes_accessed=0, transcendentals=0),
        name="attend",
    )(info, projected, projected, projected, first)


def attend_back_kernel(
    heads, blocks, info_ref, q_ref, k_ref, v_ref, o_ref, g_ref, lse_ref, first_ref,
    d_ref, keys_ref, values_ref, dk_acc, dv_acc,
):
    i = pl.program_id(0)
    shift = info_ref[0]

    @pl.when(i == 0)
    def _():
        for h in range(heads):
            keys_ref[h] = turned(k_ref[head_rows(h), :])
            values_ref[h] = turned(v_ref[head_rows(h), :])
        dk_acc[...] = jnp.zeros_like(dk_acc)
        dv_acc[...] = jnp.zeros_like(dv_acc)

    first = first_ref[pl.ds(i, 1), :]
    scale = jnp.bfloat16(HEAD_DIM**-0.5)
    centre = [
        jnp.sum(
            g_ref[head_rows(h), :].astype(jnp.float32) * o_ref[head_rows(h), :].astype(jnp.float32),
            axis=0,
            keepdims=True,
        )
        for h in range(heads)
    ]

    def step(j, carry):
        place = pl.ds(pl.multiple_of(lax.rem(j + shift, blocks) * BLK, BLK), BLK)
        allowed = allowed_tile(i, j, first)
        out = []
        for h in range(heads):
            rows = head_rows(h)
            query = q_ref[rows, :] * scale
            grad = g_ref[rows, :]
            scores = jnp.where(allowed, nn(keys_ref[h, place, :], query), NEG)
            probs = jnp.exp(scores - lse_ref[h : h + 1, :])
            prob_grad = nn(values_ref[h, place, :], grad)
            score_grad = (probs * (prob_grad - centre[h])).astype(jnp.bfloat16)
            dv_acc[rows, place] += nt(grad, probs.astype(jnp.bfloat16))
            dk_acc[rows, place] += nt(query, score_grad)
            out.append(carry[h] + nn(k_ref[rows, place], score_grad))
        return tuple(out)

    start = tuple(jnp.zeros((HEAD_DIM, BLK), jnp.float32) for h in range(heads))
    done = lax.fori_loop(info_ref[1 + i], i + 1, step, start)
    mine = pl.ds(pl.multiple_of(lax.rem(i + shift, blocks) * BLK, BLK), BLK)
    for h in range(heads):
        d_ref[head_rows(2 * heads + h), mine] = (done[h] * HEAD_DIM**-0.5).astype(jnp.bfloat16)

    @pl.when(i == blocks - 1)
    def _():
        d_ref[: heads * HEAD_DIM, :] = dk_acc[...].astype(jnp.bfloat16)
        d_ref[heads * HEAD_DIM : 2 * heads * HEAD_DIM, :] = dv_acc[...].astype(jnp.bfloat16)


def attend_back(info, projected, attended, grad, log_totals, first, heads):
    tokens = projected.shape[1]
    wide, blocks = heads * HEAD_DIM, tokens // BLK
    at = lambda i, s: lax.rem(i + s[0], blocks)
    block = pl.BlockSpec((wide, BLK), lambda i, s: (0, at(i, s)))
    whole = lambda part: pl.BlockSpec((wide, tokens), lambda i, s: (part, 0))
    return pl.pallas_call(
        functools.partial(attend_back_kernel, heads, blocks),
        grid_spec=pltpu.PrefetchScalarGridSpec(
            num_scalar_prefetch=1,
            grid=(blocks,),
            in_specs=[
                block,
                whole(1),
                whole(2),
                block,
                block,
                pl.BlockSpec((8, BLK), lambda i, s: (0, i)),
                pl.BlockSpec((blocks, BLK), lambda i, s: (0, 0)),
            ],
            out_specs=pl.BlockSpec((3 * wide, tokens), lambda i, s: (0, 0)),
            scratch_shapes=[
                pltpu.VMEM((heads, tokens, HEAD_DIM), jnp.bfloat16),
                pltpu.VMEM((heads, tokens, HEAD_DIM), jnp.bfloat16),
                pltpu.VMEM((wide, tokens), jnp.float32),
                pltpu.VMEM((wide, tokens), jnp.float32),
            ],
        ),
        out_shape=jax.ShapeDtypeStruct((3 * wide, tokens), jnp.bfloat16),
        compiler_params=pltpu.CompilerParams(vmem_limit_bytes=KERNEL_VMEM),
        cost_estimate=pl.CostEstimate(flops=0, bytes_accessed=0, transcendentals=0),
        name="attend_back",
    )(info, projected, projected, projected, attended, grad, log_totals, first)


def call(body, name, grid, specs, args, out_specs, out_shapes, scalars=None, vmem=KERNEL_VMEM):
    return pl.pallas_call(
        body,
        grid_spec=pltpu.PrefetchScalarGridSpec(
            num_scalar_prefetch=1, grid=grid, in_specs=specs, out_specs=out_specs
        ),
        out_shape=out_shapes,
        compiler_params=pltpu.CompilerParams(vmem_limit_bytes=vmem),
        cost_estimate=pl.CostEstimate(flops=0, bytes_accessed=0, transcendentals=0),
        name=name,
    )(jnp.zeros((1,), jnp.int32) if scalars is None else scalars, *args)


f32 = jnp.float32
bf16 = jnp.bfloat16


def shape(*dims, dtype=jnp.bfloat16):
    return jax.ShapeDtypeStruct(dims, dtype)


def whole_spec(value):
    zeros = (0,) * value.ndim
    return pl.BlockSpec(value.shape, lambda *_: zeros)


def chunks(size, step):
    return [slice(i, min(i + step, size)) for i in range(0, size, step)]


def project(weight, own, other, bias):
    parts, depth, width = weight.shape
    count = own.shape[1]

    def body(_, w_ref, own_ref, other_ref, b_ref, o_ref):
        def run(ref):
            for cols in chunks(count, 256):
                o_ref[:, cols] = (tn(w_ref[0], ref[:, cols]) + b_ref[0]).astype(jnp.bfloat16)

        pl.when(pl.program_id(0) == 0)(lambda: run(own_ref))
        pl.when(pl.program_id(0) == 1)(lambda: run(other_ref))

    return call(
        body, "project", (2, parts),
        [
            pl.BlockSpec((1, depth, width), lambda i, j, _: (j, 0, 0)),
            whole_spec(own),
            whole_spec(other),
            pl.BlockSpec((1, width, 1), lambda i, j, _: (j, 0, 0)),
        ],
        (weight, own, other, bias),
        pl.BlockSpec((width, count), lambda i, j, _: (j, i)),
        shape(parts * width, 2 * count),
    )


def hidden(weight, own, other, bias):
    depth, width = weight.shape
    count = own.shape[1]
    block = 256
    half = count // block

    def body(_, w_ref, own_ref, other_ref, b_ref, act_ref, slope_ref):
        tokens = jnp.where(pl.program_id(0) < half, own_ref[...], other_ref[...])
        for rows in chunks(width, 256):
            pre = tn(w_ref[:, rows], tokens) + b_ref[rows, :]
            square = pre * pre
            bend = jnp.tanh(pre * (gelu_root + (gelu_root * gelu_cubic) * square))
            lift = 0.5 * (1.0 + bend)
            act_ref[rows, :] = (pre * lift).astype(jnp.bfloat16)
            slope_ref[rows, :] = lift + (pre * lift) * (1.0 - bend) * (
                gelu_root + (3.0 * gelu_root * gelu_cubic) * square
            )

    tile = pl.BlockSpec((width, block), lambda i, _: (0, i))
    return call(
        body, "hidden", (2 * half,),
        [
            whole_spec(weight),
            pl.BlockSpec((depth, block), lambda i, _: (0, jnp.minimum(i, half - 1))),
            pl.BlockSpec((depth, block), lambda i, _: (0, jnp.maximum(i - half, 0))),
            whole_spec(bias),
        ],
        (weight, own, other, bias),
        [tile, tile],
        [shape(width, 2 * count), shape(width, 2 * count, dtype=jnp.float32)],
    )


def hidden_back(weight, own, other, slope):
    depth, width = weight.shape
    count = own.shape[1]
    block = 256
    half = count // block

    def body(_, w_ref, own_ref, other_ref, s_ref, o_ref, sum_ref):
        tokens = jnp.where(pl.program_id(0) < half, own_ref[...], other_ref[...])

        @pl.when(pl.program_id(0) == 0)
        def _():
            sum_ref[...] = jnp.zeros_like(sum_ref)

        for rows in chunks(width, 256):
            grad = (tn(w_ref[:, rows], tokens) * s_ref[rows, :]).astype(jnp.bfloat16)
            o_ref[rows, :] = grad
            grad = grad.astype(jnp.float32)
            sum_ref[rows, :] += grad[:, :128] + grad[:, 128:]

    tile = pl.BlockSpec((width, block), lambda i, _: (0, i))
    return call(
        body, "hidden_back", (2 * half,),
        [
            whole_spec(weight),
            pl.BlockSpec((depth, block), lambda i, _: (0, jnp.minimum(i, half - 1))),
            pl.BlockSpec((depth, block), lambda i, _: (0, jnp.maximum(i - half, 0))),
            tile,
        ],
        (weight, own, other, slope),
        [tile, pl.BlockSpec((width, 128), lambda i, _: (0, 0))],
        [shape(width, 2 * count), shape(width, 128, dtype=jnp.float32)],
    )


def mapped(weight, tokens, part, turn, received=None):
    depth, count = weight.shape[0 if turn else 1], tokens.shape[1] // 2
    rows = weight.shape[1 if turn else 0]
    block = rows if turn else 400
    step = 256 if turn else block

    def body(_, w_ref, t_ref, *refs):
        o_ref = refs[-1]
        for cut in chunks(block, step):
            part = tn(w_ref[:, cut], t_ref[...]) if turn else nn(w_ref[cut, :], t_ref[...])
            if received is not None:
                part = part + refs[0][cut, :].astype(jnp.float32)
            o_ref[cut, :] = part.astype(jnp.bfloat16)

    extra = () if received is None else (received,)
    if turn:
        cols = 256
        grid = (count // cols,)
        tile = pl.BlockSpec((rows, cols), lambda i, _: (0, i))
        specs = [
            whole_spec(weight),
            pl.BlockSpec((depth, cols), lambda i, _: (0, part * (count // cols) + i)),
        ] + [tile] * len(extra)
    else:
        grid = (rows // block,)
        tile = pl.BlockSpec((block, count), lambda i, _: (i, 0))
        specs = [
            pl.BlockSpec((block, depth), lambda i, _: (i, 0)),
            pl.BlockSpec((depth, count), lambda i, _: (0, part)),
        ] + [tile] * len(extra)
    return call(body, "mapped", grid, specs, (weight, tokens) + extra, tile, shape(rows, count))


def mapped_three(weight, parts, part, received=None):
    count = parts.shape[1] // 2
    _, rows, width = weight.shape
    block = 400

    def body(_, w_ref, p_ref, *refs):
        total = sum(nn(w_ref[(i + 1) % 3], p_ref[i * width : (i + 1) * width, :]) for i in range(3))
        if received is not None:
            total = total + refs[0][...].astype(jnp.float32)
        refs[-1][...] = total.astype(refs[-1].dtype)

    tile = pl.BlockSpec((block, count), lambda i, _: (i, 0))
    extra = () if received is None else (received,)
    return call(
        body, "mapped_three", (rows // block,),
        [
            pl.BlockSpec((3, block, width), lambda i, _: (0, i, 0)),
            pl.BlockSpec((3 * width, count), lambda i, _: (0, part)),
        ] + [tile] * len(extra),
        (weight, parts) + extra,
        tile,
        shape(rows, count, dtype=jnp.bfloat16 if received is None else jnp.float32),
    )


def attended_back(weight, own, other):
    width, depth = weight.shape
    count = own.shape[1]

    def body(_, w_ref, own_ref, other_ref, o_ref):
        def run(ref):
            for cols in chunks(count, 256):
                o_ref[:, cols] = nn(w_ref[...], ref[:, cols]).astype(jnp.bfloat16)

        pl.when(pl.program_id(0) == 0)(lambda: run(own_ref))
        pl.when(pl.program_id(0) == 1)(lambda: run(other_ref))

    return call(
        body, "attended_back", (2,),
        [whole_spec(weight), whole_spec(own), whole_spec(other)],
        (weight, own, other),
        pl.BlockSpec((width, count), lambda i, _: (0, i)),
        shape(width, 2 * count),
    )


def weight_grad(sources, order, parts):
    rows, count = sources[0][0].shape
    size = rows // parts
    widths = [part[1] for _, _, _, part in sources]

    def body(_, *refs):
        o_ref, at = refs[-1], 0
        for i, width in enumerate(widths):
            own_ref, other_ref, r_ref = refs[3 * i : 3 * i + 3]
            grad = nt(own_ref[0], r_ref[:, :count]) + nt(other_ref[0], r_ref[:, count:])
            o_ref[0, :, at : at + width] = grad.astype(bf16)
            at += width

    tile = pl.BlockSpec((1, size, count), lambda i, s: (s[i], 0, 0))
    specs, args = [], []
    for own, other, right, (place, width) in sources:
        specs += [tile, tile, pl.BlockSpec((width, 2 * count), lambda i, s, place=place: (place, 0))]
        args += [own.reshape(parts, size, count), other.reshape(parts, size, count), right]
    return call(
        body, "weight_grad", order.shape, specs, tuple(args),
        pl.BlockSpec((1, size, sum(widths)), lambda i, s: (i, 0, 0)),
        shape(order.shape[0], size, sum(widths)),
        scalars=order,
    )


SWAP = ((0, 1), (1, 0))
f32 = jnp.float32
bf16 = jnp.bfloat16


def row_swap(value):
    return lax.ppermute(value, "row", SWAP)


def col_swap(value):
    return lax.ppermute(value, "col", SWAP)


def dp_xor(value, mask):
    return lax.ppermute(value, "dp", [(i, i ^ mask) for i in range(lax.axis_size("dp"))])


def after(value, *marks):
    return lax.optimization_barrier((value,) + marks)[0] if marks else value


def ordered(at, first, second, axis):
    return jnp.where(
        at == 0,
        jnp.concatenate([first, second], axis=axis),
        jnp.concatenate([second, first], axis=axis),
    )


def half_of(at, value, axis):
    size = value.shape[axis] // 2
    return jnp.where(
        at == 0,
        lax.slice_in_dim(value, 0, size, axis=axis),
        lax.slice_in_dim(value, size, 2 * size, axis=axis),
    )


def pick(value, at, axis):
    return lax.dynamic_index_in_dim(value, at, axis, keepdims=False)


def plus(a, b):
    return a.astype(f32) + b.astype(f32)


def pad_to(value, size, axis):
    widths = [(0, 0)] * value.ndim
    widths[axis] = (0, size - value.shape[axis])
    return jnp.pad(value, widths)


def head_slots(c, value, tail, axis, most):
    cut = lambda low, high: lax.slice_in_dim(value, low, high, axis=axis)
    size, spare = value.shape[axis], tail.shape[axis]
    less = most - HEAD_DIM
    first = jnp.where(c == 0, cut(0, most), pad_to(cut(spare, spare + less), most, axis))
    second = jnp.where(
        c == 0,
        pad_to(jnp.concatenate([cut(most, size), tail], axis=axis), most, axis),
        pad_to(cut(spare + less, size), most, axis),
    )
    return first, second


def from_slots(c, first, second, axis, spare):
    cut = lambda value, low, high: lax.slice_in_dim(value, low, high, axis=axis)
    most = first.shape[axis]
    less = most - HEAD_DIM
    tail = col_swap(cut(second, less - spare, less))
    return jnp.where(
        c == 0,
        jnp.concatenate([first, cut(second, 0, less - spare)], axis=axis),
        jnp.concatenate([tail, cut(first, 0, less), cut(second, 0, less)], axis=axis),
    )


def put_slots(o_ref, q_ref, t_ref, core, second, most):
    size, spare = q_ref.shape[-1], t_ref.shape[-1]
    less = most - HEAD_DIM

    @pl.when((core == 0) & (second == 0))
    def _():
        o_ref[...] = q_ref[:, 0, :, :most]

    @pl.when((core == 0) & (second == 1))
    def _():
        o_ref[...] = jnp.zeros_like(o_ref)
        o_ref[:, :, : size - most] = q_ref[:, 0, :, most:]
        o_ref[:, :, size - most : size - most + spare] = t_ref[:, 0]

    @pl.when((core == 1) & (second == 0))
    def _():
        o_ref[...] = jnp.zeros_like(o_ref)
        o_ref[:, :, :less] = q_ref[:, 0, :, spare : spare + less]

    @pl.when((core == 1) & (second == 1))
    def _():
        o_ref[...] = jnp.zeros_like(o_ref)
        o_ref[:, :, :less] = q_ref[:, 0, :, spare + less :]


def put_half(o_ref, f_ref, second):
    wide = f_ref.shape[-1] // 2

    @pl.when(second == 0)
    def _():
        o_ref[...] = f_ref[0, :, :wide]

    @pl.when(second == 1)
    def _():
        o_ref[...] = f_ref[0, :, wide:]


def quarters(value):
    return value.reshape(value.shape[:-2] + (4, value.shape[-2] // 4, value.shape[-1]))


def pack(qkv, tail, fc, proj, c, r, at, most):
    rows, size, spare, wide = qkv.shape[1] // 4, qkv.shape[2], tail.shape[2], fc.shape[1] // 2
    scalars = jnp.stack([at, c, r]).astype(jnp.int32)

    def body(s_ref, q_ref, t_ref, f_ref, p_ref, qo_ref, fo_ref, po_ref):
        put_slots(qo_ref, q_ref, t_ref, s_ref[1], 1 - s_ref[2], most)
        put_half(fo_ref, f_ref, 1 - s_ref[2])
        put_half(po_ref, p_ref, 1 - s_ref[2])

    return call(
        body, "pack", (1,),
        [
            pl.BlockSpec((3, 1, rows, size), lambda i, s: (0, s[0], 0, 0)),
            pl.BlockSpec((3, 1, rows, spare), lambda i, s: (0, s[0], 0, 0)),
            pl.BlockSpec((1, rows, 2 * wide), lambda i, s: (s[0], 0, 0)),
            pl.BlockSpec((1, rows, 2 * wide), lambda i, s: (s[0], 0, 0)),
        ],
        tuple(quarters(v) for v in (qkv, tail, fc, proj)),
        [pl.BlockSpec((3, rows, most), lambda i, s: (0, 0, 0))] + [pl.BlockSpec((rows, wide), lambda i, s: (0, 0))] * 2,
        [shape(3, rows, most), shape(rows, wide), shape(rows, wide)],
        scalars=scalars, vmem=WIDE_VMEM,
    )


def own_rows(mine, tail, c, r, width):
    three = mine.ndim == 3
    rows, size = mine.shape[-2] // 4, mine.shape[-1]

    def body(s_ref, m_ref, *refs):
        t_ref, o_ref = refs if three else (None,) + refs
        if three:
            put_slots(o_ref.at[:, 0], m_ref, t_ref, s_ref[1], s_ref[0], width)
        else:
            put_half(o_ref.at[0], m_ref, s_ref[0])

    lead, zero = ((3,), (0,)) if three else ((), ())
    block = lambda width, at: pl.BlockSpec(lead + (1, rows, width), lambda i, s: zero + (at(i, s), 0, 0))
    own = lambda i, s: i
    return call(
        body, "own_rows", (4,),
        [block(size, own)] + ([block(tail.shape[-1], own)] if three else []),
        tuple([quarters(mine)] + ([quarters(tail)] if three else [])),
        block(width, lambda i, s: 4 * s[0] + i), shape(*lead, 8, rows, width),
        scalars=jnp.stack([r, c]).astype(jnp.int32), vmem=WIDE_VMEM,
    )


def all_rows(held, got, r, y, z):
    lead, tile = held.shape[:-3], held.shape[-2:]
    zero = (0,) * len(lead)

    def body(s_ref, h_ref, *refs):
        o_ref = refs[-1]
        place = (pl.program_id(0) // 2 != s_ref[2]) * 2 + (pl.program_id(0) % 2 != s_ref[1])
        for i in range(4):

            @pl.when(place == i)
            def _(i=i):
                o_ref[...] = refs[i][...].reshape(o_ref.shape)

    fetched = pl.BlockSpec(lead + tile, lambda i, s: zero + (0, 0))
    out = pl.pallas_call(
        body,
        grid_spec=pltpu.PrefetchScalarGridSpec(
            num_scalar_prefetch=1,
            grid=(4,),
            in_specs=[pl.BlockSpec(memory_space=pl.ANY)] + [fetched] * 4,
            out_specs=pl.BlockSpec(lead + (1,) + tile, lambda i, s: zero + (4 * (1 - s[0]) + i, 0, 0)),
        ),
        out_shape=shape(*held.shape),
        input_output_aliases={1: 0},
        compiler_params=pltpu.CompilerParams(vmem_limit_bytes=KERNEL_VMEM),
        cost_estimate=pl.CostEstimate(flops=0, bytes_accessed=0, transcendentals=0),
        name="all_rows",
    )(jnp.stack([r, y, z]).astype(jnp.int32), held, *got)
    return out.reshape(lead + (8 * tile[0], tile[1]))


def half_rows(value, at):
    rows, count = value.shape[0] // 2, value.shape[1]

    def body(_, a_ref, o_ref):
        o_ref[...] = a_ref[...].astype(bf16)

    return call(
        body, "half_rows", (count // 256,),
        [pl.BlockSpec((rows, 256), lambda i, s: (s[0], i))], (value,),
        pl.BlockSpec((rows, 256), lambda i, s: (0, i)), shape(rows, count), scalars=at[None].astype(jnp.int32),
    )


def packed_sums(sums_two, sums_one, grad_own, hidden_sums, parts, most):
    width, half = sums_two.shape[1], sums_one.shape[1]

    def body(_, two_ref, one_ref, grad_ref, hid_ref, p_ref, o_ref):
        def over(value):
            ones = jnp.ones((8, value.shape[1]), value.dtype)
            exact = lax.Precision.HIGHEST if value.dtype == f32 else None
            return lax.dot_general(
                ones, value, (((1,), (1,)), ((), ())), preferred_element_type=f32, precision=exact
            )[0:1]

        o_ref[...] = jnp.zeros_like(o_ref)
        for i in range(3):
            o_ref[i : i + 1, :] = over(two_ref[i])
        o_ref[3:4, :half] = over(one_ref[0])
        o_ref[3:4, half:] = over(one_ref[1])
        o_ref[4:5, :half] = over(grad_ref[...])
        o_ref[8:9, :] = over(hid_ref[...])
        o_ref[9:10, :most] = over(p_ref[2 * most :, :])
        o_ref[10:11, :most] = over(p_ref[most : 2 * most, :])

    args = (sums_two, sums_one, grad_own, hidden_sums, parts)
    return call(
        body, "packed_sums", (1,), [whole_spec(v) for v in args], args,
        pl.BlockSpec((16, width), lambda i, s: (0, 0)), shape(16, width, dtype=f32),
    )


def sums_added(a, b, rows):
    def body(_, a_ref, b_ref, o_ref):
        at = lax.broadcasted_iota(jnp.int32, a_ref.shape, 0)
        o_ref[...] = a_ref[...] + jnp.where(at < rows, b_ref[...], 0.0)

    spec = whole_spec(a)
    return call(body, "sums_added", (1,), [spec, spec], (a, b), spec, shape(*a.shape, dtype=f32))


def spread_index(sizes, axis, step, value):
    places = []
    for size in reversed(sizes):
        places.insert(0, step % size)
        step = step // size
    places.insert(axis, value)
    return tuple(places) + (0, 0)


def halved(keep, got, axis, at):
    lead, tile = keep.shape[:-2], keep.shape[-2:]
    rest = lead[:axis] + lead[axis + 1 :]

    def body(_, a_ref, b_ref, c_ref, d_ref, keep_ref, send_ref):
        keep_ref[...] = (a_ref[...].astype(f32) + b_ref[...].astype(f32)).astype(bf16).reshape(keep_ref.shape)
        send_ref[...] = (c_ref[...].astype(f32) + d_ref[...].astype(f32)).astype(bf16).reshape(send_ref.shape)

    ones = (1,) * len(lead)
    mine = pl.BlockSpec(ones + tile, lambda i, s: spread_index(rest, axis, i, s[0]))
    theirs = pl.BlockSpec(ones + tile, lambda i, s: spread_index(rest, axis, i, 1 - s[0]))
    steps = math.prod(rest)
    out = pl.BlockSpec((1,) + tile, lambda i, s: (i, 0, 0))
    first, second = call(
        body, "halved", (steps,), [mine, mine, theirs, theirs], (keep, got, keep, got),
        [out, out], [shape(steps, *tile)] * 2, scalars=at[None].astype(jnp.int32),
    )
    return first.reshape(rest + tile), second.reshape(rest + tile)


def added(a, b):
    def body(_, a_ref, b_ref, o_ref):
        o_ref[...] = (a_ref[...].astype(f32) + b_ref[...].astype(f32)).astype(bf16)

    spec = whole_spec(a)
    return call(body, "added", (1,), [spec, spec], (a, b), spec, shape(*a.shape))


def chosen(flag, a, b):
    def body(s_ref, a_ref, b_ref, o_ref):
        o_ref[...] = jnp.where(s_ref[0] == 1, a_ref[...], b_ref[...])

    spec = whole_spec(a)
    return call(body, "chosen", (1,), [spec, spec], (a, b), spec, shape(*a.shape), scalars=flag[None].astype(jnp.int32))


def paired(at, first, second, axis):
    lead, tile = first.shape[:-2], first.shape[-2:]
    ones = (1,) * len(lead)
    steps = math.prod(lead)

    def body(_, a_ref, b_ref, o_ref):
        @pl.when(pl.program_id(0) == 0)
        def _():
            o_ref[...] = a_ref[...].reshape(o_ref.shape)

        @pl.when(pl.program_id(0) == 1)
        def _():
            o_ref[...] = b_ref[...].reshape(o_ref.shape)

    def place(step):
        return spread_index(lead, len(lead), step, 0)[: len(lead)] + (0, 0)

    out = lambda i, j, s: spread_index(lead, axis, j, jnp.where(i == 0, s[0], 1 - s[0]))
    return call(
        body, "paired", (2, steps),
        [
            pl.BlockSpec(ones + tile, lambda i, j, s: place(jnp.where(i == 0, j, steps - 1))),
            pl.BlockSpec(ones + tile, lambda i, j, s: place(jnp.where(i == 1, j, 0))),
        ],
        (first, second),
        pl.BlockSpec(ones + (1,) + tile, out),
        shape(*lead[:axis], 2, *lead[axis:], *tile),
        scalars=at[None].astype(jnp.int32),
    )


def widened(keep, got, at, y_last):
    rows, width = keep.shape[-2:]

    def body(s_ref, a_ref, b_ref, c_ref, d_ref, o_ref):
        if y_last:
            swap = s_ref[0] == 1
            o_ref[:, :width] = jnp.where(swap, b_ref[0, 0], a_ref[0, 0]).astype(f32)
            o_ref[:, width:] = jnp.where(swap, a_ref[0, 0], b_ref[0, 0]).astype(f32)
        else:
            other = pl.program_id(0) % 2 != s_ref[0]
            o_ref[:, :width] = jnp.where(other, b_ref[0, 0], a_ref[0, 0]).astype(f32)
            o_ref[:, width:] = jnp.where(other, d_ref[0, 0], c_ref[0, 0]).astype(f32)

    tile = (1, 1, rows, width)
    if y_last:
        one = pl.BlockSpec(tile, lambda i, s: (i // 2, i % 2, 0, 0))
        none = pl.BlockSpec(tile, lambda i, s: (0, 0, 0, 0))
        specs = [one, one, none, none]
    else:
        specs = [pl.BlockSpec(tile, lambda i, s, f=f: (f, i // 2, 0, 0)) for f in (0, 0, 1, 1)]
    return call(
        body, "widened", (4,), specs, (keep, got, keep, got),
        pl.BlockSpec((rows, 2 * width), lambda i, s: (i, 0)),
        shape(4 * rows, 2 * width, dtype=f32), scalars=at[None].astype(jnp.int32),
    )


def tails_of(keep, got, at, y_last, most, low, high):
    rows, width = keep.shape[-2:]
    count = width // most

    def body(s_ref, a_ref, b_ref, o_ref):
        second = jnp.where((s_ref[0] == 1) if y_last else (pl.program_id(0) % 2 == s_ref[0]), a_ref[0, 0], b_ref[0, 0])
        for i in range(count):
            o_ref[i, 0] = second[:, i * most + low : i * most + high]

    tile = (1, 1, rows, width)
    where = (lambda i, s: (i // 2, i % 2, 0, 0)) if y_last else (lambda i, s: (1, i // 2, 0, 0))
    return call(
        body, "tails_of", (4,), [pl.BlockSpec(tile, where)] * 2, (keep, got),
        pl.BlockSpec((count, 1, rows, high - low), lambda i, s: (0, i, 0, 0)),
        shape(count, 4, rows, high - low), scalars=at[None].astype(jnp.int32),
    )


def unslotted(keep, got, tails, at, y_last, c, most, size):
    rows, width = keep.shape[-2:]
    count, spare, less = width // most, tails.shape[-1], most - HEAD_DIM

    def body(s_ref, a_ref, b_ref, c_ref, d_ref, t_ref, o_ref):
        if y_last:
            swap = s_ref[0] == 1
            first = jnp.where(swap, b_ref[0, 0], a_ref[0, 0])
            second = jnp.where(swap, a_ref[0, 0], b_ref[0, 0])
        else:
            other = pl.program_id(0) % 2 != s_ref[0]
            first = jnp.where(other, b_ref[0, 0], a_ref[0, 0])
            second = jnp.where(other, d_ref[0, 0], c_ref[0, 0])
        first, second = first.astype(f32), second.astype(f32)

        @pl.when(s_ref[1] == 0)
        def _():
            for i in range(count):
                o_ref[i, :, :most] = first[:, i * most : (i + 1) * most]
                o_ref[i, :, most:] = second[:, i * most : i * most + size - most]

        @pl.when(s_ref[1] == 1)
        def _():
            for i in range(count):
                o_ref[i, :, :spare] = t_ref[i, 0].astype(f32)
                o_ref[i, :, spare : spare + less] = first[:, i * most : i * most + less]
                o_ref[i, :, spare + less :] = second[:, i * most : i * most + less]

    tile = (1, 1, rows, width)
    if y_last:
        one = pl.BlockSpec(tile, lambda i, s: (i // 2, i % 2, 0, 0))
        none = pl.BlockSpec(tile, lambda i, s: (0, 0, 0, 0))
        specs = [one, one, none, none]
    else:
        specs = [pl.BlockSpec(tile, lambda i, s, f=f: (f, i // 2, 0, 0)) for f in (0, 0, 1, 1)]
    return call(
        body, "unslotted", (4,),
        specs + [pl.BlockSpec((count, 1, rows, spare), lambda i, s: (0, i, 0, 0))],
        (keep, got, keep, got, tails),
        pl.BlockSpec((count, rows, size), lambda i, s: (0, i, 0)),
        shape(count, 4 * rows, size, dtype=f32), scalars=jnp.stack([at, c]).astype(jnp.int32),
    )


def side_by_side(own, got, r):
    rows, width = own.shape
    size = rows // 4

    def body(s_ref, a_ref, b_ref, o_ref):
        swap = s_ref[0] == 1
        o_ref[:, :width] = jnp.where(swap, b_ref[...], a_ref[...]).astype(f32)
        o_ref[:, width:] = jnp.where(swap, a_ref[...], b_ref[...]).astype(f32)

    return call(
        body, "side_by_side", (4,),
        [pl.BlockSpec((size, width), lambda i, s: (i, 0))] * 2,
        (own, got),
        pl.BlockSpec((size, 2 * width), lambda i, s: (i, 0)),
        shape(rows, 2 * width, dtype=f32), scalars=r[None].astype(jnp.int32),
    )


TOKENS = 256


def tile_of(rows, at=None):
    if at is None:
        return pl.BlockSpec((rows, TOKENS), lambda i, s: (0, i))
    return pl.BlockSpec((rows, TOKENS), lambda i, s: (at(s), i))


def norm_stats(parts):
    count = sum(part.shape[0] for part in parts)
    center = sum(jnp.sum(part, axis=0, keepdims=True) for part in parts) / count
    spread = sum(jnp.sum((part - center) * (part - center), axis=0, keepdims=True) for part in parts) / count
    return center, lax.rsqrt(spread + 1e-05)


def norm_one(x_own, x_peer, gain, bias, r):
    half, count = x_own.shape

    def body(s_ref, own_ref, peer_ref, g_ref, b_ref, h_ref, stat_ref):
        own, peer = own_ref[...].astype(f32), peer_ref[...].astype(f32)
        parts = [jnp.where(s_ref[0] == 0, own, peer), jnp.where(s_ref[0] == 0, peer, own)]
        center, inverse = norm_stats(parts)
        stat_ref[0:1, :] = center
        stat_ref[1:2, :] = inverse
        for i, part in enumerate(parts):
            rows = slice(i * half, (i + 1) * half)
            h_ref[rows, :] = ((part - center) * inverse * g_ref[rows, :] + b_ref[rows, :]).astype(bf16)

    return call(
        body, "norm_one", (count // TOKENS,),
        [tile_of(half), tile_of(half), whole_spec(gain), whole_spec(bias)],
        (x_own, x_peer, gain, bias),
        [tile_of(2 * half), tile_of(8)],
        [shape(2 * half, count), shape(8, count, dtype=f32)],
        scalars=r[None].astype(jnp.int32),
    )


def norm_two(x_own, x_peer, low, other, out_bias, gain, bias, r):
    half, count = x_own.shape

    def body(s_ref, own_ref, peer_ref, low_ref, other_ref, ob_ref, g_ref, b_ref, x_ref, h_ref, stat_ref):
        own, peer = own_ref[...].astype(f32), peer_ref[...].astype(f32)
        parts = [jnp.where(s_ref[0] == 0, own, peer), jnp.where(s_ref[0] == 0, peer, own)]
        for i in range(2):
            rows = slice(i * half, (i + 1) * half)
            branch = low_ref[rows, :].astype(f32) + other_ref[rows, :].astype(f32) + ob_ref[rows, :]
            parts[i] = parts[i] + branch
            x_ref[rows, :] = parts[i]
        center, inverse = norm_stats(parts)
        stat_ref[0:1, :] = center
        stat_ref[1:2, :] = inverse
        for i, part in enumerate(parts):
            rows = slice(i * half, (i + 1) * half)
            h_ref[rows, :] = ((part - center) * inverse * g_ref[rows, :] + b_ref[rows, :]).astype(bf16)

    full = tile_of(2 * half)
    return call(
        body, "norm_two", (count // TOKENS,),
        [tile_of(half), tile_of(half), full, full, whole_spec(out_bias), whole_spec(gain), whole_spec(bias)],
        (x_own, x_peer, low, other, out_bias, gain, bias),
        [full, full, tile_of(8)],
        [shape(2 * half, count, dtype=f32), shape(2 * half, count), shape(8, count, dtype=f32)],
        scalars=r[None].astype(jnp.int32),
    )


def lanes_summed(ref, at, value, first):
    total = sum(value[:, i : i + 128] for i in range(0, value.shape[1], 128))

    @pl.when(first)
    def _():
        ref[at] = total

    @pl.when(jnp.logical_not(first))
    def _():
        ref[at] += total


def norm_two_back(low, other, grad, x_mid, stats, gain):
    width, count = low.shape

    def body(_, low_ref, other_ref, g_ref, x_ref, stat_ref, gain_ref, mid_ref, branch_ref, sum_ref):
        first = pl.program_id(0) == 0
        incoming = low_ref[...].astype(f32) + other_ref[...].astype(f32)
        inverse = stat_ref[1:2, :]
        normed = (x_ref[...] - stat_ref[0:1, :]) * inverse
        scaled = incoming * gain_ref[...]
        mean = jnp.sum(scaled, axis=0, keepdims=True) / width
        along = jnp.sum(scaled * normed, axis=0, keepdims=True) / width
        mid = g_ref[...].astype(f32) + inverse * (scaled - mean - normed * along)
        mid_ref[...] = mid
        branch = mid.astype(bf16)
        branch_ref[...] = branch
        lanes_summed(sum_ref, 0, incoming * normed, first)
        lanes_summed(sum_ref, 1, incoming, first)
        lanes_summed(sum_ref, 2, branch.astype(f32), first)

    full = tile_of(width)
    return call(
        body, "norm_two_back", (count // TOKENS,),
        [full, full, full, full, tile_of(8), whole_spec(gain)],
        (low, other, grad, x_mid, stats, gain),
        [full, full, pl.BlockSpec((3, width, 128), lambda i, s: (0, 0, 0))],
        [shape(width, count, dtype=f32), shape(width, count), shape(3, width, 128, dtype=f32)],
    )


def norm_one_sums(mine, other, x_own, stats, gain, r):
    half, count = x_own.shape

    def body(_, m_ref, o_ref, x_ref, stat_ref, gain_ref, row_ref, sum_ref):
        first = pl.program_id(0) == 0
        incoming = m_ref[...] + o_ref[...].astype(f32)
        normed = (x_ref[...].astype(f32) - stat_ref[0:1, :]) * stat_ref[1:2, :]
        scaled = incoming * gain_ref[...]
        row_ref[...] = jnp.zeros_like(row_ref)
        row_ref[0:1, :] = jnp.sum(scaled, axis=0, keepdims=True)
        row_ref[1:2, :] = jnp.sum(scaled * normed, axis=0, keepdims=True)
        lanes_summed(sum_ref, 0, incoming * normed, first)
        lanes_summed(sum_ref, 1, incoming, first)

    return call(
        body, "norm_one_sums", (count // TOKENS,),
        [tile_of(half, lambda s: s[0]), tile_of(half), tile_of(half), tile_of(8), whole_spec(gain)],
        (mine, other, x_own, stats, gain),
        [tile_of(8), pl.BlockSpec((2, half, 128), lambda i, s: (0, 0, 0))],
        [shape(8, count, dtype=f32), shape(2, half, 128, dtype=f32)],
        scalars=r[None].astype(jnp.int32),
    )


def norm_one_back(mine, other, x_own, stats, gain, mid_grad, sums, sums_peer, r):
    half, count = x_own.shape

    def body(_, m_ref, o_ref, x_ref, stat_ref, gain_ref, mid_ref, a_ref, b_ref, out_ref):
        inverse = stat_ref[1:2, :]
        normed = (x_ref[...].astype(f32) - stat_ref[0:1, :]) * inverse
        scaled = (m_ref[...] + o_ref[...].astype(f32)) * gain_ref[...]
        means = (a_ref[...] + b_ref[...]) / (2 * half)
        out_ref[...] = mid_ref[...] + inverse * (scaled - means[0:1, :] - normed * means[1:2, :])

    mine_tile = tile_of(half, lambda s: s[0])
    return call(
        body, "norm_one_back", (count // TOKENS,),
        [mine_tile, tile_of(half), tile_of(half), tile_of(8), whole_spec(gain), mine_tile, tile_of(8), tile_of(8)],
        (mine, other, x_own, stats, gain, mid_grad, sums, sums_peer),
        tile_of(half), shape(half, count, dtype=f32), scalars=r[None].astype(jnp.int32),
    )


def block_result(x_mid, part, other, bias, r):
    half, count = other.shape

    def body(_, x_ref, p_ref, o_ref, b_ref, out_ref):
        out_ref[...] = (x_ref[...] + (p_ref[...].astype(f32) + o_ref[...].astype(f32)) + b_ref[...]).astype(bf16)

    mine_tile = tile_of(half, lambda s: s[0])
    return call(
        body, "block_result", (count // TOKENS,),
        [mine_tile, mine_tile, tile_of(half), whole_spec(bias)],
        (x_mid, part, other, bias),
        tile_of(half), shape(half, count), scalars=r[None].astype(jnp.int32),
    )


class Fetch:
    def __init__(self, sent):
        self.got = [row_swap(sent)]

    def more(self, *marks):
        first = after(self.got[0], *marks)
        self.got = [first, dp_xor(first, 1), dp_xor(first, 2)]

    def rest(self, *marks):
        self.got.append(dp_xor(after(self.got[2], *marks), 1))
        return self.got


class Total:
    def __init__(self, sources, r, k, y_first, y_last, *marks):
        self.rows, self.width = sources[0][0].shape[0], sum(part[1] for _, _, _, part in sources)
        self.r, self.k, self.y_first, self.y_last = r, k, y_first, y_last
        self.fast = lax.axis_size("dp") == 8
        tied = lambda marks: [(own, other, after(right, *marks), part) for own, other, right, part in sources]
        if not self.fast:
            self.grad = weight_grad(tied(marks), jnp.arange(4, dtype=jnp.int32), 4)
            return
        self.y, self.lo, self.hi = k % 2, (k // 2) % 2, k // 4
        if y_first:
            send, parts, mask = 2 * (1 - self.y) + jnp.arange(2), 4, 1
            keep = 2 * self.y + jnp.arange(2)
        else:
            send, parts, mask = (1 - self.lo) + 2 * jnp.arange(4), 8, 2
            keep = self.lo + 2 * jnp.arange(4)
        shaped = lambda v: v.reshape(2, 2, self.rows // 8, self.width)
        sent = weight_grad(tied(marks), send.astype(jnp.int32), parts)
        self.got, self.sent = dp_xor(shaped(sent), mask), [sent]
        self.kept = lambda *marks: shaped(weight_grad(tied(marks), keep.astype(jnp.int32), parts))

    def hold(self, *marks):
        if self.fast:
            self.keep = self.kept(*marks)
        return self.marks()

    def marks(self):
        return [self.keep] if self.fast else []

    def sent_marks(self):
        return self.sent if self.fast else []

    def sum_one(self, *marks):
        if self.fast:
            axis, at, mask = (1, self.lo, 2) if self.y_first else (0, self.y, 1)
            self.keep, send = halved(after(self.keep, *marks), self.got, axis, at)
            self.got = dp_xor(send, mask)
            return [self.keep]
        return []

    def sum_two(self, *marks):
        if self.fast:
            self.keep, send = halved(after(self.keep, *marks), self.got, 0, self.hi)
            self.got = dp_xor(send, 4)
            return [self.keep]
        return []

    def sum_three(self, *marks):
        if self.fast:
            cross = [
                (2 * i + j, 2 * (i ^ 1) + (j ^ 1))
                for i in range(lax.axis_size("dp"))
                for j in range(2)
                if i % 2 != j
            ]
            self.keep = added(after(self.keep, *marks), self.got)
            self.got = lax.ppermute(self.keep, ("dp", "row"), cross)
            return [self.keep]
        return []

    def spread_one(self, *marks):
        if self.fast:
            self.keep = chosen(self.y == self.r, after(self.keep, *marks), self.got)
            self.got = dp_xor(self.keep, 4)
            return [self.keep]
        return []

    def spread_two(self, *marks):
        if self.fast:
            self.keep = paired(self.hi, after(self.keep, *marks), self.got, 0)
            self.got = dp_xor(self.keep, 2 if self.y_last else 1)
            return [self.keep]
        return []

    def spread_three(self, *marks):
        if self.fast:
            if self.y_last:
                self.keep = paired(self.lo, after(self.keep, *marks), self.got, 1)
                self.got = dp_xor(self.keep, 1)
            else:
                self.keep = paired(self.y, after(self.keep, *marks), self.got, 0)
                self.got = dp_xor(self.keep, 2)
            return [self.keep]
        return []

    def tail(self, most, spare, *marks):
        if not self.fast:
            return list(marks)
        less = most - HEAD_DIM
        at = self.y if self.y_last else self.lo
        self.keep = after(self.keep, *marks)
        tails = tails_of(self.keep, self.got, at, self.y_last, most, less - spare, less)
        self.tails = col_swap(tails)
        return [tails]

    def slots(self, c, most, spare, *marks):
        less = most - HEAD_DIM
        size = 2 * less + spare
        if not self.fast:
            both = self.result()
            cut = lambda i: [v[:, i * most : (i + 1) * most] for v in both]
            return jnp.stack([from_slots(c, *cut(i), 1, spare).astype(f32) for i in range(self.width // most)])
        at = self.y if self.y_last else self.lo
        keep = after(self.keep, *marks)
        return unslotted(keep, self.got, self.tails, at, self.y_last, c, most, size)

    def wide(self, *marks):
        if self.fast:
            return widened(after(self.keep, *marks), self.got, self.y if self.y_last else self.lo, self.y_last)
        return jnp.concatenate(self.result(*marks), axis=1).astype(f32)

    def result(self, *marks):
        if not self.fast:
            halves = self.grad.reshape(2, self.rows // 2, self.width)
            keep, got = pick(halves, self.r, 0), row_swap(pick(halves, 1 - self.r, 0))
            both = lax.psum(ordered(self.r, keep[None], got[None], 0), "dp")
            return both[0], both[1]
        keep, got = after(self.keep, *marks), self.got
        if self.y_last:
            keep, got = [v.reshape(self.rows // 2, self.width) for v in (keep, got)]
            return jnp.where(self.y == 0, keep, got), jnp.where(self.y == 0, got, keep)
        both = paired(self.lo, keep, got, 2).reshape(2, self.rows // 2, self.width)
        return both[0], both[1]


class Whole:
    def __init__(self, source, r):
        self.source, self.r, self.sums = source, r, {}

    def part(self, mine, *marks):
        own, other, right, part = self.source
        first = 2 * (self.r if mine else 1 - self.r)
        order = (first + jnp.arange(2)).astype(jnp.int32)
        grad = weight_grad([(own, other, after(right, *marks), part)], order, 4)
        self.sums[mine] = lax.psum(grad.reshape(-1, grad.shape[-1]), "dp")
        return [grad]

    def swap(self, *marks):
        self.got = row_swap(after(self.sums[False], *marks))

    def wide(self, *marks):
        return side_by_side(after(self.sums[True], *marks), self.got, self.r)


def hop(value, mask):
    return dp_xor(value, mask) if lax.axis_size("dp") == 8 else None


def hop_added(value, peer, *marks):
    return value if peer is None else sums_added(after(value, *marks), peer, 16)


def per_device(
    block_in,
    out_grad,
    seq_lengths,
    ln1_gain,
    ln1_bias,
    qkv_weight,
    qv_bias,
    out_weight,
    out_bias,
    ln2_gain,
    ln2_bias,
    fc_weight,
    fc_bias,
    proj_weight,
    proj_bias,
):
    n_dp = lax.axis_size("dp")
    r, c, k = lax.axis_index("row"), lax.axis_index("col"), lax.axis_index("dp")
    x_own, grad_own = block_in.T, out_grad.T
    half, tokens = x_own.shape
    heads = 7
    most = heads * HEAD_DIM
    spare = 32
    column = lambda v: v.astype(f32)[:, None]

    y, z = k % 2, (k // 2) % 2
    qkv_tail = col_swap(qkv_weight[:, :, :spare])
    proj_turned = proj_weight.T
    qkv_sent, fc_sent, proj_sent = pack(qkv_weight, qkv_tail, fc_weight, proj_turned, c, r, 2 * z + y, most)
    qkv_fetch = Fetch(qkv_sent)
    x_peer = row_swap(after(x_own, qkv_sent))
    vectors = jnp.stack([ln1_gain, ln1_bias, out_bias, ln2_gain, ln2_bias])
    vectors = ordered(r, vectors, row_swap(vectors), 1).astype(f32)
    gain_one, bias_one, bias_out, gain_two, bias_two = [vectors[i][:, None] for i in range(5)]

    bias_first, bias_second = head_slots(c, qv_bias, col_swap(qv_bias[:, :spare]), 1, most)
    bias_mine = jnp.where(r == 0, bias_first, bias_second).astype(f32)
    bias_mine = jnp.stack([bias_mine[0], jnp.zeros_like(bias_mine[0]), bias_mine[1]])[:, :, None]

    out_first, out_second = head_slots(c, after(out_weight, qkv_sent), col_swap(out_weight[:spare]), 0, most)
    out_mine = jnp.where(r == 0, out_first, out_second)
    out_sent = jnp.where(r == 0, out_second, out_first)
    fc_bias_mine = column(half_of(r, fc_bias, 0))
    gain_half, proj_bias_half = column(ln1_gain), column(proj_bias)
    ff_size = fc_weight.shape[1] // 2
    qkv_full = own_rows(after(qkv_weight, out_sent), qkv_tail, c, r, most)
    qkv_fetch.more(qkv_full)
    fc_full = own_rows(after(fc_weight, qkv_fetch.got[0]), None, c, r, ff_size)
    qkv_fetch.rest(fc_full)
    proj_full = own_rows(after(proj_turned, fc_full, *qkv_fetch.got[1:3]), None, c, r, ff_size)

    lengths = seq_lengths[0]
    group = 2 * tokens
    places = jnp.arange(group, dtype=jnp.int32)
    ends = jnp.cumsum(lengths, dtype=jnp.int32)
    first = jnp.sum(
        jnp.where(ends[None, :] <= places[:, None], lengths[None, :], 0), axis=1, dtype=jnp.int32
    ).reshape(group // BLK, BLK)
    info = jnp.concatenate([(c * (tokens // BLK))[None].astype(jnp.int32), first[:, 0] // BLK])

    columns = [gain_one, bias_one, bias_out, gain_two, bias_two, bias_mine, fc_bias_mine, gain_half, proj_bias_half]
    h_one, stats_one = norm_one(after(x_own, proj_full, info, *columns), x_peer, gain_one, bias_one, r)
    h_one_peer = col_swap(h_one)
    fc_fetch = Fetch(after(fc_sent, h_one))
    proj_fetch = Fetch(after(proj_sent, h_one))
    out_got = row_swap(after(out_sent, h_one))
    grad_got = row_swap(after(grad_own, h_one))
    qkv_full = all_rows(after(qkv_full, h_one), qkv_fetch.got, r, y, z)
    projected = project(qkv_full, h_one, h_one_peer, bias_mine)
    fc_fetch.more(projected)
    proj_fetch.more(projected)
    out_full = ordered(r, after(out_mine, projected), out_got, 1)
    mark = [out_full, fc_fetch.got[0], proj_fetch.got[0]]
    attended, log_totals = attend(info, after(projected, *mark), first, heads)
    fc_fetch.rest(attended)
    proj_fetch.rest(attended)
    other = mapped(out_full, after(attended, *fc_fetch.got[1:3], *proj_fetch.got[1:3]), 1, True)
    low = mapped(out_full, attended, 0, True, col_swap(other))
    branch_other = row_swap(low)
    fc_full = all_rows(after(fc_full, low), fc_fetch.got, r, y, z)
    proj_full = all_rows(after(proj_full, fc_full), proj_fetch.got, r, y, z)
    x_mid, h_two, stats_two = norm_two(x_own, x_peer, after(low, proj_full), branch_other, bias_out, gain_two, bias_two, r)
    h_two_peer = col_swap(h_two)
    activated, slope = hidden(fc_full, h_two, h_two_peer, fc_bias_mine)
    grad_full = paired(r, after(grad_own, activated), grad_got, 0).reshape(2 * half, tokens)
    grad_peer = col_swap(grad_full)

    mark = [grad_peer]
    pre_grad, hidden_sums = hidden_back(proj_full, grad_full, grad_peer, slope)
    mark = [pre_grad]
    h_two_other = mapped(fc_full, after(pre_grad, *mark), 1, False)
    mark = [h_two_other]
    proj_total = Total([(grad_full, grad_peer, activated, (0, ff_size))], r, k, True, False, *mark)
    mark = proj_total.sent_marks()
    low = mapped(fc_full, after(pre_grad, *mark), 0, False, col_swap(h_two_other))
    low_other, mark = row_swap(low), [low]
    fc_total = Total([(h_two, h_two_peer, pre_grad, (0, ff_size))], r, k, False, True, *mark)
    mark = fc_total.sent_marks()
    mark = fc_total.hold(*mark)
    mark = proj_total.hold(*mark)
    mark = proj_total.sum_one(*mark)
    mid_grad, branch_grad, sums_two = norm_two_back(
        after(low, *mark), low_other, grad_full, x_mid, stats_two, gain_two
    )
    branch_peer, mark = col_swap(branch_grad), [branch_grad]
    mark = fc_total.sum_one(*mark)
    attended_grad = attended_back(out_full, after(branch_grad, *mark), branch_peer)
    mark = [attended_grad]
    parts = attend_back(info, projected, attended, after(attended_grad, *mark), log_totals, first, heads)
    mark = [parts]
    kv_total = Total([(h_one, h_one_peer, parts, (0, 2 * most))], r, k, True, False, *mark)
    mark = kv_total.sent_marks()
    three_other = mapped_three(qkv_full, after(parts, *mark), 1)
    mark = [three_other]
    mark = proj_total.sum_two(*mark)
    mark = fc_total.sum_two(*mark)
    oq_total = Total([(branch_grad, branch_peer, attended, (0, most)), (h_one, h_one_peer, parts, (2, most))], r, k, True, True, *mark)
    mark = oq_total.sent_marks()
    mark = oq_total.hold(*mark)
    mine = mapped_three(qkv_full, after(parts, *mark), 0, col_swap(three_other))
    mark = [mine]
    mark = kv_total.hold(*mark)
    send = half_rows(after(mine, *mark), 1 - r)
    one_other, mark = row_swap(send), [send]
    mark = kv_total.sum_one(*mark)
    mark = proj_total.sum_three(*mark)
    mark = oq_total.sum_one(*mark)
    mark = fc_total.sum_three(*mark)
    mark = kv_total.sum_two(*mark)
    mark = proj_total.spread_one(*mark)
    mark = oq_total.sum_two(*mark)
    mark = kv_total.sum_three(*mark)
    sums, sums_one = norm_one_sums(after(mine, *mark), one_other, x_own, stats_one, gain_half, r)
    sums_peer, mark = row_swap(sums), [sums]
    packed = packed_sums(sums_two, after(sums_one, *mark), grad_own, hidden_sums, parts, most)
    packed_peer, mark = col_swap(packed), [packed]
    mark = fc_total.spread_one(*mark)
    mark = oq_total.sum_three(*mark)
    packed = sums_added(after(packed, *mark), packed_peer, 8)
    packed_peer, mark = hop(packed, 2), [packed]
    x_grad = norm_one_back(after(mine, *mark), one_other, x_own, stats_one, gain_half, mid_grad, sums, sums_peer, r)
    mark = [x_grad]
    mark = oq_total.spread_one(*mark)
    packed = hop_added(packed, packed_peer, *mark)
    packed_peer, mark = hop(packed, 1), [packed]
    mark = proj_total.spread_two(*mark)
    mark = kv_total.spread_one(*mark)
    mark = fc_total.spread_two(*mark)
    part_other = mapped(proj_full, after(activated, *mark), 1, False)
    mark = [part_other]
    packed = hop_added(packed, packed_peer, *mark)
    packed_peer, mark = hop(packed, 4), [packed]
    mark = kv_total.spread_two(*mark)
    mark = oq_total.spread_two(*mark)
    mark = proj_total.spread_three(*mark)
    mark = kv_total.spread_three(*mark)
    mark = oq_total.spread_three(*mark)
    packed = hop_added(packed, packed_peer, *mark)
    if n_dp != 8:
        for i in range(n_dp.bit_length() - 1):
            packed = sums_added(packed, dp_xor(packed, 1 << i), 16)
    packed_peer, mark = row_swap(packed), [packed]
    mark = fc_total.spread_three(*mark)
    packed_peer = after(packed_peer, *mark)
    mark = [packed_peer]
    proj_part = mapped(proj_full, after(activated, *mark), 0, False, col_swap(part_other))
    mark = [proj_part]
    mark = kv_total.tail(most, spare, *mark)
    mark = oq_total.tail(most, spare, *mark)
    send = half_rows(after(proj_part, *mark), 1 - r)
    block_other, mark = row_swap(send), [send]
    whole = oq_total.slots(c, most, spare, *mark)
    out_weight_grad = whole[0]
    q_weight_grad = whole[1]
    mark = [whole]
    whole = kv_total.slots(c, most, spare, *mark)
    k_weight_grad = whole[0]
    v_weight_grad = whole[1]
    mark = [whole]
    block_out = block_result(after(x_mid, *mark), proj_part, block_other, proj_bias_half, r)
    mark = [block_out]
    proj_weight_grad = proj_total.wide(*mark).T
    mark = [proj_weight_grad]
    fc_weight_grad = fc_total.wide(*mark)
    mark = [fc_weight_grad]

    own = half_of(r, packed, 1)
    fc_bias_grad = ordered(r, packed[8], packed_peer[8], 0)
    qv_mine, qv_peer = packed[9:11, :most], packed_peer[9:11, :most]
    qv_bias_grad = from_slots(
        c, jnp.where(r == 0, qv_mine, qv_peer), jnp.where(r == 0, qv_peer, qv_mine), 1, spare
    )
    qkv_weight_grad = jnp.stack([q_weight_grad, k_weight_grad, v_weight_grad])
    out_weight_grad = out_weight_grad.T
    return (
        block_out.T,
        x_grad.T,
        packed[3, :half],
        packed[3, half:],
        qkv_weight_grad,
        qv_bias_grad,
        out_weight_grad,
        own[2],
        own[0],
        own[1],
        fc_weight_grad,
        fc_bias_grad,
        proj_weight_grad,
        packed[4, :half],
    )


def solution(mesh):
    placed = (
        P(("dp", "col"), "row"),
        P(("dp", "col"), "row"),
        P("dp", None),
        P("row"),
        P("row"),
        P(None, "row", "col"),
        P(None, "col"),
        P("col", "row"),
        P("row"),
        P("row"),
        P("row"),
        P("row", "col"),
        P("col"),
        P("col", "row"),
        P("row"),
    )
    return jax.shard_map(
        per_device,
        mesh=mesh,
        in_specs=placed,
        out_specs=(
            P(("dp", "col"), "row"),
            P(("dp", "col"), "row"),
            P("row"),
            P("row"),
            P(None, "row", "col"),
            P(None, "col"),
            P("col", "row"),
            P("row"),
            P("row"),
            P("row"),
            P("row", "col"),
            P("col"),
            P("col", "row"),
            P("row"),
        ),
        check_vma=False,
    )
```

```python
import functools
import math

import jax
import jax.numpy as jnp
from jax import lax
from jax.experimental import pallas as pl
from jax.experimental.pallas import tpu as pltpu
from jax.sharding import PartitionSpec as P

HEAD_DIM = 64
gelu_root = math.sqrt(2.0 / math.pi)
gelu_cubic = 0.044715
BLK = 256
NEG = -1e30
KERNEL_VMEM = 40 * 2**20
WIDE_VMEM = 58 * 2**20


def dot_over(dims, a, b):
    return lax.dot_general(a, b, (dims, ((), ())), preferred_element_type=jnp.float32)


def nn(a, b):
    return dot_over(((1,), (0,)), a, b)


def nt(a, b):
    return dot_over(((1,), (1,)), a, b)


def tn(a, b):
    return dot_over(((0,), (0,)), a, b)


def head_rows(h):
    return slice(h * HEAD_DIM, (h + 1) * HEAD_DIM)


def allowed_tile(i, j, first):
    keys = j * BLK + lax.broadcasted_iota(jnp.int32, (BLK, BLK), 0)
    queries = i * BLK + lax.broadcasted_iota(jnp.int32, (BLK, BLK), 1)
    return (keys >= first) & (keys <= queries)


def turned(x):
    return jnp.transpose(x.astype(jnp.float32)).astype(jnp.bfloat16)


def attend_kernel(heads, blocks, info_ref, q_ref, k_ref, v_ref, first_ref, o_ref, lse_ref, keys_ref):
    i = pl.program_id(0)
    shift = info_ref[0]

    @pl.when(i == 0)
    def _():
        for h in range(heads):
            keys_ref[h] = turned(k_ref[head_rows(h), :])

    first = first_ref[pl.ds(i, 1), :]
    scale = jnp.bfloat16(HEAD_DIM**-0.5)

    def step(j, carry):
        place = pl.ds(pl.multiple_of(lax.rem(j + shift, blocks) * BLK, BLK), BLK)
        allowed = allowed_tile(i, j, first)
        out = []
        for h in range(heads):
            top, total, acc = carry[h]
            scores = nn(keys_ref[h, place, :], q_ref[head_rows(h), :] * scale)
            scores = jnp.where(allowed, scores, NEG)
            new_top = jnp.maximum(top, jnp.max(scores, axis=0, keepdims=True))
            probs = jnp.exp(scores - new_top)
            shrink = jnp.exp(top - new_top)
            total = total * shrink + jnp.sum(probs, axis=0, keepdims=True)
            acc = acc * shrink + nn(v_ref[head_rows(h), place], probs.astype(jnp.bfloat16))
            out.append((new_top, total, acc))
        return tuple(out)

    row = lambda value: jnp.full((1, BLK), value, jnp.float32)
    start = tuple((row(NEG), row(0.0), jnp.zeros((HEAD_DIM, BLK), jnp.float32)) for h in range(heads))
    done = lax.fori_loop(info_ref[1 + i], i + 1, step, start)
    for h, (top, total, acc) in enumerate(done):
        o_ref[head_rows(h), :] = (acc / total).astype(jnp.bfloat16)
        lse_ref[h : h + 1, :] = top + jnp.log(total)


def attend(info, projected, first, heads):
    tokens = projected.shape[1]
    wide, blocks = heads * HEAD_DIM, tokens // BLK
    at = lambda i, s: lax.rem(i + s[0], blocks)
    return pl.pallas_call(
        functools.partial(attend_kernel, heads, blocks),
        grid_spec=pltpu.PrefetchScalarGridSpec(
            num_scalar_prefetch=1,
            grid=(blocks,),
            in_specs=[
                pl.BlockSpec((wide, BLK), lambda i, s: (0, at(i, s))),
                pl.BlockSpec((wide, tokens), lambda i, s: (1, 0)),
                pl.BlockSpec((wide, tokens), lambda i, s: (2, 0)),
                pl.BlockSpec((blocks, BLK), lambda i, s: (0, 0)),
            ],
            out_specs=[
                pl.BlockSpec((wide, BLK), lambda i, s: (0, at(i, s))),
                pl.BlockSpec((8, BLK), lambda i, s: (0, i)),
            ],
            scratch_shapes=[pltpu.VMEM((heads, tokens, HEAD_DIM), jnp.bfloat16)],
        ),
        out_shape=[
            jax.ShapeDtypeStruct((wide, tokens), jnp.bfloat16),
            jax.ShapeDtypeStruct((8, tokens), jnp.float32),
        ],
        compiler_params=pltpu.CompilerParams(vmem_limit_bytes=KERNEL_VMEM),
        cost_estimate=pl.CostEstimate(flops=0, bytes_accessed=0, transcendentals=0),
        name="attend",
    )(info, projected, projected, projected, first)


def attend_back_kernel(
    heads, blocks, info_ref, q_ref, k_ref, v_ref, o_ref, g_ref, lse_ref, first_ref,
    d_ref, keys_ref, values_ref, dk_acc, dv_acc,
):
    i = pl.program_id(0)
    shift = info_ref[0]

    @pl.when(i == 0)
    def _():
        for h in range(heads):
            keys_ref[h] = turned(k_ref[head_rows(h), :])
            values_ref[h] = turned(v_ref[head_rows(h), :])
        dk_acc[...] = jnp.zeros_like(dk_acc)
        dv_acc[...] = jnp.zeros_like(dv_acc)

    first = first_ref[pl.ds(i, 1), :]
    scale = jnp.bfloat16(HEAD_DIM**-0.5)
    centre = [
        jnp.sum(
            g_ref[head_rows(h), :].astype(jnp.float32) * o_ref[head_rows(h), :].astype(jnp.float32),
            axis=0,
            keepdims=True,
        )
        for h in range(heads)
    ]

    def step(j, carry):
        place = pl.ds(pl.multiple_of(lax.rem(j + shift, blocks) * BLK, BLK), BLK)
        allowed = allowed_tile(i, j, first)
        out = []
        for h in range(heads):
            rows = head_rows(h)
            query = q_ref[rows, :] * scale
            grad = g_ref[rows, :]
            scores = jnp.where(allowed, nn(keys_ref[h, place, :], query), NEG)
            probs = jnp.exp(scores - lse_ref[h : h + 1, :])
            prob_grad = nn(values_ref[h, place, :], grad)
            score_grad = (probs * (prob_grad - centre[h])).astype(jnp.bfloat16)
            dv_acc[rows, place] += nt(grad, probs.astype(jnp.bfloat16))
            dk_acc[rows, place] += nt(query, score_grad)
            out.append(carry[h] + nn(k_ref[rows, place], score_grad))
        return tuple(out)

    start = tuple(jnp.zeros((HEAD_DIM, BLK), jnp.float32) for h in range(heads))
    done = lax.fori_loop(info_ref[1 + i], i + 1, step, start)
    mine = pl.ds(pl.multiple_of(lax.rem(i + shift, blocks) * BLK, BLK), BLK)
    for h in range(heads):
        d_ref[head_rows(2 * heads + h), mine] = (done[h] * HEAD_DIM**-0.5).astype(jnp.bfloat16)

    @pl.when(i == blocks - 1)
    def _():
        d_ref[: heads * HEAD_DIM, :] = dk_acc[...].astype(jnp.bfloat16)
        d_ref[heads * HEAD_DIM : 2 * heads * HEAD_DIM, :] = dv_acc[...].astype(jnp.bfloat16)


def attend_back(info, projected, attended, grad, log_totals, first, heads):
    tokens = projected.shape[1]
    wide, blocks = heads * HEAD_DIM, tokens // BLK
    at = lambda i, s: lax.rem(i + s[0], blocks)
    block = pl.BlockSpec((wide, BLK), lambda i, s: (0, at(i, s)))
    whole = lambda part: pl.BlockSpec((wide, tokens), lambda i, s: (part, 0))
    return pl.pallas_call(
        functools.partial(attend_back_kernel, heads, blocks),
        grid_spec=pltpu.PrefetchScalarGridSpec(
            num_scalar_prefetch=1,
            grid=(blocks,),
            in_specs=[
                block,
                whole(1),
                whole(2),
                block,
                block,
                pl.BlockSpec((8, BLK), lambda i, s: (0, i)),
                pl.BlockSpec((blocks, BLK), lambda i, s: (0, 0)),
            ],
            out_specs=pl.BlockSpec((3 * wide, tokens), lambda i, s: (0, 0)),
            scratch_shapes=[
                pltpu.VMEM((heads, tokens, HEAD_DIM), jnp.bfloat16),
                pltpu.VMEM((heads, tokens, HEAD_DIM), jnp.bfloat16),
                pltpu.VMEM((wide, tokens), jnp.float32),
                pltpu.VMEM((wide, tokens), jnp.float32),
            ],
        ),
        out_shape=jax.ShapeDtypeStruct((3 * wide, tokens), jnp.bfloat16),
        compiler_params=pltpu.CompilerParams(vmem_limit_bytes=KERNEL_VMEM),
        cost_estimate=pl.CostEstimate(flops=0, bytes_accessed=0, transcendentals=0),
        name="attend_back",
    )(info, projected, projected, projected, attended, grad, log_totals, first)


ROW, COL, LOW_Y, LOW_Z, HIGH_Z, QUARTER, PEER, SAME = range(8)


class Here:
    places = None


def call(body, name, grid, specs, args, out_specs, out_shapes, vmem=KERNEL_VMEM):
    return pl.pallas_call(
        body,
        grid_spec=pltpu.PrefetchScalarGridSpec(
            num_scalar_prefetch=1, grid=grid, in_specs=specs, out_specs=out_specs
        ),
        out_shape=out_shapes,
        compiler_params=pltpu.CompilerParams(vmem_limit_bytes=vmem),
        cost_estimate=pl.CostEstimate(flops=0, bytes_accessed=0, transcendentals=0),
        name=name,
    )(Here.places, *args)


f32 = jnp.float32
bf16 = jnp.bfloat16


def shape(*dims, dtype=jnp.bfloat16):
    return jax.ShapeDtypeStruct(dims, dtype)


def whole_spec(value):
    zeros = (0,) * value.ndim
    return pl.BlockSpec(value.shape, lambda *_: zeros)


def chunks(size, step):
    return [slice(i, min(i + step, size)) for i in range(0, size, step)]


def project(weight, own, other, bias):
    parts, depth, width = weight.shape
    count = own.shape[1]

    def body(_, w_ref, own_ref, other_ref, b_ref, o_ref):
        def run(ref):
            for cols in chunks(count, 256):
                o_ref[:, cols] = (tn(w_ref[0], ref[:, cols]) + b_ref[0]).astype(jnp.bfloat16)

        pl.when(pl.program_id(0) == 0)(lambda: run(own_ref))
        pl.when(pl.program_id(0) == 1)(lambda: run(other_ref))

    return call(
        body, "project", (2, parts),
        [
            pl.BlockSpec((1, depth, width), lambda i, j, _: (j, 0, 0)),
            whole_spec(own),
            whole_spec(other),
            pl.BlockSpec((1, width, 1), lambda i, j, _: (j, 0, 0)),
        ],
        (weight, own, other, bias),
        pl.BlockSpec((width, count), lambda i, j, _: (j, i)),
        shape(parts * width, 2 * count),
    )


def hidden(weight, own, other, columns):
    depth, width = weight.shape
    count = own.shape[1]
    block = 256
    half = count // block

    def body(_, w_ref, own_ref, other_ref, b_ref, act_ref, slope_ref):
        tokens = jnp.where(pl.program_id(0) < half, own_ref[...], other_ref[...])
        for rows in chunks(width, 256):
            pre = tn(w_ref[:, rows], tokens) + b_ref[rows, 5:6]
            square = pre * pre
            bend = jnp.tanh(pre * (gelu_root + (gelu_root * gelu_cubic) * square))
            lift = 0.5 * (1.0 + bend)
            act_ref[rows, :] = (pre * lift).astype(jnp.bfloat16)
            slope_ref[rows, :] = lift + (pre * lift) * (1.0 - bend) * (
                gelu_root + (3.0 * gelu_root * gelu_cubic) * square
            )

    tile = pl.BlockSpec((width, block), lambda i, _: (0, i))
    return call(
        body, "hidden", (2 * half,),
        [
            whole_spec(weight),
            pl.BlockSpec((depth, block), lambda i, _: (0, jnp.minimum(i, half - 1))),
            pl.BlockSpec((depth, block), lambda i, _: (0, jnp.maximum(i - half, 0))),
            whole_spec(columns),
        ],
        (weight, own, other, columns),
        [tile, tile],
        [shape(width, 2 * count), shape(width, 2 * count, dtype=jnp.float32)],
    )


def hidden_back(weight, own, other, slope):
    depth, width = weight.shape
    count = own.shape[1]
    block = 256
    half = count // block

    def body(_, w_ref, own_ref, other_ref, s_ref, o_ref, sum_ref):
        tokens = jnp.where(pl.program_id(0) < half, own_ref[...], other_ref[...])

        @pl.when(pl.program_id(0) == 0)
        def _():
            sum_ref[...] = jnp.zeros_like(sum_ref)

        for rows in chunks(width, 256):
            grad = (tn(w_ref[:, rows], tokens) * s_ref[rows, :]).astype(jnp.bfloat16)
            o_ref[rows, :] = grad
            grad = grad.astype(jnp.float32)
            sum_ref[rows, :] += grad[:, :128] + grad[:, 128:]

    tile = pl.BlockSpec((width, block), lambda i, _: (0, i))
    return call(
        body, "hidden_back", (2 * half,),
        [
            whole_spec(weight),
            pl.BlockSpec((depth, block), lambda i, _: (0, jnp.minimum(i, half - 1))),
            pl.BlockSpec((depth, block), lambda i, _: (0, jnp.maximum(i - half, 0))),
            tile,
        ],
        (weight, own, other, slope),
        [tile, pl.BlockSpec((width, 128), lambda i, _: (0, 0))],
        [shape(width, 2 * count), shape(width, 128, dtype=jnp.float32)], vmem=WIDE_VMEM,
    )


def mapped(weight, tokens, part, turn, received=None):
    depth, count = weight.shape[0 if turn else 1], tokens.shape[1] // 2
    rows = weight.shape[1 if turn else 0]
    block = rows if turn else 400
    step = 256 if turn else block

    def body(_, w_ref, t_ref, *refs):
        o_ref = refs[-1]
        for cut in chunks(block, step):
            part = tn(w_ref[:, cut], t_ref[...]) if turn else nn(w_ref[cut, :], t_ref[...])
            if received is not None:
                part = part + refs[0][cut, :].astype(jnp.float32)
            o_ref[cut, :] = part.astype(jnp.bfloat16)

    extra = () if received is None else (received,)
    if turn:
        cols = 256
        grid = (count // cols,)
        tile = pl.BlockSpec((rows, cols), lambda i, _: (0, i))
        specs = [
            whole_spec(weight),
            pl.BlockSpec((depth, cols), lambda i, _: (0, part * (count // cols) + i)),
        ] + [tile] * len(extra)
    else:
        grid = (rows // block,)
        tile = pl.BlockSpec((block, count), lambda i, _: (i, 0))
        specs = [
            pl.BlockSpec((block, depth), lambda i, _: (i, 0)),
            pl.BlockSpec((depth, count), lambda i, _: (0, part)),
        ] + [tile] * len(extra)
    return call(body, "mapped", grid, specs, (weight, tokens) + extra, tile, shape(rows, count))


def mapped_three(weight, parts, part, received=None):
    count = parts.shape[1] // 2
    _, rows, width = weight.shape
    block = 400

    def body(_, w_ref, p_ref, *refs):
        total = sum(nn(w_ref[(i + 1) % 3], p_ref[i * width : (i + 1) * width, :]) for i in range(3))
        if received is not None:
            total = total + refs[0][...].astype(jnp.float32)
        refs[-1][...] = total.astype(refs[-1].dtype)

    tile = pl.BlockSpec((block, count), lambda i, _: (i, 0))
    extra = () if received is None else (received,)
    return call(
        body, "mapped_three", (rows // block,),
        [
            pl.BlockSpec((3, block, width), lambda i, _: (0, i, 0)),
            pl.BlockSpec((3 * width, count), lambda i, _: (0, part)),
        ] + [tile] * len(extra),
        (weight, parts) + extra,
        tile,
        shape(rows, count, dtype=jnp.bfloat16 if received is None else jnp.float32),
    )


def attended_back(weight, own, other):
    width, depth = weight.shape
    count = own.shape[1]

    def body(_, w_ref, own_ref, other_ref, o_ref):
        def run(ref):
            for cols in chunks(count, 256):
                o_ref[:, cols] = nn(w_ref[...], ref[:, cols]).astype(jnp.bfloat16)

        pl.when(pl.program_id(0) == 0)(lambda: run(own_ref))
        pl.when(pl.program_id(0) == 1)(lambda: run(other_ref))

    return call(
        body, "attended_back", (2,),
        [whole_spec(weight), whole_spec(own), whole_spec(other)],
        (weight, own, other),
        pl.BlockSpec((width, count), lambda i, _: (0, i)),
        shape(width, 2 * count),
    )


def weight_grad(sources, place_of, blocks, parts):
    rows, count = sources[0][0].shape
    size = rows // parts
    widths = [part[1] for _, _, _, part in sources]

    def body(_, *refs):
        o_ref, at = refs[-1], 0
        for i, width in enumerate(widths):
            own_ref, other_ref, r_ref = refs[3 * i : 3 * i + 3]
            grad = nt(own_ref[0], r_ref[:, :count]) + nt(other_ref[0], r_ref[:, count:])
            o_ref[0, :, at : at + width] = grad.astype(bf16)
            at += width

    tile = pl.BlockSpec((1, size, count), lambda i, s: (place_of(i, s), 0, 0))
    specs, args = [], []
    for own, other, right, (place, width) in sources:
        specs += [tile, tile, pl.BlockSpec((width, 2 * count), lambda i, s, place=place: (place, 0))]
        args += [own.reshape(parts, size, count), other.reshape(parts, size, count), right]
    return call(
        body, "weight_grad", (blocks,), specs, tuple(args),
        pl.BlockSpec((1, size, sum(widths)), lambda i, s: (i, 0, 0)),
        shape(blocks, size, sum(widths)), vmem=WIDE_VMEM,
    )


SWAP = ((0, 1), (1, 0))
f32 = jnp.float32
bf16 = jnp.bfloat16


def row_swap(value):
    return lax.ppermute(value, "row", SWAP)


def col_swap(value):
    return lax.ppermute(value, "col", SWAP)


def dp_xor(value, mask):
    return lax.ppermute(value, "dp", [(i, i ^ mask) for i in range(lax.axis_size("dp"))])


def after(value, *marks):
    return lax.optimization_barrier((value,) + marks)[0] if marks else value


def ordered(at, first, second, axis):
    return jnp.where(
        at == 0,
        jnp.concatenate([first, second], axis=axis),
        jnp.concatenate([second, first], axis=axis),
    )


def half_of(at, value, axis):
    size = value.shape[axis] // 2
    return jnp.where(
        at == 0,
        lax.slice_in_dim(value, 0, size, axis=axis),
        lax.slice_in_dim(value, size, 2 * size, axis=axis),
    )


def pick(value, at, axis):
    return lax.dynamic_index_in_dim(value, at, axis, keepdims=False)


def plus(a, b):
    return a.astype(f32) + b.astype(f32)


def pad_to(value, size, axis):
    widths = [(0, 0)] * value.ndim
    widths[axis] = (0, size - value.shape[axis])
    return jnp.pad(value, widths)


def head_slots(c, value, tail, axis, most):
    cut = lambda low, high: lax.slice_in_dim(value, low, high, axis=axis)
    size, spare = value.shape[axis], tail.shape[axis]
    less = most - HEAD_DIM
    first = jnp.where(c == 0, cut(0, most), pad_to(cut(spare, spare + less), most, axis))
    second = jnp.where(
        c == 0,
        pad_to(jnp.concatenate([cut(most, size), tail], axis=axis), most, axis),
        pad_to(cut(spare + less, size), most, axis),
    )
    return first, second


def from_slots(c, first, second, axis, spare):
    cut = lambda value, low, high: lax.slice_in_dim(value, low, high, axis=axis)
    most = first.shape[axis]
    less = most - HEAD_DIM
    tail = col_swap(cut(second, less - spare, less))
    return jnp.where(
        c == 0,
        jnp.concatenate([first, cut(second, 0, less - spare)], axis=axis),
        jnp.concatenate([tail, cut(first, 0, less), cut(second, 0, less)], axis=axis),
    )


def put_slots(o_ref, q_ref, t_ref, core, second, most):
    size, spare = q_ref.shape[-1], t_ref.shape[-1]
    less = most - HEAD_DIM

    @pl.when((core == 0) & (second == 0))
    def _():
        o_ref[...] = q_ref[:, 0, :, :most]

    @pl.when((core == 0) & (second == 1))
    def _():
        o_ref[...] = jnp.zeros_like(o_ref)
        o_ref[:, :, : size - most] = q_ref[:, 0, :, most:]
        o_ref[:, :, size - most : size - most + spare] = t_ref[:, 0]

    @pl.when((core == 1) & (second == 0))
    def _():
        o_ref[...] = jnp.zeros_like(o_ref)
        o_ref[:, :, :less] = q_ref[:, 0, :, spare : spare + less]

    @pl.when((core == 1) & (second == 1))
    def _():
        o_ref[...] = jnp.zeros_like(o_ref)
        o_ref[:, :, :less] = q_ref[:, 0, :, spare + less :]


def put_half(o_ref, f_ref, second):
    wide = f_ref.shape[-1] // 2

    @pl.when(second == 0)
    def _():
        o_ref[...] = f_ref[0, :, :wide]

    @pl.when(second == 1)
    def _():
        o_ref[...] = f_ref[0, :, wide:]


def quarters(value):
    return value.reshape(value.shape[:-2] + (4, value.shape[-2] // 4, value.shape[-1]))


def pack_heads(qkv, tail, most):
    rows, size, spare = qkv.shape[1] // 4, qkv.shape[2], tail.shape[2]

    def body(s_ref, q_ref, t_ref, o_ref):
        put_slots(o_ref, q_ref, t_ref, s_ref[COL], s_ref[PEER], most)

    return call(
        body, "pack_heads", (3,),
        [
            pl.BlockSpec((1, 1, rows, size), lambda i, s: (i, s[QUARTER], 0, 0)),
            pl.BlockSpec((1, 1, rows, spare), lambda i, s: (i, s[QUARTER], 0, 0)),
        ],
        (quarters(qkv), quarters(tail)),
        pl.BlockSpec((1, rows, most), lambda i, s: (i, 0, 0)), shape(3, rows, most),
        vmem=WIDE_VMEM,
    )


def pack(fc, proj):
    rows, wide = fc.shape[0] // 4, fc.shape[1] // 2

    def body(s_ref, f_ref, p_ref, fo_ref, po_ref):
        put_half(fo_ref, f_ref, s_ref[PEER])
        put_half(po_ref, p_ref, s_ref[PEER])

    return call(
        body, "pack", (1,),
        [pl.BlockSpec((1, rows, 2 * wide), lambda i, s: (s[QUARTER], 0, 0))] * 2,
        (quarters(fc), quarters(proj)),
        [pl.BlockSpec((rows, wide), lambda i, s: (0, 0))] * 2,
        [shape(rows, wide)] * 2,
        vmem=WIDE_VMEM,
    )


def own_rows(mine, tail, width):
    three = mine.ndim == 3
    rows, size = mine.shape[-2] // 4, mine.shape[-1]

    def body(s_ref, m_ref, *refs):
        t_ref, o_ref = refs if three else (None,) + refs
        if three:
            put_slots(o_ref.at[:, 0], m_ref, t_ref, s_ref[COL], s_ref[ROW], width)
        else:
            put_half(o_ref.at[0], m_ref, s_ref[ROW])

    lead, zero = ((3,), (0,)) if three else ((), ())
    block = lambda width, at: pl.BlockSpec(lead + (1, rows, width), lambda i, s: zero + (at(i, s), 0, 0))
    own = lambda i, s: i
    return call(
        body, "own_rows", (4,),
        [block(size, own)] + ([block(tail.shape[-1], own)] if three else []),
        tuple([quarters(mine)] + ([quarters(tail)] if three else [])),
        block(width, lambda i, s: 4 * s[ROW] + i), shape(*lead, 8, rows, width),
        vmem=WIDE_VMEM,
    )


def all_rows(held, got):
    lead, tile = held.shape[:-3], held.shape[-2:]
    zero = (0,) * len(lead)

    def body(s_ref, h_ref, *refs):
        o_ref = refs[-1]
        place = (pl.program_id(0) // 2 != s_ref[LOW_Z]) * 2 + (pl.program_id(0) % 2 != s_ref[LOW_Y])
        for i in range(4):

            @pl.when(place == i)
            def _(i=i):
                o_ref[...] = refs[i][...].reshape(o_ref.shape)

    fetched = pl.BlockSpec(lead + tile, lambda i, s: zero + (0, 0))
    out = pl.pallas_call(
        body,
        grid_spec=pltpu.PrefetchScalarGridSpec(
            num_scalar_prefetch=1,
            grid=(4,),
            in_specs=[pl.BlockSpec(memory_space=pl.ANY)] + [fetched] * 4,
            out_specs=pl.BlockSpec(lead + (1,) + tile, lambda i, s: zero + (4 * s[PEER] + i, 0, 0)),
        ),
        out_shape=shape(*held.shape),
        input_output_aliases={1: 0},
        compiler_params=pltpu.CompilerParams(vmem_limit_bytes=WIDE_VMEM),
        cost_estimate=pl.CostEstimate(flops=0, bytes_accessed=0, transcendentals=0),
        name="all_rows",
    )(Here.places, held, *got)
    return out.reshape(lead + (8 * tile[0], tile[1]))


def half_rows(value, at):
    rows, count = value.shape[0] // 2, value.shape[1]

    def body(_, a_ref, o_ref):
        o_ref[...] = a_ref[...].astype(bf16)

    return call(
        body, "half_rows", (count // 256,),
        [pl.BlockSpec((rows, 256), lambda i, s: (s[at], i))], (value,),
        pl.BlockSpec((rows, 256), lambda i, s: (0, i)), shape(rows, count),
    )


def packed_sums(sums_two, sums_one, grad_own, hidden_sums, parts, most):
    width, half = sums_two.shape[1], sums_one.shape[1]

    def body(_, two_ref, one_ref, grad_ref, hid_ref, p_ref, o_ref):
        def over(value):
            ones = jnp.ones((8, value.shape[1]), value.dtype)
            exact = lax.Precision.HIGHEST if value.dtype == f32 else None
            return lax.dot_general(
                ones, value, (((1,), (1,)), ((), ())), preferred_element_type=f32, precision=exact
            )[0:1]

        o_ref[...] = jnp.zeros_like(o_ref)
        for i in range(3):
            o_ref[i : i + 1, :] = over(two_ref[i])
        o_ref[3:4, :half] = over(one_ref[0])
        o_ref[3:4, half:] = over(one_ref[1])
        o_ref[4:5, :half] = over(grad_ref[...])
        o_ref[8:9, :] = over(hid_ref[...])
        o_ref[9:10, :most] = over(p_ref[2 * most :, :])
        o_ref[10:11, :most] = over(p_ref[most : 2 * most, :])

    args = (sums_two, sums_one, grad_own, hidden_sums, parts)
    return call(
        body, "packed_sums", (1,), [whole_spec(v) for v in args], args,
        pl.BlockSpec((16, width), lambda i, s: (0, 0)), shape(16, width, dtype=f32),
    )


def sums_added(a, b, rows):
    def body(_, a_ref, b_ref, o_ref):
        at = lax.broadcasted_iota(jnp.int32, a_ref.shape, 0)
        o_ref[...] = a_ref[...] + jnp.where(at < rows, b_ref[...], 0.0)

    spec = whole_spec(a)
    return call(body, "sums_added", (1,), [spec, spec], (a, b), spec, shape(*a.shape, dtype=f32))


def spread_index(sizes, axis, step, value):
    places = []
    for size in reversed(sizes):
        places.insert(0, step % size)
        step = step // size
    places.insert(axis, value)
    return tuple(places) + (0, 0)


def halved(keep, got, axis, at):
    lead, tile = keep.shape[:-2], keep.shape[-2:]
    rest = lead[:axis] + lead[axis + 1 :]

    def body(_, a_ref, b_ref, c_ref, d_ref, keep_ref, send_ref):
        keep_ref[...] = (a_ref[...].astype(f32) + b_ref[...].astype(f32)).astype(bf16).reshape(keep_ref.shape)
        send_ref[...] = (c_ref[...].astype(f32) + d_ref[...].astype(f32)).astype(bf16).reshape(send_ref.shape)

    ones = (1,) * len(lead)
    mine = pl.BlockSpec(ones + tile, lambda i, s: spread_index(rest, axis, i, s[at]))
    theirs = pl.BlockSpec(ones + tile, lambda i, s: spread_index(rest, axis, i, 1 - s[at]))
    steps = math.prod(rest)
    out = pl.BlockSpec((1,) + tile, lambda i, s: (i, 0, 0))
    first, second = call(
        body, "halved", (steps,), [mine, mine, theirs, theirs], (keep, got, keep, got),
        [out, out], [shape(steps, *tile)] * 2,
    )
    return first.reshape(rest + tile), second.reshape(rest + tile)


def added(a, b):
    def body(_, a_ref, b_ref, o_ref):
        o_ref[...] = (a_ref[...].astype(f32) + b_ref[...].astype(f32)).astype(bf16)

    spec = whole_spec(a)
    return call(body, "added", (1,), [spec, spec], (a, b), spec, shape(*a.shape))


def chosen(a, b):
    def body(s_ref, a_ref, b_ref, o_ref):
        o_ref[...] = jnp.where(s_ref[SAME] == 1, a_ref[...], b_ref[...])

    spec = whole_spec(a)
    return call(body, "chosen", (1,), [spec, spec], (a, b), spec, shape(*a.shape))


def paired(at, first, second, axis):
    lead, tile = first.shape[:-2], first.shape[-2:]
    ones = (1,) * len(lead)
    steps = math.prod(lead)

    def body(_, a_ref, b_ref, o_ref):
        @pl.when(pl.program_id(0) == 0)
        def _():
            o_ref[...] = a_ref[...].reshape(o_ref.shape)

        @pl.when(pl.program_id(0) == 1)
        def _():
            o_ref[...] = b_ref[...].reshape(o_ref.shape)

    def place(step):
        return spread_index(lead, len(lead), step, 0)[: len(lead)] + (0, 0)

    out = lambda i, j, s: spread_index(lead, axis, j, jnp.where(i == 0, s[at], 1 - s[at]))
    return call(
        body, "paired", (2, steps),
        [
            pl.BlockSpec(ones + tile, lambda i, j, s: place(jnp.where(i == 0, j, steps - 1))),
            pl.BlockSpec(ones + tile, lambda i, j, s: place(jnp.where(i == 1, j, 0))),
        ],
        (first, second),
        pl.BlockSpec(ones + (1,) + tile, out),
        shape(*lead[:axis], 2, *lead[axis:], *tile),
    )


def widened(keep, got, at, y_last):
    rows, width = keep.shape[-2:]

    def body(s_ref, a_ref, b_ref, c_ref, d_ref, o_ref):
        if y_last:
            swap = s_ref[at] == 1
            o_ref[:, :width] = jnp.where(swap, b_ref[0, 0], a_ref[0, 0]).astype(f32)
            o_ref[:, width:] = jnp.where(swap, a_ref[0, 0], b_ref[0, 0]).astype(f32)
        else:
            other = pl.program_id(0) % 2 != s_ref[at]
            o_ref[:, :width] = jnp.where(other, b_ref[0, 0], a_ref[0, 0]).astype(f32)
            o_ref[:, width:] = jnp.where(other, d_ref[0, 0], c_ref[0, 0]).astype(f32)

    tile = (1, 1, rows, width)
    if y_last:
        one = pl.BlockSpec(tile, lambda i, s: (i // 2, i % 2, 0, 0))
        none = pl.BlockSpec(tile, lambda i, s: (0, 0, 0, 0))
        specs = [one, one, none, none]
    else:
        specs = [pl.BlockSpec(tile, lambda i, s, f=f: (f, i // 2, 0, 0)) for f in (0, 0, 1, 1)]
    return call(
        body, "widened", (4,), specs, (keep, got, keep, got),
        pl.BlockSpec((rows, 2 * width), lambda i, s: (i, 0)),
        shape(4 * rows, 2 * width, dtype=f32),
    )


def tails_of(keep, got, at, y_last, most, low, high):
    rows, width = keep.shape[-2:]
    count = width // most

    def body(s_ref, a_ref, b_ref, o_ref):
        second = jnp.where((s_ref[at] == 1) if y_last else (pl.program_id(0) % 2 == s_ref[at]), a_ref[0, 0], b_ref[0, 0])
        for i in range(count):
            o_ref[i, 0] = second[:, i * most + low : i * most + high]

    tile = (1, 1, rows, width)
    where = (lambda i, s: (i // 2, i % 2, 0, 0)) if y_last else (lambda i, s: (1, i // 2, 0, 0))
    return call(
        body, "tails_of", (4,), [pl.BlockSpec(tile, where)] * 2, (keep, got),
        pl.BlockSpec((count, 1, rows, high - low), lambda i, s: (0, i, 0, 0)),
        shape(count, 4, rows, high - low),
    )


def unslotted(keep, got, tails, at, y_last, most, size):
    rows, width = keep.shape[-2:]
    count, spare, less = width // most, tails.shape[-1], most - HEAD_DIM

    def body(s_ref, a_ref, b_ref, c_ref, d_ref, t_ref, o_ref):
        if y_last:
            swap = s_ref[at] == 1
            first = jnp.where(swap, b_ref[0, 0], a_ref[0, 0])
            second = jnp.where(swap, a_ref[0, 0], b_ref[0, 0])
        else:
            other = pl.program_id(0) % 2 != s_ref[at]
            first = jnp.where(other, b_ref[0, 0], a_ref[0, 0])
            second = jnp.where(other, d_ref[0, 0], c_ref[0, 0])
        first, second = first.astype(f32), second.astype(f32)

        @pl.when(s_ref[COL] == 0)
        def _():
            for i in range(count):
                o_ref[i, :, :most] = first[:, i * most : (i + 1) * most]
                o_ref[i, :, most:] = second[:, i * most : i * most + size - most]

        @pl.when(s_ref[COL] == 1)
        def _():
            for i in range(count):
                o_ref[i, :, :spare] = t_ref[i, 0].astype(f32)
                o_ref[i, :, spare : spare + less] = first[:, i * most : i * most + less]
                o_ref[i, :, spare + less :] = second[:, i * most : i * most + less]

    tile = (1, 1, rows, width)
    if y_last:
        one = pl.BlockSpec(tile, lambda i, s: (i // 2, i % 2, 0, 0))
        none = pl.BlockSpec(tile, lambda i, s: (0, 0, 0, 0))
        specs = [one, one, none, none]
    else:
        specs = [pl.BlockSpec(tile, lambda i, s, f=f: (f, i // 2, 0, 0)) for f in (0, 0, 1, 1)]
    return call(
        body, "unslotted", (4,),
        specs + [pl.BlockSpec((count, 1, rows, spare), lambda i, s: (0, i, 0, 0))],
        (keep, got, keep, got, tails),
        pl.BlockSpec((count, rows, size), lambda i, s: (0, i, 0)),
        shape(count, 4 * rows, size, dtype=f32),
    )


TOKENS = 256


def tile_of(rows, at=None):
    if at is None:
        return pl.BlockSpec((rows, TOKENS), lambda i, s: (0, i))
    return pl.BlockSpec((rows, TOKENS), lambda i, s: (at(s), i))


def norm_stats(parts):
    count = sum(part.shape[0] for part in parts)
    center = sum(jnp.sum(part, axis=0, keepdims=True) for part in parts) / count
    spread = sum(jnp.sum((part - center) * (part - center), axis=0, keepdims=True) for part in parts) / count
    return center, lax.rsqrt(spread + 1e-05)


def norm_one(x_own, x_peer, columns):
    half, count = x_own.shape

    def body(s_ref, own_ref, peer_ref, c_ref, h_ref, stat_ref):
        own, peer = own_ref[...].astype(f32), peer_ref[...].astype(f32)
        parts = [jnp.where(s_ref[ROW] == 0, own, peer), jnp.where(s_ref[ROW] == 0, peer, own)]
        center, inverse = norm_stats(parts)
        stat_ref[0:1, :] = center
        stat_ref[1:2, :] = inverse
        for i, part in enumerate(parts):
            rows = slice(i * half, (i + 1) * half)
            h_ref[rows, :] = ((part - center) * inverse * c_ref[rows, 0:1] + c_ref[rows, 1:2]).astype(bf16)

    return call(
        body, "norm_one", (count // TOKENS,),
        [tile_of(half), tile_of(half), whole_spec(columns)],
        (x_own, x_peer, columns),
        [tile_of(2 * half), tile_of(8)],
        [shape(2 * half, count), shape(8, count, dtype=f32)],
    )


def norm_two(x_own, x_peer, low, other, columns):
    half, count = x_own.shape

    def body(s_ref, own_ref, peer_ref, low_ref, other_ref, c_ref, x_ref, h_ref, stat_ref):
        own, peer = own_ref[...].astype(f32), peer_ref[...].astype(f32)
        parts = [jnp.where(s_ref[ROW] == 0, own, peer), jnp.where(s_ref[ROW] == 0, peer, own)]
        for i in range(2):
            rows = slice(i * half, (i + 1) * half)
            branch = low_ref[rows, :].astype(f32) + other_ref[rows, :].astype(f32) + c_ref[rows, 2:3]
            parts[i] = parts[i] + branch
            x_ref[rows, :] = parts[i]
        center, inverse = norm_stats(parts)
        stat_ref[0:1, :] = center
        stat_ref[1:2, :] = inverse
        for i, part in enumerate(parts):
            rows = slice(i * half, (i + 1) * half)
            h_ref[rows, :] = ((part - center) * inverse * c_ref[rows, 3:4] + c_ref[rows, 4:5]).astype(bf16)

    full = tile_of(2 * half)
    return call(
        body, "norm_two", (count // TOKENS,),
        [tile_of(half), tile_of(half), full, full, whole_spec(columns)],
        (x_own, x_peer, low, other, columns),
        [full, full, tile_of(8)],
        [shape(2 * half, count, dtype=f32), shape(2 * half, count), shape(8, count, dtype=f32)],
    )


def lanes_summed(ref, at, value, first):
    total = sum(value[:, i : i + 128] for i in range(0, value.shape[1], 128))

    @pl.when(first)
    def _():
        ref[at] = total

    @pl.when(jnp.logical_not(first))
    def _():
        ref[at] += total


def norm_two_back(low, other, grad, x_mid, stats, columns):
    width, count = low.shape

    def body(_, low_ref, other_ref, g_ref, x_ref, stat_ref, gain_ref, mid_ref, branch_ref, sum_ref):
        first = pl.program_id(0) == 0
        incoming = low_ref[...].astype(f32) + other_ref[...].astype(f32)
        inverse = stat_ref[1:2, :]
        normed = (x_ref[...] - stat_ref[0:1, :]) * inverse
        scaled = incoming * gain_ref[:, 3:4]
        mean = jnp.sum(scaled, axis=0, keepdims=True) / width
        along = jnp.sum(scaled * normed, axis=0, keepdims=True) / width
        mid = g_ref[...].astype(f32) + inverse * (scaled - mean - normed * along)
        mid_ref[...] = mid
        branch = mid.astype(bf16)
        branch_ref[...] = branch
        lanes_summed(sum_ref, 0, incoming * normed, first)
        lanes_summed(sum_ref, 1, incoming, first)
        lanes_summed(sum_ref, 2, branch.astype(f32), first)

    full = tile_of(width)
    return call(
        body, "norm_two_back", (count // TOKENS,),
        [full, full, full, full, tile_of(8), whole_spec(columns)],
        (low, other, grad, x_mid, stats, columns),
        [full, full, pl.BlockSpec((3, width, 128), lambda i, s: (0, 0, 0))],
        [shape(width, count, dtype=f32), shape(width, count), shape(3, width, 128, dtype=f32)],
    )


def norm_one_sums(mine, other, x_own, stats, columns):
    half, count = x_own.shape

    def body(_, m_ref, o_ref, x_ref, stat_ref, gain_ref, row_ref, sum_ref):
        first = pl.program_id(0) == 0
        incoming = m_ref[...] + o_ref[...].astype(f32)
        normed = (x_ref[...].astype(f32) - stat_ref[0:1, :]) * stat_ref[1:2, :]
        scaled = incoming * gain_ref[:, 0:1]
        row_ref[...] = jnp.zeros_like(row_ref)
        row_ref[0:1, :] = jnp.sum(scaled, axis=0, keepdims=True)
        row_ref[1:2, :] = jnp.sum(scaled * normed, axis=0, keepdims=True)
        lanes_summed(sum_ref, 0, incoming * normed, first)
        lanes_summed(sum_ref, 1, incoming, first)

    return call(
        body, "norm_one_sums", (count // TOKENS,),
        [tile_of(half, lambda s: s[ROW]), tile_of(half), tile_of(half), tile_of(8), pl.BlockSpec((half, columns.shape[1]), lambda i, s: (s[ROW], 0))],
        (mine, other, x_own, stats, columns),
        [tile_of(8), pl.BlockSpec((2, half, 128), lambda i, s: (0, 0, 0))],
        [shape(8, count, dtype=f32), shape(2, half, 128, dtype=f32)],
    )


def norm_one_back(mine, other, x_own, stats, columns, mid_grad, sums, sums_peer):
    half, count = x_own.shape

    def body(_, m_ref, o_ref, x_ref, stat_ref, gain_ref, mid_ref, a_ref, b_ref, out_ref):
        inverse = stat_ref[1:2, :]
        normed = (x_ref[...].astype(f32) - stat_ref[0:1, :]) * inverse
        scaled = (m_ref[...] + o_ref[...].astype(f32)) * gain_ref[:, 0:1]
        means = (a_ref[...] + b_ref[...]) / (2 * half)
        out_ref[...] = mid_ref[...] + inverse * (scaled - means[0:1, :] - normed * means[1:2, :])

    mine_tile = tile_of(half, lambda s: s[ROW])
    return call(
        body, "norm_one_back", (count // TOKENS,),
        [mine_tile, tile_of(half), tile_of(half), tile_of(8), pl.BlockSpec((half, columns.shape[1]), lambda i, s: (s[ROW], 0)), mine_tile, tile_of(8), tile_of(8)],
        (mine, other, x_own, stats, columns, mid_grad, sums, sums_peer),
        tile_of(half), shape(half, count, dtype=f32),
    )


def block_result(x_mid, part, other, columns):
    half, count = other.shape

    def body(_, x_ref, p_ref, o_ref, b_ref, out_ref):
        out_ref[...] = (x_ref[...] + (p_ref[...].astype(f32) + o_ref[...].astype(f32)) + b_ref[:, 6:7]).astype(bf16)

    mine_tile = tile_of(half, lambda s: s[ROW])
    return call(
        body, "block_result", (count // TOKENS,),
        [mine_tile, mine_tile, tile_of(half), pl.BlockSpec((half, columns.shape[1]), lambda i, s: (s[ROW], 0))],
        (x_mid, part, other, columns),
        tile_of(half), shape(half, count),
    )


class Fetch:
    def __init__(self, sent):
        self.got = [row_swap(sent)]

    def more(self, *marks):
        first = after(self.got[0], *marks)
        self.got = [first, dp_xor(first, 1), dp_xor(first, 2)]

    def rest(self, first, *marks):
        self.got.append(dp_xor(after(self.got[first], *marks), 3 - first))
        return self.got


class Total:
    def __init__(self, sources, r, k, y_first, y_last, *marks):
        self.rows, self.width = sources[0][0].shape[0], sum(part[1] for _, _, _, part in sources)
        self.r, self.k, self.y_first, self.y_last = r, k, y_first, y_last
        self.fast = lax.axis_size("dp") == 8
        tied = lambda marks: [(own, other, after(right, *marks), part) for own, other, right, part in sources]
        if not self.fast:
            self.grad = weight_grad(tied(marks), lambda i, s: i, 4, 4)
            return
        if y_first:
            send, keep = (lambda i, s: 2 * (1 - s[LOW_Y]) + i), (lambda i, s: 2 * s[LOW_Y] + i)
            blocks, parts, mask = 2, 4, 1
        else:
            send, keep = (lambda i, s: 1 - s[LOW_Z] + 2 * i), (lambda i, s: s[LOW_Z] + 2 * i)
            blocks, parts, mask = 4, 8, 2
        shaped = lambda v: v.reshape(2, 2, self.rows // 8, self.width)
        sent = weight_grad(tied(marks), send, blocks, parts)
        self.got, self.sent = dp_xor(shaped(sent), mask), [sent]
        self.kept = lambda *marks: shaped(weight_grad(tied(marks), keep, blocks, parts))

    def hold(self, *marks):
        if self.fast:
            self.keep = self.kept(*marks)
        return self.marks()

    def marks(self):
        return [self.keep] if self.fast else []

    def sent_marks(self):
        return self.sent if self.fast else []

    def sum_one(self, *marks):
        if self.fast:
            axis, at, mask = (1, LOW_Z, 2) if self.y_first else (0, LOW_Y, 1)
            self.keep, send = halved(after(self.keep, *marks), self.got, axis, at)
            self.got = dp_xor(send, mask)
            return [self.keep]
        return []

    def sum_two(self, *marks):
        if self.fast:
            self.keep, send = halved(after(self.keep, *marks), self.got, 0, HIGH_Z)
            self.got = dp_xor(send, 4)
            return [self.keep]
        return []

    def sum_three(self, *marks):
        if self.fast:
            cross = [
                (2 * i + j, 2 * (i ^ 1) + (j ^ 1))
                for i in range(lax.axis_size("dp"))
                for j in range(2)
                if i % 2 != j
            ]
            self.keep = added(after(self.keep, *marks), self.got)
            self.got = lax.ppermute(self.keep, ("dp", "row"), cross)
            return [self.keep]
        return []

    def spread_one(self, *marks):
        if self.fast:
            self.keep = chosen(after(self.keep, *marks), self.got)
            self.got = dp_xor(self.keep, 4)
            return [self.keep]
        return []

    def spread_two(self, *marks):
        if self.fast:
            self.keep = paired(HIGH_Z, after(self.keep, *marks), self.got, 0)
            self.got = dp_xor(self.keep, 2 if self.y_last else 1)
            return [self.keep]
        return []

    def spread_three(self, *marks):
        if self.fast:
            if self.y_last:
                self.keep = paired(LOW_Z, after(self.keep, *marks), self.got, 1)
                self.got = dp_xor(self.keep, 1)
            else:
                self.keep = paired(LOW_Y, after(self.keep, *marks), self.got, 0)
                self.got = dp_xor(self.keep, 2)
            return [self.keep]
        return []

    def tail(self, most, spare, *marks):
        if not self.fast:
            return list(marks)
        less = most - HEAD_DIM
        at = LOW_Y if self.y_last else LOW_Z
        self.keep = after(self.keep, *marks)
        tails = tails_of(self.keep, self.got, at, self.y_last, most, less - spare, less)
        self.tails = col_swap(tails)
        return [tails]

    def slots(self, c, most, spare, *marks):
        less = most - HEAD_DIM
        size = 2 * less + spare
        if not self.fast:
            both = self.result()
            cut = lambda i: [v[:, i * most : (i + 1) * most] for v in both]
            return jnp.stack([from_slots(c, *cut(i), 1, spare).astype(f32) for i in range(self.width // most)])
        at = LOW_Y if self.y_last else LOW_Z
        keep = after(self.keep, *marks)
        return unslotted(keep, self.got, self.tails, at, self.y_last, most, size)

    def wide(self, *marks):
        if self.fast:
            return widened(after(self.keep, *marks), self.got, LOW_Y if self.y_last else LOW_Z, self.y_last)
        return jnp.concatenate(self.result(), axis=1).astype(f32)

    def result(self):
        halves = self.grad.reshape(2, self.rows // 2, self.width)
        keep, got = pick(halves, self.r, 0), row_swap(pick(halves, 1 - self.r, 0))
        both = lax.psum(ordered(self.r, keep[None], got[None], 0), "dp")
        return both[0], both[1]


def hop(value, mask):
    return dp_xor(value, mask) if lax.axis_size("dp") == 8 else None


def hop_added(value, peer, *marks):
    return value if peer is None else sums_added(after(value, *marks), peer, 16)


def per_device(
    block_in,
    out_grad,
    seq_lengths,
    ln1_gain,
    ln1_bias,
    qkv_weight,
    qv_bias,
    out_weight,
    out_bias,
    ln2_gain,
    ln2_bias,
    fc_weight,
    fc_bias,
    proj_weight,
    proj_bias,
):
    n_dp = lax.axis_size("dp")
    r, c, k = lax.axis_index("row"), lax.axis_index("col"), lax.axis_index("dp")
    x_own, grad_own = block_in.T, out_grad.T
    half, tokens = x_own.shape
    heads = 7
    most = heads * HEAD_DIM
    spare = 32
    column = lambda v: v.astype(f32)[:, None]

    y, z = k % 2, (k // 2) % 2
    at = jnp.arange(8)
    held = (r, c, y, z, (k // 4) % 2, 2 * z + y, 1 - r, (y == r).astype(r.dtype))
    Here.places = sum(jnp.where(at == i, value, 0) for i, value in enumerate(held)).astype(jnp.int32)
    qkv_tail = col_swap(qkv_weight[:, :, :spare])
    proj_turned = proj_weight.T
    qkv_sent = pack_heads(qkv_weight, qkv_tail, most)
    fc_sent, proj_sent = pack(after(fc_weight, qkv_sent), proj_turned)
    qkv_fetch = Fetch(qkv_sent)
    x_peer = row_swap(after(x_own, qkv_sent))
    vectors = after(jnp.stack([ln1_gain, ln1_bias, out_bias, ln2_gain, ln2_bias]), qkv_sent)
    vectors = ordered(r, vectors, row_swap(vectors), 1)
    both = jnp.stack([half_of(r, fc_bias, 0), jnp.concatenate([proj_bias, proj_bias])])
    columns = jnp.concatenate([vectors, both, jnp.zeros_like(both[:1])]).astype(f32).T
    qv_bias = after(qv_bias, qkv_sent)
    bias_first, bias_second = head_slots(c, qv_bias, col_swap(qv_bias[:, :spare]), 1, most)
    bias_mine = jnp.where(r == 0, bias_first, bias_second).astype(f32)
    bias_mine = jnp.stack([bias_mine[0], jnp.zeros_like(bias_mine[0]), bias_mine[1]])[:, :, None]

    out_weight = after(out_weight, qkv_sent)
    out_first, out_second = head_slots(c, out_weight, col_swap(out_weight[:spare]), 0, most)
    out_mine = jnp.where(r == 0, out_first, out_second)
    out_sent = jnp.where(r == 0, out_second, out_first)
    ff_size = fc_weight.shape[1] // 2
    qkv_full = own_rows(after(qkv_weight, fc_sent, out_sent), qkv_tail, most)
    qkv_fetch.more(qkv_full)
    fc_full = own_rows(after(fc_weight, qkv_fetch.got[0]), None, ff_size)
    qkv_fetch.rest(2, fc_full)
    proj_full = own_rows(after(proj_turned, fc_full, *qkv_fetch.got[1:3]), None, ff_size)

    lengths = after(seq_lengths, qkv_sent)[0]
    group = 2 * tokens
    places = jnp.arange(group, dtype=jnp.int32)
    ends = jnp.cumsum(lengths, dtype=jnp.int32)
    first = jnp.sum(
        jnp.where(ends[None, :] <= places[:, None], lengths[None, :], 0), axis=1, dtype=jnp.int32
    ).reshape(group // BLK, BLK)
    info = jnp.concatenate([(c * (tokens // BLK))[None].astype(jnp.int32), first[:, 0] // BLK])

    h_one, stats_one = norm_one(after(x_own, proj_full, info, bias_mine), x_peer, columns)
    qkv_full = all_rows(after(qkv_full, h_one), qkv_fetch.got)
    h_one_peer = col_swap(after(h_one, qkv_full))
    out_got = row_swap(after(out_sent, qkv_full))
    fc_fetch = Fetch(after(fc_sent, qkv_full))
    proj_fetch = Fetch(after(proj_sent, qkv_full))
    projected = project(qkv_full, h_one, h_one_peer, bias_mine)
    out_full = ordered(r, after(out_mine, projected), out_got, 1)
    attended, log_totals = attend(info, after(projected, out_full), first, heads)
    fc_fetch.more(attended)
    proj_fetch.more(attended)
    other = mapped(out_full, after(attended, fc_fetch.got[0], proj_fetch.got[0]), 1, True)
    low = mapped(out_full, attended, 0, True, col_swap(other))
    branch_other = row_swap(low)
    grad_got = row_swap(after(grad_own, low))
    fc_fetch.rest(1, low)
    proj_fetch.rest(2, low)
    fc_full = all_rows(after(fc_full, low), fc_fetch.got)
    proj_full = all_rows(after(proj_full, fc_full), proj_fetch.got)
    x_mid, h_two, stats_two = norm_two(x_own, x_peer, after(low, proj_full), branch_other, columns)
    h_two_peer = col_swap(h_two)
    activated, slope = hidden(fc_full, h_two, h_two_peer, columns)
    grad_full = paired(ROW, after(grad_own, activated), grad_got, 0).reshape(2 * half, tokens)
    grad_peer = col_swap(grad_full)

    mark = [grad_peer]
    pre_grad, hidden_sums = hidden_back(proj_full, grad_full, grad_peer, slope)
    mark = [pre_grad]
    h_two_other = mapped(fc_full, after(pre_grad, *mark), 1, False)
    mark = [h_two_other]
    fc_total = Total([(h_two, h_two_peer, pre_grad, (0, ff_size))], r, k, False, True, *mark)
    mark = fc_total.sent_marks()
    low = mapped(fc_full, after(pre_grad, *mark), 0, False, col_swap(h_two_other))
    low_other, mark = row_swap(low), [low]
    proj_total = Total([(grad_full, grad_peer, activated, (0, ff_size))], r, k, True, False, *mark)
    mark = proj_total.sent_marks()
    part_other = mapped(proj_full, after(activated, *mark), 1, False)
    mark = [part_other]
    mark = proj_total.hold(*mark)
    mark = fc_total.hold(*mark)
    mark = fc_total.sum_one(*mark)
    mid_grad, branch_grad, sums_two = norm_two_back(
        after(low, *mark), low_other, grad_full, x_mid, stats_two, columns
    )
    branch_peer, mark = col_swap(branch_grad), [branch_grad]
    mark = proj_total.sum_one(*mark)
    attended_grad = attended_back(out_full, after(branch_grad, *mark), branch_peer)
    mark = [attended_grad]
    parts = attend_back(info, projected, attended, after(attended_grad, *mark), log_totals, first, heads)
    mark = [parts]
    three_other = mapped_three(qkv_full, after(parts, *mark), 1)
    mark = [three_other]
    oq_total = Total([(branch_grad, branch_peer, attended, (0, most)), (h_one, h_one_peer, parts, (2, most))], r, k, True, True, *mark)
    mark = oq_total.sent_marks()
    mark = fc_total.sum_two(*mark)
    mark = proj_total.sum_two(*mark)
    kv_total = Total([(h_one, h_one_peer, parts, (0, 2 * most))], r, k, True, False, *mark)
    mark = kv_total.sent_marks()
    proj_part = mapped(proj_full, after(activated, *mark), 0, False, col_swap(part_other))
    mark = [proj_part]
    mark = oq_total.hold(*mark)
    mark = oq_total.sum_one(*mark)
    mine = mapped_three(qkv_full, after(parts, *mark), 0, col_swap(three_other))
    mark = [mine]
    send = half_rows(after(mine, *mark), PEER)
    one_other, mark = row_swap(send), [send]
    mark = kv_total.hold(*mark)
    mark = kv_total.sum_one(*mark)
    mark = proj_total.sum_three(*mark)
    mark = fc_total.sum_three(*mark)
    mark = oq_total.sum_two(*mark)
    mark = kv_total.sum_two(*mark)
    mark = oq_total.sum_three(*mark)
    mark = proj_total.spread_one(*mark)
    mark = fc_total.spread_one(*mark)
    sums, sums_one = norm_one_sums(after(mine, *mark), one_other, x_own, stats_one, columns)
    sums_peer, mark = row_swap(sums), [sums]
    mark = kv_total.sum_three(*mark)
    mark = oq_total.spread_one(*mark)
    packed = packed_sums(sums_two, after(sums_one, *mark), grad_own, hidden_sums, parts, most)
    packed_peer, mark = col_swap(packed), [packed]
    packed = sums_added(after(packed, *mark), packed_peer, 8)
    packed_peer, mark = hop(packed, 2), [packed]
    mark = proj_total.spread_two(*mark)
    mark = kv_total.spread_one(*mark)
    packed = hop_added(packed, packed_peer, *mark)
    packed_peer, mark = hop(packed, 1), [packed]
    x_grad = norm_one_back(after(mine, *mark), one_other, x_own, stats_one, columns, mid_grad, sums, sums_peer)
    mark = [x_grad]
    mark = fc_total.spread_two(*mark)
    mark = kv_total.spread_two(*mark)
    mark = oq_total.spread_two(*mark)
    mark = kv_total.spread_three(*mark)
    packed = hop_added(packed, packed_peer, *mark)
    packed_peer, mark = hop(packed, 4), [packed]
    mark = oq_total.spread_three(*mark)
    packed = hop_added(packed, packed_peer, *mark)
    if n_dp != 8:
        for i in range(n_dp.bit_length() - 1):
            packed = sums_added(packed, dp_xor(packed, 1 << i), 16)
    packed_peer, mark = row_swap(packed), [packed]
    mark = proj_total.spread_three(*mark)
    packed_peer = after(packed_peer, *mark)
    mark = [packed_peer]
    mark = fc_total.spread_three(*mark)
    mark = kv_total.tail(most, spare, *mark)
    mark = oq_total.tail(most, spare, *mark)
    send = half_rows(after(proj_part, *mark), PEER)
    block_other, mark = row_swap(send), [send]
    whole = oq_total.slots(c, most, spare, *mark)
    out_weight_grad = whole[0]
    q_weight_grad = whole[1]
    mark = [whole]
    whole = kv_total.slots(c, most, spare, *mark)
    k_weight_grad = whole[0]
    v_weight_grad = whole[1]
    mark = [whole]
    block_out = block_result(after(x_mid, *mark), proj_part, block_other, columns)
    mark = [block_out]
    proj_weight_grad = proj_total.wide(*mark).T
    mark = [proj_weight_grad]
    fc_weight_grad = fc_total.wide(*mark)
    mark = [fc_weight_grad]

    own = half_of(r, packed, 1)
    fc_bias_grad = ordered(r, packed[8], packed_peer[8], 0)
    qv_mine, qv_peer = packed[9:11, :most], packed_peer[9:11, :most]
    qv_bias_grad = from_slots(
        c, jnp.where(r == 0, qv_mine, qv_peer), jnp.where(r == 0, qv_peer, qv_mine), 1, spare
    )
    qkv_weight_grad = jnp.stack([q_weight_grad, k_weight_grad, v_weight_grad])
    out_weight_grad = out_weight_grad.T
    return (
        block_out.T,
        x_grad.T,
        packed[3, :half],
        packed[3, half:],
        qkv_weight_grad,
        qv_bias_grad,
        out_weight_grad,
        own[2],
        own[0],
        own[1],
        fc_weight_grad,
        fc_bias_grad,
        proj_weight_grad,
        packed[4, :half],
    )


def solution(mesh):
    placed = (
        P(("dp", "col"), "row"),
        P(("dp", "col"), "row"),
        P("dp", None),
        P("row"),
        P("row"),
        P(None, "row", "col"),
        P(None, "col"),
        P("col", "row"),
        P("row"),
        P("row"),
        P("row"),
        P("row", "col"),
        P("col"),
        P("col", "row"),
        P("row"),
    )
    return jax.shard_map(
        per_device,
        mesh=mesh,
        in_specs=placed,
        out_specs=(
            P(("dp", "col"), "row"),
            P(("dp", "col"), "row"),
            P("row"),
            P("row"),
            P(None, "row", "col"),
            P(None, "col"),
            P("col", "row"),
            P("row"),
            P("row"),
            P("row"),
            P("row", "col"),
            P("col"),
            P("col", "row"),
            P("row"),
        ),
        check_vma=False,
    )
```

```python
import functools
import math

import jax
import jax.numpy as jnp
from jax import lax
from jax.experimental import pallas as pl
from jax.experimental.pallas import tpu as pltpu
from jax.sharding import PartitionSpec as P

HEAD_DIM = 64
gelu_root = math.sqrt(2.0 / math.pi)
gelu_cubic = 0.044715
BLK = 256
NEG = -1e30
KERNEL_VMEM = 40 * 2**20
WIDE_VMEM = 58 * 2**20


def dot_over(dims, a, b):
    return lax.dot_general(a, b, (dims, ((), ())), preferred_element_type=jnp.float32)


def nn(a, b):
    return dot_over(((1,), (0,)), a, b)


def nt(a, b):
    return dot_over(((1,), (1,)), a, b)


def tn(a, b):
    return dot_over(((0,), (0,)), a, b)


def head_rows(h):
    return slice(h * HEAD_DIM, (h + 1) * HEAD_DIM)


def allowed_tile(i, j, first):
    keys = j * BLK + lax.broadcasted_iota(jnp.int32, (BLK, BLK), 0)
    queries = i * BLK + lax.broadcasted_iota(jnp.int32, (BLK, BLK), 1)
    return (keys >= first) & (keys <= queries)


def turned(x):
    return jnp.transpose(x.astype(jnp.float32)).astype(jnp.bfloat16)


def attend_kernel(heads, blocks, info_ref, q_ref, k_ref, v_ref, first_ref, o_ref, lse_ref, keys_ref):
    i = pl.program_id(0)
    shift = info_ref[0]

    @pl.when(i == 0)
    def _():
        for h in range(heads):
            keys_ref[h] = turned(k_ref[head_rows(h), :])

    first = first_ref[pl.ds(i, 1), :]
    scale = jnp.bfloat16(HEAD_DIM**-0.5)

    def step(j, carry):
        place = pl.ds(pl.multiple_of(lax.rem(j + shift, blocks) * BLK, BLK), BLK)
        allowed = allowed_tile(i, j, first)
        out = []
        for h in range(heads):
            top, total, acc = carry[h]
            scores = nn(keys_ref[h, place, :], q_ref[head_rows(h), :] * scale)
            scores = jnp.where(allowed, scores, NEG)
            new_top = jnp.maximum(top, jnp.max(scores, axis=0, keepdims=True))
            probs = jnp.exp(scores - new_top)
            shrink = jnp.exp(top - new_top)
            total = total * shrink + jnp.sum(probs, axis=0, keepdims=True)
            acc = acc * shrink + nn(v_ref[head_rows(h), place], probs.astype(jnp.bfloat16))
            out.append((new_top, total, acc))
        return tuple(out)

    row = lambda value: jnp.full((1, BLK), value, jnp.float32)
    start = tuple((row(NEG), row(0.0), jnp.zeros((HEAD_DIM, BLK), jnp.float32)) for h in range(heads))
    done = lax.fori_loop(info_ref[1 + i], i + 1, step, start)
    for h, (top, total, acc) in enumerate(done):
        o_ref[head_rows(h), :] = (acc / total).astype(jnp.bfloat16)
        lse_ref[h : h + 1, :] = top + jnp.log(total)


def attend(info, projected, first, heads):
    tokens = projected.shape[1]
    wide, blocks = heads * HEAD_DIM, tokens // BLK
    at = lambda i, s: lax.rem(i + s[0], blocks)
    return pl.pallas_call(
        functools.partial(attend_kernel, heads, blocks),
        grid_spec=pltpu.PrefetchScalarGridSpec(
            num_scalar_prefetch=1,
            grid=(blocks,),
            in_specs=[
                pl.BlockSpec((wide, BLK), lambda i, s: (0, at(i, s))),
                pl.BlockSpec((wide, tokens), lambda i, s: (1, 0)),
                pl.BlockSpec((wide, tokens), lambda i, s: (2, 0)),
                pl.BlockSpec((blocks, BLK), lambda i, s: (0, 0)),
            ],
            out_specs=[
                pl.BlockSpec((wide, BLK), lambda i, s: (0, at(i, s))),
                pl.BlockSpec((8, BLK), lambda i, s: (0, i)),
            ],
            scratch_shapes=[pltpu.VMEM((heads, tokens, HEAD_DIM), jnp.bfloat16)],
        ),
        out_shape=[
            jax.ShapeDtypeStruct((wide, tokens), jnp.bfloat16),
            jax.ShapeDtypeStruct((8, tokens), jnp.float32),
        ],
        compiler_params=pltpu.CompilerParams(vmem_limit_bytes=KERNEL_VMEM),
        cost_estimate=pl.CostEstimate(flops=0, bytes_accessed=0, transcendentals=0),
        name="attend",
    )(info, projected, projected, projected, first)


def attend_back_kernel(
    heads, blocks, info_ref, q_ref, k_ref, v_ref, o_ref, g_ref, lse_ref, first_ref,
    d_ref, keys_ref, values_ref, dk_acc, dv_acc,
):
    i = pl.program_id(0)
    shift = info_ref[0]

    @pl.when(i == 0)
    def _():
        for h in range(heads):
            keys_ref[h] = turned(k_ref[head_rows(h), :])
            values_ref[h] = turned(v_ref[head_rows(h), :])
        dk_acc[...] = jnp.zeros_like(dk_acc)
        dv_acc[...] = jnp.zeros_like(dv_acc)

    first = first_ref[pl.ds(i, 1), :]
    scale = jnp.bfloat16(HEAD_DIM**-0.5)
    centre = [
        jnp.sum(
            g_ref[head_rows(h), :].astype(jnp.float32) * o_ref[head_rows(h), :].astype(jnp.float32),
            axis=0,
            keepdims=True,
        )
        for h in range(heads)
    ]

    def step(j, carry):
        place = pl.ds(pl.multiple_of(lax.rem(j + shift, blocks) * BLK, BLK), BLK)
        allowed = allowed_tile(i, j, first)
        out = []
        for h in range(heads):
            rows = head_rows(h)
            query = q_ref[rows, :] * scale
            grad = g_ref[rows, :]
            scores = jnp.where(allowed, nn(keys_ref[h, place, :], query), NEG)
            probs = jnp.exp(scores - lse_ref[h : h + 1, :])
            prob_grad = nn(values_ref[h, place, :], grad)
            score_grad = (probs * (prob_grad - centre[h])).astype(jnp.bfloat16)
            dv_acc[rows, place] += nt(grad, probs.astype(jnp.bfloat16))
            dk_acc[rows, place] += nt(query, score_grad)
            out.append(carry[h] + nn(k_ref[rows, place], score_grad))
        return tuple(out)

    start = tuple(jnp.zeros((HEAD_DIM, BLK), jnp.float32) for h in range(heads))
    done = lax.fori_loop(info_ref[1 + i], i + 1, step, start)
    mine = pl.ds(pl.multiple_of(lax.rem(i + shift, blocks) * BLK, BLK), BLK)
    for h in range(heads):
        d_ref[head_rows(2 * heads + h), mine] = (done[h] * HEAD_DIM**-0.5).astype(jnp.bfloat16)

    @pl.when(i == blocks - 1)
    def _():
        d_ref[: heads * HEAD_DIM, :] = dk_acc[...].astype(jnp.bfloat16)
        d_ref[heads * HEAD_DIM : 2 * heads * HEAD_DIM, :] = dv_acc[...].astype(jnp.bfloat16)


def attend_back(info, projected, attended, grad, log_totals, first, heads):
    tokens = projected.shape[1]
    wide, blocks = heads * HEAD_DIM, tokens // BLK
    at = lambda i, s: lax.rem(i + s[0], blocks)
    block = pl.BlockSpec((wide, BLK), lambda i, s: (0, at(i, s)))
    whole = lambda part: pl.BlockSpec((wide, tokens), lambda i, s: (part, 0))
    return pl.pallas_call(
        functools.partial(attend_back_kernel, heads, blocks),
        grid_spec=pltpu.PrefetchScalarGridSpec(
            num_scalar_prefetch=1,
            grid=(blocks,),
            in_specs=[
                block,
                whole(1),
                whole(2),
                block,
                block,
                pl.BlockSpec((8, BLK), lambda i, s: (0, i)),
                pl.BlockSpec((blocks, BLK), lambda i, s: (0, 0)),
            ],
            out_specs=pl.BlockSpec((3 * wide, tokens), lambda i, s: (0, 0)),
            scratch_shapes=[
                pltpu.VMEM((heads, tokens, HEAD_DIM), jnp.bfloat16),
                pltpu.VMEM((heads, tokens, HEAD_DIM), jnp.bfloat16),
                pltpu.VMEM((wide, tokens), jnp.float32),
                pltpu.VMEM((wide, tokens), jnp.float32),
            ],
        ),
        out_shape=jax.ShapeDtypeStruct((3 * wide, tokens), jnp.bfloat16),
        compiler_params=pltpu.CompilerParams(vmem_limit_bytes=KERNEL_VMEM),
        cost_estimate=pl.CostEstimate(flops=0, bytes_accessed=0, transcendentals=0),
        name="attend_back",
    )(info, projected, projected, projected, attended, grad, log_totals, first)


ROW, COL, LOW_Y, LOW_Z, HIGH_Z, QUARTER, PEER, SAME = range(8)


class Here:
    places = None


def call(body, name, grid, specs, args, out_specs, out_shapes, vmem=KERNEL_VMEM):
    return pl.pallas_call(
        body,
        grid_spec=pltpu.PrefetchScalarGridSpec(
            num_scalar_prefetch=1, grid=grid, in_specs=specs, out_specs=out_specs
        ),
        out_shape=out_shapes,
        compiler_params=pltpu.CompilerParams(vmem_limit_bytes=vmem),
        cost_estimate=pl.CostEstimate(flops=0, bytes_accessed=0, transcendentals=0),
        name=name,
    )(Here.places, *args)


f32 = jnp.float32
bf16 = jnp.bfloat16


def shape(*dims, dtype=jnp.bfloat16):
    return jax.ShapeDtypeStruct(dims, dtype)


def whole_spec(value):
    zeros = (0,) * value.ndim
    return pl.BlockSpec(value.shape, lambda *_: zeros)


def chunks(size, step):
    return [slice(i, min(i + step, size)) for i in range(0, size, step)]


def project(weight, own, other, bias):
    parts, depth, width = weight.shape
    count = own.shape[1]

    def body(_, w_ref, own_ref, other_ref, b_ref, o_ref):
        def run(ref):
            for cols in chunks(count, 256):
                o_ref[:, cols] = (tn(w_ref[0], ref[:, cols]) + b_ref[0]).astype(jnp.bfloat16)

        pl.when(pl.program_id(0) == 0)(lambda: run(own_ref))
        pl.when(pl.program_id(0) == 1)(lambda: run(other_ref))

    return call(
        body, "project", (2, parts),
        [
            pl.BlockSpec((1, depth, width), lambda i, j, _: (j, 0, 0)),
            whole_spec(own),
            whole_spec(other),
            pl.BlockSpec((1, width, 1), lambda i, j, _: (j, 0, 0)),
        ],
        (weight, own, other, bias),
        pl.BlockSpec((width, count), lambda i, j, _: (j, i)),
        shape(parts * width, 2 * count),
    )


def hidden(weight, own, other, columns):
    depth, width = weight.shape
    count = own.shape[1]
    block = 256
    half = count // block

    def body(_, w_ref, own_ref, other_ref, b_ref, act_ref, slope_ref):
        tokens = jnp.where(pl.program_id(0) < half, own_ref[...], other_ref[...])
        for rows in chunks(width, 256):
            pre = tn(w_ref[:, rows], tokens) + b_ref[rows, 5:6]
            square = pre * pre
            bend = jnp.tanh(pre * (gelu_root + (gelu_root * gelu_cubic) * square))
            lift = 0.5 * (1.0 + bend)
            act_ref[rows, :] = (pre * lift).astype(jnp.bfloat16)
            slope_ref[rows, :] = lift + (pre * lift) * (1.0 - bend) * (
                gelu_root + (3.0 * gelu_root * gelu_cubic) * square
            )

    tile = pl.BlockSpec((width, block), lambda i, _: (0, i))
    return call(
        body, "hidden", (2 * half,),
        [
            whole_spec(weight),
            pl.BlockSpec((depth, block), lambda i, _: (0, jnp.minimum(i, half - 1))),
            pl.BlockSpec((depth, block), lambda i, _: (0, jnp.maximum(i - half, 0))),
            whole_spec(columns),
        ],
        (weight, own, other, columns),
        [tile, tile],
        [shape(width, 2 * count), shape(width, 2 * count, dtype=jnp.float32)],
    )


def hidden_back(weight, own, other, slope):
    depth, width = weight.shape
    count = own.shape[1]
    block = 256
    half = count // block

    def body(_, w_ref, own_ref, other_ref, s_ref, o_ref, sum_ref):
        tokens = jnp.where(pl.program_id(0) < half, own_ref[...], other_ref[...])

        @pl.when(pl.program_id(0) == 0)
        def _():
            sum_ref[...] = jnp.zeros_like(sum_ref)

        for rows in chunks(width, 256):
            grad = (tn(w_ref[:, rows], tokens) * s_ref[rows, :]).astype(jnp.bfloat16)
            o_ref[rows, :] = grad
            grad = grad.astype(jnp.float32)
            sum_ref[rows, :] += grad[:, :128] + grad[:, 128:]

    tile = pl.BlockSpec((width, block), lambda i, _: (0, i))
    return call(
        body, "hidden_back", (2 * half,),
        [
            whole_spec(weight),
            pl.BlockSpec((depth, block), lambda i, _: (0, jnp.minimum(i, half - 1))),
            pl.BlockSpec((depth, block), lambda i, _: (0, jnp.maximum(i - half, 0))),
            tile,
        ],
        (weight, own, other, slope),
        [tile, pl.BlockSpec((width, 128), lambda i, _: (0, 0))],
        [shape(width, 2 * count), shape(width, 128, dtype=jnp.float32)], vmem=WIDE_VMEM,
    )


def mapped(weight, tokens, part, turn, received=None):
    depth, count = weight.shape[0 if turn else 1], tokens.shape[1] // 2
    rows = weight.shape[1 if turn else 0]
    block = rows if turn else 400
    step = 256 if turn else block

    def body(_, w_ref, t_ref, *refs):
        o_ref = refs[-1]
        for cut in chunks(block, step):
            part = tn(w_ref[:, cut], t_ref[...]) if turn else nn(w_ref[cut, :], t_ref[...])
            if received is not None:
                part = part + refs[0][cut, :].astype(jnp.float32)
            o_ref[cut, :] = part.astype(jnp.bfloat16)

    extra = () if received is None else (received,)
    if turn:
        cols = 256
        grid = (count // cols,)
        tile = pl.BlockSpec((rows, cols), lambda i, _: (0, i))
        specs = [
            whole_spec(weight),
            pl.BlockSpec((depth, cols), lambda i, _: (0, part * (count // cols) + i)),
        ] + [tile] * len(extra)
    else:
        grid = (rows // block,)
        tile = pl.BlockSpec((block, count), lambda i, _: (i, 0))
        specs = [
            pl.BlockSpec((block, depth), lambda i, _: (i, 0)),
            pl.BlockSpec((depth, count), lambda i, _: (0, part)),
        ] + [tile] * len(extra)
    return call(body, "mapped", grid, specs, (weight, tokens) + extra, tile, shape(rows, count))


def mapped_three(weight, parts, part, received=None):
    count = parts.shape[1] // 2
    _, rows, width = weight.shape
    block = 400

    def body(_, w_ref, p_ref, *refs):
        total = sum(nn(w_ref[(i + 1) % 3], p_ref[i * width : (i + 1) * width, :]) for i in range(3))
        if received is not None:
            total = total + refs[0][...].astype(jnp.float32)
        refs[-1][...] = total.astype(refs[-1].dtype)

    tile = pl.BlockSpec((block, count), lambda i, _: (i, 0))
    extra = () if received is None else (received,)
    return call(
        body, "mapped_three", (rows // block,),
        [
            pl.BlockSpec((3, block, width), lambda i, _: (0, i, 0)),
            pl.BlockSpec((3 * width, count), lambda i, _: (0, part)),
        ] + [tile] * len(extra),
        (weight, parts) + extra,
        tile,
        shape(rows, count, dtype=jnp.bfloat16 if received is None else jnp.float32),
    )


def attended_back(weight, own, other):
    width, depth = weight.shape
    count = own.shape[1]

    def body(_, w_ref, own_ref, other_ref, o_ref):
        def run(ref):
            for cols in chunks(count, 256):
                o_ref[:, cols] = nn(w_ref[...], ref[:, cols]).astype(jnp.bfloat16)

        pl.when(pl.program_id(0) == 0)(lambda: run(own_ref))
        pl.when(pl.program_id(0) == 1)(lambda: run(other_ref))

    return call(
        body, "attended_back", (2,),
        [whole_spec(weight), whole_spec(own), whole_spec(other)],
        (weight, own, other),
        pl.BlockSpec((width, count), lambda i, _: (0, i)),
        shape(width, 2 * count),
    )


def weight_grad(sources, place_of, blocks, parts):
    rows, count = sources[0][0].shape
    size = rows // parts
    widths = [part[1] for _, _, _, part in sources]

    def body(_, *refs):
        o_ref, at = refs[-1], 0
        for i, width in enumerate(widths):
            own_ref, other_ref, r_ref = refs[3 * i : 3 * i + 3]
            grad = nt(own_ref[0], r_ref[:, :count]) + nt(other_ref[0], r_ref[:, count:])
            o_ref[0, :, at : at + width] = grad.astype(bf16)
            at += width

    tile = pl.BlockSpec((1, size, count), lambda i, s: (place_of(i, s), 0, 0))
    specs, args = [], []
    for own, other, right, (place, width) in sources:
        specs += [tile, tile, pl.BlockSpec((width, 2 * count), lambda i, s, place=place: (place, 0))]
        args += [own.reshape(parts, size, count), other.reshape(parts, size, count), right]
    return call(
        body, "weight_grad", (blocks,), specs, tuple(args),
        pl.BlockSpec((1, size, sum(widths)), lambda i, s: (i, 0, 0)),
        shape(blocks, size, sum(widths)), vmem=WIDE_VMEM,
    )


SWAP = ((0, 1), (1, 0))
f32 = jnp.float32
bf16 = jnp.bfloat16


def row_swap(value):
    return lax.ppermute(value, "row", SWAP)


def col_swap(value):
    return lax.ppermute(value, "col", SWAP)


def dp_xor(value, mask):
    return lax.ppermute(value, "dp", [(i, i ^ mask) for i in range(lax.axis_size("dp"))])


def after(value, *marks):
    return lax.optimization_barrier((value,) + marks)[0] if marks else value


def ordered(at, first, second, axis):
    return jnp.where(
        at == 0,
        jnp.concatenate([first, second], axis=axis),
        jnp.concatenate([second, first], axis=axis),
    )


def half_of(at, value, axis):
    size = value.shape[axis] // 2
    return jnp.where(
        at == 0,
        lax.slice_in_dim(value, 0, size, axis=axis),
        lax.slice_in_dim(value, size, 2 * size, axis=axis),
    )


def pick(value, at, axis):
    return lax.dynamic_index_in_dim(value, at, axis, keepdims=False)


def plus(a, b):
    return a.astype(f32) + b.astype(f32)


def pad_to(value, size, axis):
    widths = [(0, 0)] * value.ndim
    widths[axis] = (0, size - value.shape[axis])
    return jnp.pad(value, widths)


def head_slots(c, value, tail, axis, most):
    cut = lambda low, high: lax.slice_in_dim(value, low, high, axis=axis)
    size, spare = value.shape[axis], tail.shape[axis]
    less = most - HEAD_DIM
    first = jnp.where(c == 0, cut(0, most), pad_to(cut(spare, spare + less), most, axis))
    second = jnp.where(
        c == 0,
        pad_to(jnp.concatenate([cut(most, size), tail], axis=axis), most, axis),
        pad_to(cut(spare + less, size), most, axis),
    )
    return first, second


def from_slots(c, first, second, axis, spare):
    cut = lambda value, low, high: lax.slice_in_dim(value, low, high, axis=axis)
    most = first.shape[axis]
    less = most - HEAD_DIM
    tail = col_swap(cut(second, less - spare, less))
    return jnp.where(
        c == 0,
        jnp.concatenate([first, cut(second, 0, less - spare)], axis=axis),
        jnp.concatenate([tail, cut(first, 0, less), cut(second, 0, less)], axis=axis),
    )


def put_slots(o_ref, q_ref, t_ref, core, second, most):
    size, spare = q_ref.shape[-1], t_ref.shape[-1]
    less = most - HEAD_DIM

    @pl.when((core == 0) & (second == 0))
    def _():
        o_ref[...] = q_ref[:, 0, :, :most]

    @pl.when((core == 0) & (second == 1))
    def _():
        o_ref[...] = jnp.zeros_like(o_ref)
        o_ref[:, :, : size - most] = q_ref[:, 0, :, most:]
        o_ref[:, :, size - most : size - most + spare] = t_ref[:, 0]

    @pl.when((core == 1) & (second == 0))
    def _():
        o_ref[...] = jnp.zeros_like(o_ref)
        o_ref[:, :, :less] = q_ref[:, 0, :, spare : spare + less]

    @pl.when((core == 1) & (second == 1))
    def _():
        o_ref[...] = jnp.zeros_like(o_ref)
        o_ref[:, :, :less] = q_ref[:, 0, :, spare + less :]


def put_half(o_ref, f_ref, second):
    wide = f_ref.shape[-1] // 2

    @pl.when(second == 0)
    def _():
        o_ref[...] = f_ref[0, :, :wide]

    @pl.when(second == 1)
    def _():
        o_ref[...] = f_ref[0, :, wide:]


def quarters(value):
    return value.reshape(value.shape[:-2] + (4, value.shape[-2] // 4, value.shape[-1]))


def pack_heads(qkv, tail, most):
    rows, size, spare = qkv.shape[1] // 4, qkv.shape[2], tail.shape[2]

    def body(s_ref, q_ref, t_ref, o_ref):
        put_slots(o_ref, q_ref, t_ref, s_ref[COL], s_ref[PEER], most)

    return call(
        body, "pack_heads", (3,),
        [
            pl.BlockSpec((1, 1, rows, size), lambda i, s: (i, s[QUARTER], 0, 0)),
            pl.BlockSpec((1, 1, rows, spare), lambda i, s: (i, s[QUARTER], 0, 0)),
        ],
        (quarters(qkv), quarters(tail)),
        pl.BlockSpec((1, rows, most), lambda i, s: (i, 0, 0)), shape(3, rows, most),
        vmem=WIDE_VMEM,
    )


def pack(fc, proj):
    rows, wide = fc.shape[0] // 4, fc.shape[1] // 2

    def body(s_ref, f_ref, p_ref, fo_ref, po_ref):
        put_half(fo_ref, f_ref, s_ref[PEER])
        put_half(po_ref, p_ref, s_ref[PEER])

    return call(
        body, "pack", (1,),
        [pl.BlockSpec((1, rows, 2 * wide), lambda i, s: (s[QUARTER], 0, 0))] * 2,
        (quarters(fc), quarters(proj)),
        [pl.BlockSpec((rows, wide), lambda i, s: (0, 0))] * 2,
        [shape(rows, wide)] * 2,
        vmem=WIDE_VMEM,
    )


def own_rows(mine, tail, width):
    three = mine.ndim == 3
    rows, size = mine.shape[-2] // 4, mine.shape[-1]

    def body(s_ref, m_ref, *refs):
        t_ref, o_ref = refs if three else (None,) + refs
        if three:
            put_slots(o_ref.at[:, 0], m_ref, t_ref, s_ref[COL], s_ref[ROW], width)
        else:
            put_half(o_ref.at[0], m_ref, s_ref[ROW])

    lead, zero = ((3,), (0,)) if three else ((), ())
    block = lambda width, at: pl.BlockSpec(lead + (1, rows, width), lambda i, s: zero + (at(i, s), 0, 0))
    own = lambda i, s: i
    return call(
        body, "own_rows", (4,),
        [block(size, own)] + ([block(tail.shape[-1], own)] if three else []),
        tuple([quarters(mine)] + ([quarters(tail)] if three else [])),
        block(width, lambda i, s: 4 * s[ROW] + i), shape(*lead, 8, rows, width),
        vmem=WIDE_VMEM,
    )


def all_rows(held, got):
    lead, tile = held.shape[:-3], held.shape[-2:]
    zero = (0,) * len(lead)

    def body(s_ref, h_ref, *refs):
        o_ref = refs[-1]
        place = (pl.program_id(0) // 2 != s_ref[LOW_Z]) * 2 + (pl.program_id(0) % 2 != s_ref[LOW_Y])
        for i in range(4):

            @pl.when(place == i)
            def _(i=i):
                o_ref[...] = refs[i][...].reshape(o_ref.shape)

    fetched = pl.BlockSpec(lead + tile, lambda i, s: zero + (0, 0))
    out = pl.pallas_call(
        body,
        grid_spec=pltpu.PrefetchScalarGridSpec(
            num_scalar_prefetch=1,
            grid=(4,),
            in_specs=[pl.BlockSpec(memory_space=pl.ANY)] + [fetched] * 4,
            out_specs=pl.BlockSpec(lead + (1,) + tile, lambda i, s: zero + (4 * s[PEER] + i, 0, 0)),
        ),
        out_shape=shape(*held.shape),
        input_output_aliases={1: 0},
        compiler_params=pltpu.CompilerParams(vmem_limit_bytes=WIDE_VMEM),
        cost_estimate=pl.CostEstimate(flops=0, bytes_accessed=0, transcendentals=0),
        name="all_rows",
    )(Here.places, held, *got)
    return out.reshape(lead + (8 * tile[0], tile[1]))


def half_rows(value, at):
    rows, count = value.shape[0] // 2, value.shape[1]

    def body(_, a_ref, o_ref):
        o_ref[...] = a_ref[...].astype(bf16)

    return call(
        body, "half_rows", (count // 256,),
        [pl.BlockSpec((rows, 256), lambda i, s: (s[at], i))], (value,),
        pl.BlockSpec((rows, 256), lambda i, s: (0, i)), shape(rows, count),
    )


def packed_sums(sums_two, sums_one, grad_own, hidden_sums, parts, most):
    width, half = sums_two.shape[1], sums_one.shape[1]

    def body(_, two_ref, one_ref, grad_ref, hid_ref, p_ref, o_ref):
        def over(value):
            ones = jnp.ones((8, value.shape[1]), value.dtype)
            exact = lax.Precision.HIGHEST if value.dtype == f32 else None
            return lax.dot_general(
                ones, value, (((1,), (1,)), ((), ())), preferred_element_type=f32, precision=exact
            )[0:1]

        o_ref[...] = jnp.zeros_like(o_ref)
        for i in range(3):
            o_ref[i : i + 1, :] = over(two_ref[i])
        o_ref[3:4, :half] = over(one_ref[0])
        o_ref[3:4, half:] = over(one_ref[1])
        o_ref[4:5, :half] = over(grad_ref[...])
        o_ref[8:9, :] = over(hid_ref[...])
        o_ref[9:10, :most] = over(p_ref[2 * most :, :])
        o_ref[10:11, :most] = over(p_ref[most : 2 * most, :])

    args = (sums_two, sums_one, grad_own, hidden_sums, parts)
    return call(
        body, "packed_sums", (1,), [whole_spec(v) for v in args], args,
        pl.BlockSpec((16, width), lambda i, s: (0, 0)), shape(16, width, dtype=f32),
    )


def sums_added(a, b, rows):
    def body(_, a_ref, b_ref, o_ref):
        at = lax.broadcasted_iota(jnp.int32, a_ref.shape, 0)
        o_ref[...] = a_ref[...] + jnp.where(at < rows, b_ref[...], 0.0)

    spec = whole_spec(a)
    return call(body, "sums_added", (1,), [spec, spec], (a, b), spec, shape(*a.shape, dtype=f32))


def spread_index(sizes, axis, step, value):
    places = []
    for size in reversed(sizes):
        places.insert(0, step % size)
        step = step // size
    places.insert(axis, value)
    return tuple(places) + (0, 0)


def halved(keep, got, axis, at):
    lead, tile = keep.shape[:-2], keep.shape[-2:]
    rest = lead[:axis] + lead[axis + 1 :]

    def body(_, a_ref, b_ref, c_ref, d_ref, keep_ref, send_ref):
        keep_ref[...] = (a_ref[...].astype(f32) + b_ref[...].astype(f32)).astype(bf16).reshape(keep_ref.shape)
        send_ref[...] = (c_ref[...].astype(f32) + d_ref[...].astype(f32)).astype(bf16).reshape(send_ref.shape)

    ones = (1,) * len(lead)
    mine = pl.BlockSpec(ones + tile, lambda i, s: spread_index(rest, axis, i, s[at]))
    theirs = pl.BlockSpec(ones + tile, lambda i, s: spread_index(rest, axis, i, 1 - s[at]))
    steps = math.prod(rest)
    out = pl.BlockSpec((1,) + tile, lambda i, s: (i, 0, 0))
    first, second = call(
        body, "halved", (steps,), [mine, mine, theirs, theirs], (keep, got, keep, got),
        [out, out], [shape(steps, *tile)] * 2,
    )
    return first.reshape(rest + tile), second.reshape(rest + tile)


def added(a, b):
    def body(_, a_ref, b_ref, o_ref):
        o_ref[...] = (a_ref[...].astype(f32) + b_ref[...].astype(f32)).astype(bf16)

    spec = whole_spec(a)
    return call(body, "added", (1,), [spec, spec], (a, b), spec, shape(*a.shape))


def chosen(a, b):
    def body(s_ref, a_ref, b_ref, o_ref):
        o_ref[...] = jnp.where(s_ref[SAME] == 1, a_ref[...], b_ref[...])

    spec = whole_spec(a)
    return call(body, "chosen", (1,), [spec, spec], (a, b), spec, shape(*a.shape))


def paired(at, first, second, axis):
    lead, tile = first.shape[:-2], first.shape[-2:]
    ones = (1,) * len(lead)
    steps = math.prod(lead)

    def body(_, a_ref, b_ref, o_ref):
        @pl.when(pl.program_id(0) == 0)
        def _():
            o_ref[...] = a_ref[...].reshape(o_ref.shape)

        @pl.when(pl.program_id(0) == 1)
        def _():
            o_ref[...] = b_ref[...].reshape(o_ref.shape)

    def place(step):
        return spread_index(lead, len(lead), step, 0)[: len(lead)] + (0, 0)

    out = lambda i, j, s: spread_index(lead, axis, j, jnp.where(i == 0, s[at], 1 - s[at]))
    return call(
        body, "paired", (2, steps),
        [
            pl.BlockSpec(ones + tile, lambda i, j, s: place(jnp.where(i == 0, j, steps - 1))),
            pl.BlockSpec(ones + tile, lambda i, j, s: place(jnp.where(i == 1, j, 0))),
        ],
        (first, second),
        pl.BlockSpec(ones + (1,) + tile, out),
        shape(*lead[:axis], 2, *lead[axis:], *tile),
    )


def widened(keep, got, at, y_last):
    rows, width = keep.shape[-2:]

    def body(s_ref, a_ref, b_ref, c_ref, d_ref, o_ref):
        if y_last:
            swap = s_ref[at] == 1
            o_ref[:, :width] = jnp.where(swap, b_ref[0, 0], a_ref[0, 0]).astype(f32)
            o_ref[:, width:] = jnp.where(swap, a_ref[0, 0], b_ref[0, 0]).astype(f32)
        else:
            other = pl.program_id(0) % 2 != s_ref[at]
            o_ref[:, :width] = jnp.where(other, b_ref[0, 0], a_ref[0, 0]).astype(f32)
            o_ref[:, width:] = jnp.where(other, d_ref[0, 0], c_ref[0, 0]).astype(f32)

    tile = (1, 1, rows, width)
    if y_last:
        one = pl.BlockSpec(tile, lambda i, s: (i // 2, i % 2, 0, 0))
        none = pl.BlockSpec(tile, lambda i, s: (0, 0, 0, 0))
        specs = [one, one, none, none]
    else:
        specs = [pl.BlockSpec(tile, lambda i, s, f=f: (f, i // 2, 0, 0)) for f in (0, 0, 1, 1)]
    return call(
        body, "widened", (4,), specs, (keep, got, keep, got),
        pl.BlockSpec((rows, 2 * width), lambda i, s: (i, 0)),
        shape(4 * rows, 2 * width, dtype=f32),
    )


def tails_of(keep, got, at, y_last, most, low, high):
    rows, width = keep.shape[-2:]
    count = width // most

    def body(s_ref, a_ref, b_ref, o_ref):
        second = jnp.where((s_ref[at] == 1) if y_last else (pl.program_id(0) % 2 == s_ref[at]), a_ref[0, 0], b_ref[0, 0])
        for i in range(count):
            o_ref[i, 0] = second[:, i * most + low : i * most + high]

    tile = (1, 1, rows, width)
    where = (lambda i, s: (i // 2, i % 2, 0, 0)) if y_last else (lambda i, s: (1, i // 2, 0, 0))
    return call(
        body, "tails_of", (4,), [pl.BlockSpec(tile, where)] * 2, (keep, got),
        pl.BlockSpec((count, 1, rows, high - low), lambda i, s: (0, i, 0, 0)),
        shape(count, 4, rows, high - low),
    )


def unslotted(keep, got, tails, at, y_last, most, size):
    rows, width = keep.shape[-2:]
    count, spare, less = width // most, tails.shape[-1], most - HEAD_DIM

    def body(s_ref, a_ref, b_ref, c_ref, d_ref, t_ref, o_ref):
        if y_last:
            swap = s_ref[at] == 1
            first = jnp.where(swap, b_ref[0, 0], a_ref[0, 0])
            second = jnp.where(swap, a_ref[0, 0], b_ref[0, 0])
        else:
            other = pl.program_id(0) % 2 != s_ref[at]
            first = jnp.where(other, b_ref[0, 0], a_ref[0, 0])
            second = jnp.where(other, d_ref[0, 0], c_ref[0, 0])
        first, second = first.astype(f32), second.astype(f32)

        @pl.when(s_ref[COL] == 0)
        def _():
            for i in range(count):
                o_ref[i, :, :most] = first[:, i * most : (i + 1) * most]
                o_ref[i, :, most:] = second[:, i * most : i * most + size - most]

        @pl.when(s_ref[COL] == 1)
        def _():
            for i in range(count):
                o_ref[i, :, :spare] = t_ref[i, 0].astype(f32)
                o_ref[i, :, spare : spare + less] = first[:, i * most : i * most + less]
                o_ref[i, :, spare + less :] = second[:, i * most : i * most + less]

    tile = (1, 1, rows, width)
    if y_last:
        one = pl.BlockSpec(tile, lambda i, s: (i // 2, i % 2, 0, 0))
        none = pl.BlockSpec(tile, lambda i, s: (0, 0, 0, 0))
        specs = [one, one, none, none]
    else:
        specs = [pl.BlockSpec(tile, lambda i, s, f=f: (f, i // 2, 0, 0)) for f in (0, 0, 1, 1)]
    return call(
        body, "unslotted", (4,),
        specs + [pl.BlockSpec((count, 1, rows, spare), lambda i, s: (0, i, 0, 0))],
        (keep, got, keep, got, tails),
        pl.BlockSpec((count, rows, size), lambda i, s: (0, i, 0)),
        shape(count, 4 * rows, size, dtype=f32),
    )


TOKENS = 256


def tile_of(rows, at=None):
    if at is None:
        return pl.BlockSpec((rows, TOKENS), lambda i, s: (0, i))
    return pl.BlockSpec((rows, TOKENS), lambda i, s: (at(s), i))


def norm_stats(parts):
    count = sum(part.shape[0] for part in parts)
    center = sum(jnp.sum(part, axis=0, keepdims=True) for part in parts) / count
    spread = sum(jnp.sum((part - center) * (part - center), axis=0, keepdims=True) for part in parts) / count
    return center, lax.rsqrt(spread + 1e-05)


def norm_one(x_own, x_peer, columns):
    half, count = x_own.shape

    def body(s_ref, own_ref, peer_ref, c_ref, h_ref, stat_ref):
        own, peer = own_ref[...].astype(f32), peer_ref[...].astype(f32)
        parts = [jnp.where(s_ref[ROW] == 0, own, peer), jnp.where(s_ref[ROW] == 0, peer, own)]
        center, inverse = norm_stats(parts)
        stat_ref[0:1, :] = center
        stat_ref[1:2, :] = inverse
        for i, part in enumerate(parts):
            rows = slice(i * half, (i + 1) * half)
            h_ref[rows, :] = ((part - center) * inverse * c_ref[rows, 0:1] + c_ref[rows, 1:2]).astype(bf16)

    return call(
        body, "norm_one", (count // TOKENS,),
        [tile_of(half), tile_of(half), whole_spec(columns)],
        (x_own, x_peer, columns),
        [tile_of(2 * half), tile_of(8)],
        [shape(2 * half, count), shape(8, count, dtype=f32)],
    )


def norm_two(x_own, x_peer, low, other, columns):
    half, count = x_own.shape

    def body(s_ref, own_ref, peer_ref, low_ref, other_ref, c_ref, x_ref, h_ref, stat_ref):
        own, peer = own_ref[...].astype(f32), peer_ref[...].astype(f32)
        parts = [jnp.where(s_ref[ROW] == 0, own, peer), jnp.where(s_ref[ROW] == 0, peer, own)]
        for i in range(2):
            rows = slice(i * half, (i + 1) * half)
            branch = low_ref[rows, :].astype(f32) + other_ref[rows, :].astype(f32) + c_ref[rows, 2:3]
            parts[i] = parts[i] + branch
            x_ref[rows, :] = parts[i]
        center, inverse = norm_stats(parts)
        stat_ref[0:1, :] = center
        stat_ref[1:2, :] = inverse
        for i, part in enumerate(parts):
            rows = slice(i * half, (i + 1) * half)
            h_ref[rows, :] = ((part - center) * inverse * c_ref[rows, 3:4] + c_ref[rows, 4:5]).astype(bf16)

    full = tile_of(2 * half)
    return call(
        body, "norm_two", (count // TOKENS,),
        [tile_of(half), tile_of(half), full, full, whole_spec(columns)],
        (x_own, x_peer, low, other, columns),
        [full, full, tile_of(8)],
        [shape(2 * half, count, dtype=f32), shape(2 * half, count), shape(8, count, dtype=f32)],
    )


def lanes_summed(ref, at, value, first):
    total = sum(value[:, i : i + 128] for i in range(0, value.shape[1], 128))

    @pl.when(first)
    def _():
        ref[at] = total

    @pl.when(jnp.logical_not(first))
    def _():
        ref[at] += total


def norm_two_back(low, other, grad, x_mid, stats, columns):
    width, count = low.shape

    def body(_, low_ref, other_ref, g_ref, x_ref, stat_ref, gain_ref, mid_ref, branch_ref, sum_ref):
        first = pl.program_id(0) == 0
        incoming = low_ref[...].astype(f32) + other_ref[...].astype(f32)
        inverse = stat_ref[1:2, :]
        normed = (x_ref[...] - stat_ref[0:1, :]) * inverse
        scaled = incoming * gain_ref[:, 3:4]
        mean = jnp.sum(scaled, axis=0, keepdims=True) / width
        along = jnp.sum(scaled * normed, axis=0, keepdims=True) / width
        mid = g_ref[...].astype(f32) + inverse * (scaled - mean - normed * along)
        mid_ref[...] = mid
        branch = mid.astype(bf16)
        branch_ref[...] = branch
        lanes_summed(sum_ref, 0, incoming * normed, first)
        lanes_summed(sum_ref, 1, incoming, first)
        lanes_summed(sum_ref, 2, branch.astype(f32), first)

    full = tile_of(width)
    return call(
        body, "norm_two_back", (count // TOKENS,),
        [full, full, full, full, tile_of(8), whole_spec(columns)],
        (low, other, grad, x_mid, stats, columns),
        [full, full, pl.BlockSpec((3, width, 128), lambda i, s: (0, 0, 0))],
        [shape(width, count, dtype=f32), shape(width, count), shape(3, width, 128, dtype=f32)],
    )


def norm_one_sums(mine, other, x_own, stats, columns):
    half, count = x_own.shape

    def body(_, m_ref, o_ref, x_ref, stat_ref, gain_ref, row_ref, sum_ref):
        first = pl.program_id(0) == 0
        incoming = m_ref[...] + o_ref[...].astype(f32)
        normed = (x_ref[...].astype(f32) - stat_ref[0:1, :]) * stat_ref[1:2, :]
        scaled = incoming * gain_ref[:, 0:1]
        row_ref[...] = jnp.zeros_like(row_ref)
        row_ref[0:1, :] = jnp.sum(scaled, axis=0, keepdims=True)
        row_ref[1:2, :] = jnp.sum(scaled * normed, axis=0, keepdims=True)
        lanes_summed(sum_ref, 0, incoming * normed, first)
        lanes_summed(sum_ref, 1, incoming, first)

    return call(
        body, "norm_one_sums", (count // TOKENS,),
        [tile_of(half, lambda s: s[ROW]), tile_of(half), tile_of(half), tile_of(8), pl.BlockSpec((half, columns.shape[1]), lambda i, s: (s[ROW], 0))],
        (mine, other, x_own, stats, columns),
        [tile_of(8), pl.BlockSpec((2, half, 128), lambda i, s: (0, 0, 0))],
        [shape(8, count, dtype=f32), shape(2, half, 128, dtype=f32)],
    )


def norm_one_back(mine, other, x_own, stats, columns, mid_grad, sums, sums_peer):
    half, count = x_own.shape

    def body(_, m_ref, o_ref, x_ref, stat_ref, gain_ref, mid_ref, a_ref, b_ref, out_ref):
        inverse = stat_ref[1:2, :]
        normed = (x_ref[...].astype(f32) - stat_ref[0:1, :]) * inverse
        scaled = (m_ref[...] + o_ref[...].astype(f32)) * gain_ref[:, 0:1]
        means = (a_ref[...] + b_ref[...]) / (2 * half)
        out_ref[...] = mid_ref[...] + inverse * (scaled - means[0:1, :] - normed * means[1:2, :])

    mine_tile = tile_of(half, lambda s: s[ROW])
    return call(
        body, "norm_one_back", (count // TOKENS,),
        [mine_tile, tile_of(half), tile_of(half), tile_of(8), pl.BlockSpec((half, columns.shape[1]), lambda i, s: (s[ROW], 0)), mine_tile, tile_of(8), tile_of(8)],
        (mine, other, x_own, stats, columns, mid_grad, sums, sums_peer),
        tile_of(half), shape(half, count, dtype=f32),
    )


def block_result(x_mid, part, other, columns):
    half, count = other.shape

    def body(_, x_ref, p_ref, o_ref, b_ref, out_ref):
        out_ref[...] = (x_ref[...] + (p_ref[...].astype(f32) + o_ref[...].astype(f32)) + b_ref[:, 6:7]).astype(bf16)

    mine_tile = tile_of(half, lambda s: s[ROW])
    return call(
        body, "block_result", (count // TOKENS,),
        [mine_tile, mine_tile, tile_of(half), pl.BlockSpec((half, columns.shape[1]), lambda i, s: (s[ROW], 0))],
        (x_mid, part, other, columns),
        tile_of(half), shape(half, count),
    )


class Fetch:
    def __init__(self, sent):
        self.got = [row_swap(sent)]

    def more(self, *marks):
        first = after(self.got[0], *marks)
        self.got = [first, dp_xor(first, 1), dp_xor(first, 2)]

    def rest(self, first, *marks):
        self.got.append(dp_xor(after(self.got[first], *marks), 3 - first))
        return self.got


class Total:
    def __init__(self, sources, r, k, y_first, y_last, *marks):
        self.rows, self.width = sources[0][0].shape[0], sum(part[1] for _, _, _, part in sources)
        self.r, self.k, self.y_first, self.y_last = r, k, y_first, y_last
        self.fast = lax.axis_size("dp") == 8
        tied = lambda marks: [(own, other, after(right, *marks), part) for own, other, right, part in sources]
        if not self.fast:
            self.grad = weight_grad(tied(marks), lambda i, s: i, 4, 4)
            return
        if y_first:
            send, keep = (lambda i, s: 2 * (1 - s[LOW_Y]) + i), (lambda i, s: 2 * s[LOW_Y] + i)
            blocks, parts, mask = 2, 4, 1
        else:
            send, keep = (lambda i, s: 1 - s[LOW_Z] + 2 * i), (lambda i, s: s[LOW_Z] + 2 * i)
            blocks, parts, mask = 4, 8, 2
        shaped = lambda v: v.reshape(2, 2, self.rows // 8, self.width)
        sent = weight_grad(tied(marks), send, blocks, parts)
        self.got, self.sent = dp_xor(shaped(sent), mask), [sent]
        self.kept = lambda *marks: shaped(weight_grad(tied(marks), keep, blocks, parts))

    def hold(self, *marks):
        if self.fast:
            self.keep = self.kept(*marks)
        return self.marks()

    def marks(self):
        return [self.keep] if self.fast else []

    def sent_marks(self):
        return self.sent if self.fast else []

    def sum_one(self, *marks):
        if self.fast:
            axis, at, mask = (1, LOW_Z, 2) if self.y_first else (0, LOW_Y, 1)
            self.keep, send = halved(after(self.keep, *marks), self.got, axis, at)
            self.got = dp_xor(send, mask)
            return [self.keep]
        return []

    def sum_two(self, *marks):
        if self.fast:
            self.keep, send = halved(after(self.keep, *marks), self.got, 0, HIGH_Z)
            self.got = dp_xor(send, 4)
            return [self.keep]
        return []

    def sum_three(self, *marks):
        if self.fast:
            cross = [
                (2 * i + j, 2 * (i ^ 1) + (j ^ 1))
                for i in range(lax.axis_size("dp"))
                for j in range(2)
                if i % 2 != j
            ]
            self.keep = added(after(self.keep, *marks), self.got)
            self.got = lax.ppermute(self.keep, ("dp", "row"), cross)
            return [self.keep]
        return []

    def spread_one(self, *marks):
        if self.fast:
            self.keep = chosen(after(self.keep, *marks), self.got)
            self.got = dp_xor(self.keep, 4)
            return [self.keep]
        return []

    def spread_two(self, *marks):
        if self.fast:
            self.keep = paired(HIGH_Z, after(self.keep, *marks), self.got, 0)
            self.got = dp_xor(self.keep, 2 if self.y_last else 1)
            return [self.keep]
        return []

    def spread_three(self, *marks):
        if self.fast:
            if self.y_last:
                self.keep = paired(LOW_Z, after(self.keep, *marks), self.got, 1)
                self.got = dp_xor(self.keep, 1)
            else:
                self.keep = paired(LOW_Y, after(self.keep, *marks), self.got, 0)
                self.got = dp_xor(self.keep, 2)
            return [self.keep]
        return []

    def tail(self, most, spare, *marks):
        if not self.fast:
            return list(marks)
        less = most - HEAD_DIM
        at = LOW_Y if self.y_last else LOW_Z
        self.keep = after(self.keep, *marks)
        tails = tails_of(self.keep, self.got, at, self.y_last, most, less - spare, less)
        self.tails = col_swap(tails)
        return [tails]

    def slots(self, c, most, spare, *marks):
        less = most - HEAD_DIM
        size = 2 * less + spare
        if not self.fast:
            both = self.result()
            cut = lambda i: [v[:, i * most : (i + 1) * most] for v in both]
            return jnp.stack([from_slots(c, *cut(i), 1, spare).astype(f32) for i in range(self.width // most)])
        at = LOW_Y if self.y_last else LOW_Z
        keep = after(self.keep, *marks)
        return unslotted(keep, self.got, self.tails, at, self.y_last, most, size)

    def wide(self, *marks):
        if self.fast:
            return widened(after(self.keep, *marks), self.got, LOW_Y if self.y_last else LOW_Z, self.y_last)
        return jnp.concatenate(self.result(), axis=1).astype(f32)

    def result(self):
        halves = self.grad.reshape(2, self.rows // 2, self.width)
        keep, got = pick(halves, self.r, 0), row_swap(pick(halves, 1 - self.r, 0))
        both = lax.psum(ordered(self.r, keep[None], got[None], 0), "dp")
        return both[0], both[1]


def hop(value, mask):
    return dp_xor(value, mask) if lax.axis_size("dp") == 8 else None


def hop_added(value, peer, *marks):
    return value if peer is None else sums_added(after(value, *marks), peer, 16)


def per_device(
    block_in,
    out_grad,
    seq_lengths,
    ln1_gain,
    ln1_bias,
    qkv_weight,
    qv_bias,
    out_weight,
    out_bias,
    ln2_gain,
    ln2_bias,
    fc_weight,
    fc_bias,
    proj_weight,
    proj_bias,
):
    n_dp = lax.axis_size("dp")
    r, c, k = lax.axis_index("row"), lax.axis_index("col"), lax.axis_index("dp")
    x_own, grad_own = block_in.T, out_grad.T
    half, tokens = x_own.shape
    heads = 7
    most = heads * HEAD_DIM
    spare = 32
    column = lambda v: v.astype(f32)[:, None]

    y, z = k % 2, (k // 2) % 2
    at = jnp.arange(8)
    held = (r, c, y, z, (k // 4) % 2, 2 * z + y, 1 - r, (y == r).astype(r.dtype))
    Here.places = sum(jnp.where(at == i, value, 0) for i, value in enumerate(held)).astype(jnp.int32)
    qkv_tail = col_swap(qkv_weight[:, :, :spare])
    proj_turned = proj_weight.T
    qkv_sent = pack_heads(qkv_weight, qkv_tail, most)
    fc_sent, proj_sent = pack(after(fc_weight, qkv_sent), proj_turned)
    qkv_fetch = Fetch(qkv_sent)
    x_peer = row_swap(after(x_own, qkv_sent))
    vectors = after(jnp.stack([ln1_gain, ln1_bias, out_bias, ln2_gain, ln2_bias]), qkv_sent)
    vectors = ordered(r, vectors, row_swap(vectors), 1)
    both = jnp.stack([half_of(r, fc_bias, 0), jnp.concatenate([proj_bias, proj_bias])])
    columns = jnp.concatenate([vectors, both, jnp.zeros_like(both[:1])]).astype(f32).T
    qv_bias = after(qv_bias, qkv_sent)
    bias_first, bias_second = head_slots(c, qv_bias, col_swap(qv_bias[:, :spare]), 1, most)
    bias_mine = jnp.where(r == 0, bias_first, bias_second).astype(f32)
    bias_mine = jnp.stack([bias_mine[0], jnp.zeros_like(bias_mine[0]), bias_mine[1]])[:, :, None]

    out_weight = after(out_weight, qkv_sent)
    out_first, out_second = head_slots(c, out_weight, col_swap(out_weight[:spare]), 0, most)
    out_mine = jnp.where(r == 0, out_first, out_second)
    out_sent = jnp.where(r == 0, out_second, out_first)
    ff_size = fc_weight.shape[1] // 2
    qkv_full = own_rows(after(qkv_weight, fc_sent, out_sent), qkv_tail, most)
    qkv_fetch.more(qkv_full)
    fc_full = own_rows(after(fc_weight, qkv_fetch.got[0]), None, ff_size)
    qkv_fetch.rest(2, fc_full)
    proj_full = own_rows(after(proj_turned, fc_full, *qkv_fetch.got[1:3]), None, ff_size)

    lengths = after(seq_lengths, qkv_sent)[0]
    group = 2 * tokens
    places = jnp.arange(group, dtype=jnp.int32)
    ends = jnp.cumsum(lengths, dtype=jnp.int32)
    first = jnp.sum(
        jnp.where(ends[None, :] <= places[:, None], lengths[None, :], 0), axis=1, dtype=jnp.int32
    ).reshape(group // BLK, BLK)
    info = jnp.concatenate([(c * (tokens // BLK))[None].astype(jnp.int32), first[:, 0] // BLK])

    h_one, stats_one = norm_one(after(x_own, proj_full, info, bias_mine), x_peer, columns)
    qkv_full = all_rows(after(qkv_full, h_one), qkv_fetch.got)
    h_one_peer = col_swap(after(h_one, qkv_full))
    out_got = row_swap(after(out_sent, qkv_full))
    fc_fetch = Fetch(after(fc_sent, qkv_full))
    proj_fetch = Fetch(after(proj_sent, qkv_full))
    projected = project(qkv_full, h_one, h_one_peer, bias_mine)
    out_full = ordered(r, after(out_mine, projected), out_got, 1)
    attended, log_totals = attend(info, after(projected, out_full), first, heads)
    fc_fetch.more(attended)
    proj_fetch.more(attended)
    other = mapped(out_full, after(attended, fc_fetch.got[0], proj_fetch.got[0]), 1, True)
    low = mapped(out_full, attended, 0, True, col_swap(other))
    branch_other = row_swap(low)
    grad_got = row_swap(after(grad_own, low))
    fc_fetch.rest(1, low)
    proj_fetch.rest(2, low)
    fc_full = all_rows(after(fc_full, low), fc_fetch.got)
    proj_full = all_rows(after(proj_full, fc_full), proj_fetch.got)
    x_mid, h_two, stats_two = norm_two(x_own, x_peer, after(low, proj_full), branch_other, columns)
    h_two_peer = col_swap(h_two)
    activated, slope = hidden(fc_full, h_two, h_two_peer, columns)
    grad_full = paired(ROW, after(grad_own, activated), grad_got, 0).reshape(2 * half, tokens)
    grad_peer = col_swap(grad_full)

    mark = [grad_peer]
    pre_grad, hidden_sums = hidden_back(proj_full, grad_full, grad_peer, slope)
    mark = [pre_grad]
    h_two_other = mapped(fc_full, after(pre_grad, *mark), 1, False)
    mark = [h_two_other]
    fc_total = Total([(h_two, h_two_peer, pre_grad, (0, ff_size))], r, k, False, True, *mark)
    mark = fc_total.sent_marks()
    low = mapped(fc_full, after(pre_grad, *mark), 0, False, col_swap(h_two_other))
    low_other, mark = row_swap(low), [low]
    proj_total = Total([(grad_full, grad_peer, activated, (0, ff_size))], r, k, True, False, *mark)
    mark = proj_total.sent_marks()
    part_other = mapped(proj_full, after(activated, *mark), 1, False)
    mark = [part_other]
    mark = proj_total.hold(*mark)
    mark = fc_total.hold(*mark)
    mark = fc_total.sum_one(*mark)
    mid_grad, branch_grad, sums_two = norm_two_back(
        after(low, *mark), low_other, grad_full, x_mid, stats_two, columns
    )
    branch_peer, mark = col_swap(branch_grad), [branch_grad]
    mark = proj_total.sum_one(*mark)
    attended_grad = attended_back(out_full, after(branch_grad, *mark), branch_peer)
    mark = [attended_grad]
    parts = attend_back(info, projected, attended, after(attended_grad, *mark), log_totals, first, heads)
    mark = [parts]
    three_other = mapped_three(qkv_full, after(parts, *mark), 1)
    mark = [three_other]
    oq_total = Total([(branch_grad, branch_peer, attended, (0, most)), (h_one, h_one_peer, parts, (2, most))], r, k, True, True, *mark)
    mark = oq_total.sent_marks()
    mark = fc_total.sum_two(*mark)
    mark = proj_total.sum_two(*mark)
    kv_total = Total([(h_one, h_one_peer, parts, (0, 2 * most))], r, k, True, False, *mark)
    mark = kv_total.sent_marks()
    proj_part = mapped(proj_full, after(activated, *mark), 0, False, col_swap(part_other))
    mark = [proj_part]
    mark = oq_total.hold(*mark)
    mark = oq_total.sum_one(*mark)
    mine = mapped_three(qkv_full, after(parts, *mark), 0, col_swap(three_other))
    mark = [mine]
    send = half_rows(after(mine, *mark), PEER)
    one_other, mark = row_swap(send), [send]
    mark = kv_total.hold(*mark)
    mark = kv_total.sum_one(*mark)
    mark = proj_total.sum_three(*mark)
    mark = fc_total.sum_three(*mark)
    mark = oq_total.sum_two(*mark)
    mark = kv_total.sum_two(*mark)
    mark = oq_total.sum_three(*mark)
    mark = proj_total.spread_one(*mark)
    mark = fc_total.spread_one(*mark)
    sums, sums_one = norm_one_sums(after(mine, *mark), one_other, x_own, stats_one, columns)
    sums_peer, mark = row_swap(sums), [sums]
    mark = kv_total.sum_three(*mark)
    mark = oq_total.spread_one(*mark)
    packed = packed_sums(sums_two, after(sums_one, *mark), grad_own, hidden_sums, parts, most)
    packed_peer, mark = col_swap(packed), [packed]
    packed = sums_added(after(packed, *mark), packed_peer, 8)
    packed_peer, mark = hop(packed, 2), [packed]
    mark = proj_total.spread_two(*mark)
    mark = kv_total.spread_one(*mark)
    packed = hop_added(packed, packed_peer, *mark)
    packed_peer, mark = hop(packed, 1), [packed]
    x_grad = norm_one_back(after(mine, *mark), one_other, x_own, stats_one, columns, mid_grad, sums, sums_peer)
    mark = [x_grad]
    mark = fc_total.spread_two(*mark)
    mark = kv_total.spread_two(*mark)
    mark = oq_total.spread_two(*mark)
    mark = kv_total.spread_three(*mark)
    packed = hop_added(packed, packed_peer, *mark)
    packed_peer, mark = hop(packed, 4), [packed]
    mark = oq_total.spread_three(*mark)
    packed = hop_added(packed, packed_peer, *mark)
    if n_dp != 8:
        for i in range(n_dp.bit_length() - 1):
            packed = sums_added(packed, dp_xor(packed, 1 << i), 16)
    packed_peer, mark = row_swap(packed), [packed]
    mark = proj_total.spread_three(*mark)
    packed_peer = after(packed_peer, *mark)
    mark = [packed_peer]
    mark = fc_total.spread_three(*mark)
    mark = kv_total.tail(most, spare, *mark)
    mark = oq_total.tail(most, spare, *mark)
    send = half_rows(after(proj_part, *mark), PEER)
    block_other, mark = row_swap(send), [send]
    whole = oq_total.slots(c, most, spare, *mark)
    out_weight_grad = whole[0]
    q_weight_grad = whole[1]
    mark = [whole]
    whole = kv_total.slots(c, most, spare, *mark)
    k_weight_grad = whole[0]
    v_weight_grad = whole[1]
    mark = [whole]
    block_out = block_result(after(x_mid, *mark), proj_part, block_other, columns)
    mark = [block_out]
    fc_weight_grad = fc_total.wide(*mark)
    mark = [fc_weight_grad]
    proj_weight_grad = proj_total.wide(*mark).T
    mark = [proj_weight_grad]

    own = half_of(r, packed, 1)
    fc_bias_grad = ordered(r, packed[8], packed_peer[8], 0)
    qv_mine, qv_peer = packed[9:11, :most], packed_peer[9:11, :most]
    qv_bias_grad = from_slots(
        c, jnp.where(r == 0, qv_mine, qv_peer), jnp.where(r == 0, qv_peer, qv_mine), 1, spare
    )
    qkv_weight_grad = jnp.stack([q_weight_grad, k_weight_grad, v_weight_grad])
    out_weight_grad = out_weight_grad.T
    return (
        block_out.T,
        x_grad.T,
        packed[3, :half],
        packed[3, half:],
        qkv_weight_grad,
        qv_bias_grad,
        out_weight_grad,
        own[2],
        own[0],
        own[1],
        fc_weight_grad,
        fc_bias_grad,
        proj_weight_grad,
        packed[4, :half],
    )


def solution(mesh):
    placed = (
        P(("dp", "col"), "row"),
        P(("dp", "col"), "row"),
        P("dp", None),
        P("row"),
        P("row"),
        P(None, "row", "col"),
        P(None, "col"),
        P("col", "row"),
        P("row"),
        P("row"),
        P("row"),
        P("row", "col"),
        P("col"),
        P("col", "row"),
        P("row"),
    )
    return jax.shard_map(
        per_device,
        mesh=mesh,
        in_specs=placed,
        out_specs=(
            P(("dp", "col"), "row"),
            P(("dp", "col"), "row"),
            P("row"),
            P("row"),
            P(None, "row", "col"),
            P(None, "col"),
            P("col", "row"),
            P("row"),
            P("row"),
            P("row"),
            P("row", "col"),
            P("col"),
            P("col", "row"),
            P("row"),
        ),
        check_vma=False,
    )
```

```python
import functools
import math

import jax
import jax.numpy as jnp
from jax import lax
from jax.experimental import pallas as pl
from jax.experimental.pallas import tpu as pltpu
from jax.sharding import PartitionSpec as P

HEAD_DIM = 64
gelu_root = math.sqrt(2.0 / math.pi)
gelu_cubic = 0.044715
BLK = 256
NEG = -1e30
KERNEL_VMEM = 40 * 2**20
WIDE_VMEM = 58 * 2**20


def dot_over(dims, a, b):
    return lax.dot_general(a, b, (dims, ((), ())), preferred_element_type=jnp.float32)


def nn(a, b):
    return dot_over(((1,), (0,)), a, b)


def nt(a, b):
    return dot_over(((1,), (1,)), a, b)


def tn(a, b):
    return dot_over(((0,), (0,)), a, b)


def head_rows(h):
    return slice(h * HEAD_DIM, (h + 1) * HEAD_DIM)


def allowed_tile(i, j, first):
    keys = j * BLK + lax.broadcasted_iota(jnp.int32, (BLK, BLK), 0)
    queries = i * BLK + lax.broadcasted_iota(jnp.int32, (BLK, BLK), 1)
    return (keys >= first) & (keys <= queries)


def turned(x):
    return jnp.transpose(x.astype(jnp.float32)).astype(jnp.bfloat16)


def attend_kernel(heads, blocks, info_ref, q_ref, k_ref, v_ref, first_ref, o_ref, lse_ref, keys_ref, queries_ref):
    i = pl.program_id(0)
    shift = info_ref[0]

    @pl.when(i == 0)
    def _():
        for h in range(heads):
            keys_ref[h] = turned(k_ref[head_rows(h), :])

    first = first_ref[pl.ds(i, 1), :]
    queries_ref[...] = q_ref[...] * jnp.bfloat16(HEAD_DIM**-0.5)
    ones = jnp.ones((16, BLK), jnp.bfloat16)

    def step(j, carry):
        place = pl.ds(pl.multiple_of(lax.rem(j + shift, blocks) * BLK, BLK), BLK)
        allowed = allowed_tile(i, j, first)
        out = []
        for h in range(heads):
            top, acc = carry[h]
            scores = nn(keys_ref[h, place, :], queries_ref[head_rows(h), :])
            scores = jnp.where(allowed, scores, NEG)
            new_top = jnp.maximum(top, jnp.max(scores, axis=0, keepdims=True))
            probs = jnp.exp(scores - new_top)
            shrink = jnp.exp(top - new_top)
            values = jnp.concatenate([v_ref[head_rows(h), place], ones], axis=0)
            acc = acc * shrink + nn(values, probs.astype(jnp.bfloat16))
            out.append((new_top, acc))
        return tuple(out)

    row = lambda value: jnp.full((1, BLK), value, jnp.float32)
    start = tuple((row(NEG), jnp.zeros((HEAD_DIM + 16, BLK), jnp.float32)) for h in range(heads))
    done = lax.fori_loop(info_ref[1 + i], i + 1, step, start)
    for h, (top, acc) in enumerate(done):
        total = acc[HEAD_DIM : HEAD_DIM + 1, :]
        o_ref[head_rows(h), :] = (acc[:HEAD_DIM] / total).astype(jnp.bfloat16)
        lse_ref[h : h + 1, :] = top + jnp.log(total)


def attend(info, projected, first, heads):
    tokens = projected.shape[1]
    wide, blocks = heads * HEAD_DIM, tokens // BLK
    at = lambda i, s: lax.rem(i + s[0], blocks)
    return pl.pallas_call(
        functools.partial(attend_kernel, heads, blocks),
        grid_spec=pltpu.PrefetchScalarGridSpec(
            num_scalar_prefetch=1,
            grid=(blocks,),
            in_specs=[
                pl.BlockSpec((wide, BLK), lambda i, s: (0, at(i, s))),
                pl.BlockSpec((wide, tokens), lambda i, s: (1, 0)),
                pl.BlockSpec((wide, tokens), lambda i, s: (2, 0)),
                pl.BlockSpec((blocks, BLK), lambda i, s: (0, 0)),
            ],
            out_specs=[
                pl.BlockSpec((wide, BLK), lambda i, s: (0, at(i, s))),
                pl.BlockSpec((8, BLK), lambda i, s: (0, i)),
            ],
            scratch_shapes=[
                pltpu.VMEM((heads, tokens, HEAD_DIM), jnp.bfloat16),
                pltpu.VMEM((wide, BLK), jnp.bfloat16),
            ],
        ),
        out_shape=[
            jax.ShapeDtypeStruct((wide, tokens), jnp.bfloat16),
            jax.ShapeDtypeStruct((8, tokens), jnp.float32),
        ],
        compiler_params=pltpu.CompilerParams(vmem_limit_bytes=KERNEL_VMEM),
        cost_estimate=pl.CostEstimate(flops=0, bytes_accessed=0, transcendentals=0),
        name="attend",
    )(info, projected, projected, projected, first)


def attend_back_kernel(
    heads, blocks, info_ref, q_ref, k_ref, v_ref, o_ref, g_ref, lse_ref, first_ref,
    d_ref, keys_ref, values_ref, queries_ref, dk_acc, dv_acc,
):
    i = pl.program_id(0)
    shift = info_ref[0]

    @pl.when(i == 0)
    def _():
        for h in range(heads):
            keys_ref[h] = turned(k_ref[head_rows(h), :])
            values_ref[h] = turned(v_ref[head_rows(h), :])
        dk_acc[...] = jnp.zeros_like(dk_acc)
        dv_acc[...] = jnp.zeros_like(dv_acc)

    first = first_ref[pl.ds(i, 1), :]
    queries_ref[...] = q_ref[...] * jnp.bfloat16(HEAD_DIM**-0.5)
    centre = [
        jnp.sum(
            g_ref[head_rows(h), :].astype(jnp.float32) * o_ref[head_rows(h), :].astype(jnp.float32),
            axis=0,
            keepdims=True,
        )
        for h in range(heads)
    ]

    def step(j, carry):
        place = pl.ds(pl.multiple_of(lax.rem(j + shift, blocks) * BLK, BLK), BLK)
        allowed = allowed_tile(i, j, first)
        out = []
        for h in range(heads):
            rows = head_rows(h)
            query = queries_ref[rows, :]
            grad = g_ref[rows, :]
            scores = jnp.where(allowed, nn(keys_ref[h, place, :], query), NEG)
            probs = jnp.exp(scores - lse_ref[h : h + 1, :])
            prob_grad = nn(values_ref[h, place, :], grad)
            score_grad = (probs * (prob_grad - centre[h])).astype(jnp.bfloat16)
            dv_acc[rows, place] += nt(grad, probs.astype(jnp.bfloat16))
            dk_acc[rows, place] += nt(query, score_grad)
            out.append(carry[h] + nn(k_ref[rows, place], score_grad))
        return tuple(out)

    start = tuple(jnp.zeros((HEAD_DIM, BLK), jnp.float32) for h in range(heads))
    done = lax.fori_loop(info_ref[1 + i], i + 1, step, start)
    mine = pl.ds(pl.multiple_of(lax.rem(i + shift, blocks) * BLK, BLK), BLK)
    for h in range(heads):
        d_ref[head_rows(2 * heads + h), mine] = (done[h] * HEAD_DIM**-0.5).astype(jnp.bfloat16)

    @pl.when(i == blocks - 1)
    def _():
        d_ref[: heads * HEAD_DIM, :] = dk_acc[...].astype(jnp.bfloat16)
        d_ref[heads * HEAD_DIM : 2 * heads * HEAD_DIM, :] = dv_acc[...].astype(jnp.bfloat16)


def attend_back(info, projected, attended, grad, log_totals, first, heads):
    tokens = projected.shape[1]
    wide, blocks = heads * HEAD_DIM, tokens // BLK
    at = lambda i, s: lax.rem(i + s[0], blocks)
    block = pl.BlockSpec((wide, BLK), lambda i, s: (0, at(i, s)))
    whole = lambda part: pl.BlockSpec((wide, tokens), lambda i, s: (part, 0))
    return pl.pallas_call(
        functools.partial(attend_back_kernel, heads, blocks),
        grid_spec=pltpu.PrefetchScalarGridSpec(
            num_scalar_prefetch=1,
            grid=(blocks,),
            in_specs=[
                block,
                whole(1),
                whole(2),
                block,
                block,
                pl.BlockSpec((8, BLK), lambda i, s: (0, i)),
                pl.BlockSpec((blocks, BLK), lambda i, s: (0, 0)),
            ],
            out_specs=pl.BlockSpec((3 * wide, tokens), lambda i, s: (0, 0)),
            scratch_shapes=[
                pltpu.VMEM((heads, tokens, HEAD_DIM), jnp.bfloat16),
                pltpu.VMEM((heads, tokens, HEAD_DIM), jnp.bfloat16),
                pltpu.VMEM((wide, BLK), jnp.bfloat16),
                pltpu.VMEM((wide, tokens), jnp.float32),
                pltpu.VMEM((wide, tokens), jnp.float32),
            ],
        ),
        out_shape=jax.ShapeDtypeStruct((3 * wide, tokens), jnp.bfloat16),
        compiler_params=pltpu.CompilerParams(vmem_limit_bytes=KERNEL_VMEM),
        cost_estimate=pl.CostEstimate(flops=0, bytes_accessed=0, transcendentals=0),
        name="attend_back",
    )(info, projected, projected, projected, attended, grad, log_totals, first)


ROW, COL, LOW_Y, LOW_Z, HIGH_Z, QUARTER, PEER, SAME = range(8)


class Here:
    places = None


def call(body, name, grid, specs, args, out_specs, out_shapes, vmem=KERNEL_VMEM):
    return pl.pallas_call(
        body,
        grid_spec=pltpu.PrefetchScalarGridSpec(
            num_scalar_prefetch=1, grid=grid, in_specs=specs, out_specs=out_specs
        ),
        out_shape=out_shapes,
        compiler_params=pltpu.CompilerParams(vmem_limit_bytes=vmem),
        cost_estimate=pl.CostEstimate(flops=0, bytes_accessed=0, transcendentals=0),
        name=name,
    )(Here.places, *args)


f32 = jnp.float32
bf16 = jnp.bfloat16


def shape(*dims, dtype=jnp.bfloat16):
    return jax.ShapeDtypeStruct(dims, dtype)


def whole_spec(value):
    zeros = (0,) * value.ndim
    return pl.BlockSpec(value.shape, lambda *_: zeros)


def chunks(size, step):
    return [slice(i, min(i + step, size)) for i in range(0, size, step)]


def project(weight, own, other, bias):
    parts, depth, width = weight.shape
    count = own.shape[1]

    def body(_, w_ref, own_ref, other_ref, b_ref, o_ref):
        def run(ref):
            for cols in chunks(count, 256):
                o_ref[:, cols] = (tn(w_ref[0], ref[:, cols]) + b_ref[0]).astype(jnp.bfloat16)

        pl.when(pl.program_id(0) == 0)(lambda: run(own_ref))
        pl.when(pl.program_id(0) == 1)(lambda: run(other_ref))

    return call(
        body, "project", (2, parts),
        [
            pl.BlockSpec((1, depth, width), lambda i, j, _: (j, 0, 0)),
            whole_spec(own),
            whole_spec(other),
            pl.BlockSpec((1, width, 1), lambda i, j, _: (j, 0, 0)),
        ],
        (weight, own, other, bias),
        pl.BlockSpec((width, count), lambda i, j, _: (j, i)),
        shape(parts * width, 2 * count),
    )


def hidden(weight, own, other, columns):
    depth, width = weight.shape
    count = own.shape[1]
    block = 256
    half = count // block

    def body(_, w_ref, own_ref, other_ref, b_ref, act_ref, slope_ref):
        tokens = jnp.where(pl.program_id(0) < half, own_ref[...], other_ref[...])
        for rows in chunks(width, 256):
            pre = tn(w_ref[:, rows], tokens) + b_ref[rows, 5:6]
            square = pre * pre
            bend = jnp.tanh(pre * (gelu_root + (gelu_root * gelu_cubic) * square))
            lift = 0.5 * (1.0 + bend)
            act_ref[rows, :] = (pre * lift).astype(jnp.bfloat16)
            slope_ref[rows, :] = lift + (pre * lift) * (1.0 - bend) * (
                gelu_root + (3.0 * gelu_root * gelu_cubic) * square
            )

    tile = pl.BlockSpec((width, block), lambda i, _: (0, i))
    return call(
        body, "hidden", (2 * half,),
        [
            whole_spec(weight),
            pl.BlockSpec((depth, block), lambda i, _: (0, jnp.minimum(i, half - 1))),
            pl.BlockSpec((depth, block), lambda i, _: (0, jnp.maximum(i - half, 0))),
            whole_spec(columns),
        ],
        (weight, own, other, columns),
        [tile, tile],
        [shape(width, 2 * count), shape(width, 2 * count, dtype=jnp.float32)],
    )


def hidden_back(weight, own, other, slope):
    depth, width = weight.shape
    count = own.shape[1]
    block = 256
    half = count // block

    def body(_, w_ref, own_ref, other_ref, s_ref, o_ref, sum_ref):
        tokens = jnp.where(pl.program_id(0) < half, own_ref[...], other_ref[...])

        @pl.when(pl.program_id(0) == 0)
        def _():
            sum_ref[...] = jnp.zeros_like(sum_ref)

        for rows in chunks(width, 256):
            grad = (tn(w_ref[:, rows], tokens) * s_ref[rows, :]).astype(jnp.bfloat16)
            o_ref[rows, :] = grad
            grad = grad.astype(jnp.float32)
            sum_ref[rows, :] += grad[:, :128] + grad[:, 128:]

    tile = pl.BlockSpec((width, block), lambda i, _: (0, i))
    return call(
        body, "hidden_back", (2 * half,),
        [
            whole_spec(weight),
            pl.BlockSpec((depth, block), lambda i, _: (0, jnp.minimum(i, half - 1))),
            pl.BlockSpec((depth, block), lambda i, _: (0, jnp.maximum(i - half, 0))),
            tile,
        ],
        (weight, own, other, slope),
        [tile, pl.BlockSpec((width, 128), lambda i, _: (0, 0))],
        [shape(width, 2 * count), shape(width, 128, dtype=jnp.float32)], vmem=WIDE_VMEM,
    )


def mapped(weight, tokens, part, turn, received=None):
    depth, count = weight.shape[0 if turn else 1], tokens.shape[1] // 2
    rows = weight.shape[1 if turn else 0]
    block = rows if turn else 400
    step = 256 if turn else block

    def body(_, w_ref, t_ref, *refs):
        o_ref = refs[-1]
        for cut in chunks(block, step):
            part = tn(w_ref[:, cut], t_ref[...]) if turn else nn(w_ref[cut, :], t_ref[...])
            if received is not None:
                part = part + refs[0][cut, :].astype(jnp.float32)
            o_ref[cut, :] = part.astype(jnp.bfloat16)

    extra = () if received is None else (received,)
    if turn:
        cols = 256
        grid = (count // cols,)
        tile = pl.BlockSpec((rows, cols), lambda i, _: (0, i))
        specs = [
            whole_spec(weight),
            pl.BlockSpec((depth, cols), lambda i, _: (0, part * (count // cols) + i)),
        ] + [tile] * len(extra)
    else:
        grid = (rows // block,)
        tile = pl.BlockSpec((block, count), lambda i, _: (i, 0))
        specs = [
            pl.BlockSpec((block, depth), lambda i, _: (i, 0)),
            pl.BlockSpec((depth, count), lambda i, _: (0, part)),
        ] + [tile] * len(extra)
    return call(body, "mapped", grid, specs, (weight, tokens) + extra, tile, shape(rows, count))


def mapped_three(weight, parts, part, received=None):
    count = parts.shape[1] // 2
    _, rows, width = weight.shape
    block = 400

    def body(_, w_ref, p_ref, *refs):
        total = sum(nn(w_ref[(i + 1) % 3], p_ref[i * width : (i + 1) * width, :]) for i in range(3))
        if received is not None:
            total = total + refs[0][...].astype(jnp.float32)
        refs[-1][...] = total.astype(refs[-1].dtype)

    tile = pl.BlockSpec((block, count), lambda i, _: (i, 0))
    extra = () if received is None else (received,)
    return call(
        body, "mapped_three", (rows // block,),
        [
            pl.BlockSpec((3, block, width), lambda i, _: (0, i, 0)),
            pl.BlockSpec((3 * width, count), lambda i, _: (0, part)),
        ] + [tile] * len(extra),
        (weight, parts) + extra,
        tile,
        shape(rows, count, dtype=jnp.bfloat16 if received is None else jnp.float32),
    )


def attended_back(weight, own, other):
    width, depth = weight.shape
    count = own.shape[1]

    def body(_, w_ref, own_ref, other_ref, o_ref):
        def run(ref):
            for cols in chunks(count, 256):
                o_ref[:, cols] = nn(w_ref[...], ref[:, cols]).astype(jnp.bfloat16)

        pl.when(pl.program_id(0) == 0)(lambda: run(own_ref))
        pl.when(pl.program_id(0) == 1)(lambda: run(other_ref))

    return call(
        body, "attended_back", (2,),
        [whole_spec(weight), whole_spec(own), whole_spec(other)],
        (weight, own, other),
        pl.BlockSpec((width, count), lambda i, _: (0, i)),
        shape(width, 2 * count),
    )


def weight_grad(sources, place_of, blocks, parts):
    rows, count = sources[0][0].shape
    size = rows // parts
    widths = [part[1] for _, _, _, part in sources]

    def body(_, *refs):
        o_ref, at = refs[-1], 0
        for i, width in enumerate(widths):
            own_ref, other_ref, r_ref = refs[3 * i : 3 * i + 3]
            grad = nt(own_ref[0], r_ref[:, :count]) + nt(other_ref[0], r_ref[:, count:])
            o_ref[0, :, at : at + width] = grad.astype(bf16)
            at += width

    tile = pl.BlockSpec((1, size, count), lambda i, s: (place_of(i, s), 0, 0))
    specs, args = [], []
    for own, other, right, (place, width) in sources:
        specs += [tile, tile, pl.BlockSpec((width, 2 * count), lambda i, s, place=place: (place, 0))]
        args += [own.reshape(parts, size, count), other.reshape(parts, size, count), right]
    return call(
        body, "weight_grad", (blocks,), specs, tuple(args),
        pl.BlockSpec((1, size, sum(widths)), lambda i, s: (i, 0, 0)),
        shape(blocks, size, sum(widths)), vmem=WIDE_VMEM,
    )


SWAP = ((0, 1), (1, 0))
f32 = jnp.float32
bf16 = jnp.bfloat16


def row_swap(value):
    return lax.ppermute(value, "row", SWAP)


def col_swap(value):
    return lax.ppermute(value, "col", SWAP)


def dp_xor(value, mask):
    return lax.ppermute(value, "dp", [(i, i ^ mask) for i in range(lax.axis_size("dp"))])


def after(value, *marks):
    return lax.optimization_barrier((value,) + marks)[0] if marks else value


def ordered(at, first, second, axis):
    return jnp.where(
        at == 0,
        jnp.concatenate([first, second], axis=axis),
        jnp.concatenate([second, first], axis=axis),
    )


def half_of(at, value, axis):
    size = value.shape[axis] // 2
    return jnp.where(
        at == 0,
        lax.slice_in_dim(value, 0, size, axis=axis),
        lax.slice_in_dim(value, size, 2 * size, axis=axis),
    )


def pick(value, at, axis):
    return lax.dynamic_index_in_dim(value, at, axis, keepdims=False)


def plus(a, b):
    return a.astype(f32) + b.astype(f32)


def pad_to(value, size, axis):
    widths = [(0, 0)] * value.ndim
    widths[axis] = (0, size - value.shape[axis])
    return jnp.pad(value, widths)


def head_slots(c, value, tail, axis, most):
    cut = lambda low, high: lax.slice_in_dim(value, low, high, axis=axis)
    size, spare = value.shape[axis], tail.shape[axis]
    less = most - HEAD_DIM
    first = jnp.where(c == 0, cut(0, most), pad_to(cut(spare, spare + less), most, axis))
    second = jnp.where(
        c == 0,
        pad_to(jnp.concatenate([cut(most, size), tail], axis=axis), most, axis),
        pad_to(cut(spare + less, size), most, axis),
    )
    return first, second


def from_slots(c, first, second, axis, spare):
    cut = lambda value, low, high: lax.slice_in_dim(value, low, high, axis=axis)
    most = first.shape[axis]
    less = most - HEAD_DIM
    tail = col_swap(cut(second, less - spare, less))
    return jnp.where(
        c == 0,
        jnp.concatenate([first, cut(second, 0, less - spare)], axis=axis),
        jnp.concatenate([tail, cut(first, 0, less), cut(second, 0, less)], axis=axis),
    )


def put_slots(o_ref, q_ref, t_ref, core, second, most):
    size, spare = q_ref.shape[-1], t_ref.shape[-1]
    less = most - HEAD_DIM

    @pl.when((core == 0) & (second == 0))
    def _():
        o_ref[...] = q_ref[:, 0, :, :most]

    @pl.when((core == 0) & (second == 1))
    def _():
        o_ref[...] = jnp.zeros_like(o_ref)
        o_ref[:, :, : size - most] = q_ref[:, 0, :, most:]
        o_ref[:, :, size - most : size - most + spare] = t_ref[:, 0]

    @pl.when((core == 1) & (second == 0))
    def _():
        o_ref[...] = jnp.zeros_like(o_ref)
        o_ref[:, :, :less] = q_ref[:, 0, :, spare : spare + less]

    @pl.when((core == 1) & (second == 1))
    def _():
        o_ref[...] = jnp.zeros_like(o_ref)
        o_ref[:, :, :less] = q_ref[:, 0, :, spare + less :]


def put_half(o_ref, f_ref, second):
    wide = f_ref.shape[-1] // 2

    @pl.when(second == 0)
    def _():
        o_ref[...] = f_ref[0, :, :wide]

    @pl.when(second == 1)
    def _():
        o_ref[...] = f_ref[0, :, wide:]


def quarters(value):
    return value.reshape(value.shape[:-2] + (4, value.shape[-2] // 4, value.shape[-1]))


def pack_heads(qkv, tail, most):
    rows, size, spare = qkv.shape[1] // 4, qkv.shape[2], tail.shape[2]

    def body(s_ref, q_ref, t_ref, o_ref):
        put_slots(o_ref, q_ref, t_ref, s_ref[COL], s_ref[PEER], most)

    return call(
        body, "pack_heads", (3,),
        [
            pl.BlockSpec((1, 1, rows, size), lambda i, s: (i, s[QUARTER], 0, 0)),
            pl.BlockSpec((1, 1, rows, spare), lambda i, s: (i, s[QUARTER], 0, 0)),
        ],
        (quarters(qkv), quarters(tail)),
        pl.BlockSpec((1, rows, most), lambda i, s: (i, 0, 0)), shape(3, rows, most),
        vmem=WIDE_VMEM,
    )


def pack(fc, proj):
    rows, wide = fc.shape[0] // 4, fc.shape[1] // 2

    def body(s_ref, f_ref, p_ref, fo_ref, po_ref):
        put_half(fo_ref, f_ref, s_ref[PEER])
        put_half(po_ref, p_ref, s_ref[PEER])

    return call(
        body, "pack", (1,),
        [pl.BlockSpec((1, rows, 2 * wide), lambda i, s: (s[QUARTER], 0, 0))] * 2,
        (quarters(fc), quarters(proj)),
        [pl.BlockSpec((rows, wide), lambda i, s: (0, 0))] * 2,
        [shape(rows, wide)] * 2,
        vmem=WIDE_VMEM,
    )


def own_rows(mine, tail, width):
    three = mine.ndim == 3
    rows, size = mine.shape[-2] // 4, mine.shape[-1]

    def body(s_ref, m_ref, *refs):
        t_ref, o_ref = refs if three else (None,) + refs
        if three:
            put_slots(o_ref.at[:, 0], m_ref, t_ref, s_ref[COL], s_ref[ROW], width)
        else:
            put_half(o_ref.at[0], m_ref, s_ref[ROW])

    lead, zero = ((3,), (0,)) if three else ((), ())
    block = lambda width, at: pl.BlockSpec(lead + (1, rows, width), lambda i, s: zero + (at(i, s), 0, 0))
    own = lambda i, s: i
    return call(
        body, "own_rows", (4,),
        [block(size, own)] + ([block(tail.shape[-1], own)] if three else []),
        tuple([quarters(mine)] + ([quarters(tail)] if three else [])),
        block(width, lambda i, s: 4 * s[ROW] + i), shape(*lead, 8, rows, width),
        vmem=WIDE_VMEM,
    )


def all_rows(held, got):
    lead, tile = held.shape[:-3], held.shape[-2:]
    zero = (0,) * len(lead)

    def body(s_ref, h_ref, *refs):
        o_ref = refs[-1]
        place = (pl.program_id(0) // 2 != s_ref[LOW_Z]) * 2 + (pl.program_id(0) % 2 != s_ref[LOW_Y])
        for i in range(4):

            @pl.when(place == i)
            def _(i=i):
                o_ref[...] = refs[i][...].reshape(o_ref.shape)

    fetched = pl.BlockSpec(lead + tile, lambda i, s: zero + (0, 0))
    out = pl.pallas_call(
        body,
        grid_spec=pltpu.PrefetchScalarGridSpec(
            num_scalar_prefetch=1,
            grid=(4,),
            in_specs=[pl.BlockSpec(memory_space=pl.ANY)] + [fetched] * 4,
            out_specs=pl.BlockSpec(lead + (1,) + tile, lambda i, s: zero + (4 * s[PEER] + i, 0, 0)),
        ),
        out_shape=shape(*held.shape),
        input_output_aliases={1: 0},
        compiler_params=pltpu.CompilerParams(vmem_limit_bytes=WIDE_VMEM),
        cost_estimate=pl.CostEstimate(flops=0, bytes_accessed=0, transcendentals=0),
        name="all_rows",
    )(Here.places, held, *got)
    return out.reshape(lead + (8 * tile[0], tile[1]))


def half_rows(value, at):
    rows, count = value.shape[0] // 2, value.shape[1]

    def body(_, a_ref, o_ref):
        o_ref[...] = a_ref[...].astype(bf16)

    return call(
        body, "half_rows", (count // 256,),
        [pl.BlockSpec((rows, 256), lambda i, s: (s[at], i))], (value,),
        pl.BlockSpec((rows, 256), lambda i, s: (0, i)), shape(rows, count),
    )


def packed_sums(sums_two, sums_one, grad_own, hidden_sums, parts, most):
    width, half = sums_two.shape[1], sums_one.shape[1]

    def body(_, two_ref, one_ref, grad_ref, hid_ref, p_ref, o_ref):
        def over(value):
            ones = jnp.ones((8, value.shape[1]), value.dtype)
            exact = lax.Precision.HIGHEST if value.dtype == f32 else None
            return lax.dot_general(
                ones, value, (((1,), (1,)), ((), ())), preferred_element_type=f32, precision=exact
            )[0:1]

        o_ref[...] = jnp.zeros_like(o_ref)
        for i in range(3):
            o_ref[i : i + 1, :] = over(two_ref[i])
        o_ref[3:4, :half] = over(one_ref[0])
        o_ref[3:4, half:] = over(one_ref[1])
        o_ref[4:5, :half] = over(grad_ref[...])
        o_ref[8:9, :] = over(hid_ref[...])
        o_ref[9:10, :most] = over(p_ref[2 * most :, :])
        o_ref[10:11, :most] = over(p_ref[most : 2 * most, :])

    args = (sums_two, sums_one, grad_own, hidden_sums, parts)
    return call(
        body, "packed_sums", (1,), [whole_spec(v) for v in args], args,
        pl.BlockSpec((16, width), lambda i, s: (0, 0)), shape(16, width, dtype=f32),
    )


def sums_added(a, b, rows):
    def body(_, a_ref, b_ref, o_ref):
        at = lax.broadcasted_iota(jnp.int32, a_ref.shape, 0)
        o_ref[...] = a_ref[...] + jnp.where(at < rows, b_ref[...], 0.0)

    spec = whole_spec(a)
    return call(body, "sums_added", (1,), [spec, spec], (a, b), spec, shape(*a.shape, dtype=f32))


def spread_index(sizes, axis, step, value):
    places = []
    for size in reversed(sizes):
        places.insert(0, step % size)
        step = step // size
    places.insert(axis, value)
    return tuple(places) + (0, 0)


def halved(keep, got, axis, at):
    lead, tile = keep.shape[:-2], keep.shape[-2:]
    rest = lead[:axis] + lead[axis + 1 :]

    def body(_, a_ref, b_ref, c_ref, d_ref, keep_ref, send_ref):
        keep_ref[...] = (a_ref[...].astype(f32) + b_ref[...].astype(f32)).astype(bf16).reshape(keep_ref.shape)
        send_ref[...] = (c_ref[...].astype(f32) + d_ref[...].astype(f32)).astype(bf16).reshape(send_ref.shape)

    ones = (1,) * len(lead)
    mine = pl.BlockSpec(ones + tile, lambda i, s: spread_index(rest, axis, i, s[at]))
    theirs = pl.BlockSpec(ones + tile, lambda i, s: spread_index(rest, axis, i, 1 - s[at]))
    steps = math.prod(rest)
    out = pl.BlockSpec((1,) + tile, lambda i, s: (i, 0, 0))
    first, second = call(
        body, "halved", (steps,), [mine, mine, theirs, theirs], (keep, got, keep, got),
        [out, out], [shape(steps, *tile)] * 2,
    )
    return first.reshape(rest + tile), second.reshape(rest + tile)


def added(a, b):
    def body(_, a_ref, b_ref, o_ref):
        o_ref[...] = (a_ref[...].astype(f32) + b_ref[...].astype(f32)).astype(bf16)

    spec = whole_spec(a)
    return call(body, "added", (1,), [spec, spec], (a, b), spec, shape(*a.shape))


def chosen(a, b):
    def body(s_ref, a_ref, b_ref, o_ref):
        o_ref[...] = jnp.where(s_ref[SAME] == 1, a_ref[...], b_ref[...])

    spec = whole_spec(a)
    return call(body, "chosen", (1,), [spec, spec], (a, b), spec, shape(*a.shape))


def paired(at, first, second, axis):
    lead, tile = first.shape[:-2], first.shape[-2:]
    ones = (1,) * len(lead)
    steps = math.prod(lead)

    def body(_, a_ref, b_ref, o_ref):
        @pl.when(pl.program_id(0) == 0)
        def _():
            o_ref[...] = a_ref[...].reshape(o_ref.shape)

        @pl.when(pl.program_id(0) == 1)
        def _():
            o_ref[...] = b_ref[...].reshape(o_ref.shape)

    def place(step):
        return spread_index(lead, len(lead), step, 0)[: len(lead)] + (0, 0)

    out = lambda i, j, s: spread_index(lead, axis, j, jnp.where(i == 0, s[at], 1 - s[at]))
    return call(
        body, "paired", (2, steps),
        [
            pl.BlockSpec(ones + tile, lambda i, j, s: place(jnp.where(i == 0, j, steps - 1))),
            pl.BlockSpec(ones + tile, lambda i, j, s: place(jnp.where(i == 1, j, 0))),
        ],
        (first, second),
        pl.BlockSpec(ones + (1,) + tile, out),
        shape(*lead[:axis], 2, *lead[axis:], *tile),
    )


def widened(keep, got, at, y_last):
    rows, width = keep.shape[-2:]

    def body(s_ref, a_ref, b_ref, c_ref, d_ref, o_ref):
        if y_last:
            swap = s_ref[at] == 1
            o_ref[:, :width] = jnp.where(swap, b_ref[0, 0], a_ref[0, 0]).astype(f32)
            o_ref[:, width:] = jnp.where(swap, a_ref[0, 0], b_ref[0, 0]).astype(f32)
        else:
            other = pl.program_id(0) % 2 != s_ref[at]
            o_ref[:, :width] = jnp.where(other, b_ref[0, 0], a_ref[0, 0]).astype(f32)
            o_ref[:, width:] = jnp.where(other, d_ref[0, 0], c_ref[0, 0]).astype(f32)

    tile = (1, 1, rows, width)
    if y_last:
        one = pl.BlockSpec(tile, lambda i, s: (i // 2, i % 2, 0, 0))
        none = pl.BlockSpec(tile, lambda i, s: (0, 0, 0, 0))
        specs = [one, one, none, none]
    else:
        specs = [pl.BlockSpec(tile, lambda i, s, f=f: (f, i // 2, 0, 0)) for f in (0, 0, 1, 1)]
    return call(
        body, "widened", (4,), specs, (keep, got, keep, got),
        pl.BlockSpec((rows, 2 * width), lambda i, s: (i, 0)),
        shape(4 * rows, 2 * width, dtype=f32),
    )


def tails_of(keep, got, at, y_last, most, low, high):
    rows, width = keep.shape[-2:]
    count = width // most

    def body(s_ref, a_ref, b_ref, o_ref):
        second = jnp.where((s_ref[at] == 1) if y_last else (pl.program_id(0) % 2 == s_ref[at]), a_ref[0, 0], b_ref[0, 0])
        for i in range(count):
            o_ref[i, 0] = second[:, i * most + low : i * most + high]

    tile = (1, 1, rows, width)
    where = (lambda i, s: (i // 2, i % 2, 0, 0)) if y_last else (lambda i, s: (1, i // 2, 0, 0))
    return call(
        body, "tails_of", (4,), [pl.BlockSpec(tile, where)] * 2, (keep, got),
        pl.BlockSpec((count, 1, rows, high - low), lambda i, s: (0, i, 0, 0)),
        shape(count, 4, rows, high - low),
    )


def unslotted(keep, got, tails, at, y_last, most, size):
    rows, width = keep.shape[-2:]
    count, spare, less = width // most, tails.shape[-1], most - HEAD_DIM

    def body(s_ref, a_ref, b_ref, c_ref, d_ref, t_ref, o_ref):
        if y_last:
            swap = s_ref[at] == 1
            first = jnp.where(swap, b_ref[0, 0], a_ref[0, 0])
            second = jnp.where(swap, a_ref[0, 0], b_ref[0, 0])
        else:
            other = pl.program_id(0) % 2 != s_ref[at]
            first = jnp.where(other, b_ref[0, 0], a_ref[0, 0])
            second = jnp.where(other, d_ref[0, 0], c_ref[0, 0])
        first, second = first.astype(f32), second.astype(f32)

        @pl.when(s_ref[COL] == 0)
        def _():
            for i in range(count):
                o_ref[i, :, :most] = first[:, i * most : (i + 1) * most]
                o_ref[i, :, most:] = second[:, i * most : i * most + size - most]

        @pl.when(s_ref[COL] == 1)
        def _():
            for i in range(count):
                o_ref[i, :, :spare] = t_ref[i, 0].astype(f32)
                o_ref[i, :, spare : spare + less] = first[:, i * most : i * most + less]
                o_ref[i, :, spare + less :] = second[:, i * most : i * most + less]

    tile = (1, 1, rows, width)
    if y_last:
        one = pl.BlockSpec(tile, lambda i, s: (i // 2, i % 2, 0, 0))
        none = pl.BlockSpec(tile, lambda i, s: (0, 0, 0, 0))
        specs = [one, one, none, none]
    else:
        specs = [pl.BlockSpec(tile, lambda i, s, f=f: (f, i // 2, 0, 0)) for f in (0, 0, 1, 1)]
    return call(
        body, "unslotted", (4,),
        specs + [pl.BlockSpec((count, 1, rows, spare), lambda i, s: (0, i, 0, 0))],
        (keep, got, keep, got, tails),
        pl.BlockSpec((count, rows, size), lambda i, s: (0, i, 0)),
        shape(count, 4 * rows, size, dtype=f32),
    )


TOKENS = 256


def tile_of(rows, at=None):
    if at is None:
        return pl.BlockSpec((rows, TOKENS), lambda i, s: (0, i))
    return pl.BlockSpec((rows, TOKENS), lambda i, s: (at(s), i))


def norm_stats(parts):
    count = sum(part.shape[0] for part in parts)
    center = sum(jnp.sum(part, axis=0, keepdims=True) for part in parts) / count
    spread = sum(jnp.sum((part - center) * (part - center), axis=0, keepdims=True) for part in parts) / count
    return center, lax.rsqrt(spread + 1e-05)


def norm_one(x_own, x_peer, columns):
    half, count = x_own.shape

    def body(s_ref, own_ref, peer_ref, c_ref, h_ref, stat_ref):
        own, peer = own_ref[...].astype(f32), peer_ref[...].astype(f32)
        parts = [jnp.where(s_ref[ROW] == 0, own, peer), jnp.where(s_ref[ROW] == 0, peer, own)]
        center, inverse = norm_stats(parts)
        stat_ref[0:1, :] = center
        stat_ref[1:2, :] = inverse
        for i, part in enumerate(parts):
            rows = slice(i * half, (i + 1) * half)
            h_ref[rows, :] = ((part - center) * inverse * c_ref[rows, 0:1] + c_ref[rows, 1:2]).astype(bf16)

    return call(
        body, "norm_one", (count // TOKENS,),
        [tile_of(half), tile_of(half), whole_spec(columns)],
        (x_own, x_peer, columns),
        [tile_of(2 * half), tile_of(8)],
        [shape(2 * half, count), shape(8, count, dtype=f32)],
    )


def norm_two(x_own, x_peer, low, other, columns):
    half, count = x_own.shape

    def body(s_ref, own_ref, peer_ref, low_ref, other_ref, c_ref, x_ref, h_ref, stat_ref):
        own, peer = own_ref[...].astype(f32), peer_ref[...].astype(f32)
        parts = [jnp.where(s_ref[ROW] == 0, own, peer), jnp.where(s_ref[ROW] == 0, peer, own)]
        for i in range(2):
            rows = slice(i * half, (i + 1) * half)
            branch = low_ref[rows, :].astype(f32) + other_ref[rows, :].astype(f32) + c_ref[rows, 2:3]
            parts[i] = parts[i] + branch
            x_ref[rows, :] = parts[i]
        center, inverse = norm_stats(parts)
        stat_ref[0:1, :] = center
        stat_ref[1:2, :] = inverse
        for i, part in enumerate(parts):
            rows = slice(i * half, (i + 1) * half)
            h_ref[rows, :] = ((part - center) * inverse * c_ref[rows, 3:4] + c_ref[rows, 4:5]).astype(bf16)

    full = tile_of(2 * half)
    return call(
        body, "norm_two", (count // TOKENS,),
        [tile_of(half), tile_of(half), full, full, whole_spec(columns)],
        (x_own, x_peer, low, other, columns),
        [full, full, tile_of(8)],
        [shape(2 * half, count, dtype=f32), shape(2 * half, count), shape(8, count, dtype=f32)],
    )


def lanes_summed(ref, at, value, first):
    total = sum(value[:, i : i + 128] for i in range(0, value.shape[1], 128))

    @pl.when(first)
    def _():
        ref[at] = total

    @pl.when(jnp.logical_not(first))
    def _():
        ref[at] += total


def norm_two_back(low, other, grad, x_mid, stats, columns):
    width, count = low.shape

    def body(_, low_ref, other_ref, g_ref, x_ref, stat_ref, gain_ref, mid_ref, branch_ref, sum_ref):
        first = pl.program_id(0) == 0
        incoming = low_ref[...].astype(f32) + other_ref[...].astype(f32)
        inverse = stat_ref[1:2, :]
        normed = (x_ref[...] - stat_ref[0:1, :]) * inverse
        scaled = incoming * gain_ref[:, 3:4]
        mean = jnp.sum(scaled, axis=0, keepdims=True) / width
        along = jnp.sum(scaled * normed, axis=0, keepdims=True) / width
        mid = g_ref[...].astype(f32) + inverse * (scaled - mean - normed * along)
        mid_ref[...] = mid
        branch = mid.astype(bf16)
        branch_ref[...] = branch
        lanes_summed(sum_ref, 0, incoming * normed, first)
        lanes_summed(sum_ref, 1, incoming, first)
        lanes_summed(sum_ref, 2, branch.astype(f32), first)

    full = tile_of(width)
    return call(
        body, "norm_two_back", (count // TOKENS,),
        [full, full, full, full, tile_of(8), whole_spec(columns)],
        (low, other, grad, x_mid, stats, columns),
        [full, full, pl.BlockSpec((3, width, 128), lambda i, s: (0, 0, 0))],
        [shape(width, count, dtype=f32), shape(width, count), shape(3, width, 128, dtype=f32)],
    )


def norm_one_sums(mine, other, x_own, stats, columns):
    half, count = x_own.shape

    def body(_, m_ref, o_ref, x_ref, stat_ref, gain_ref, row_ref, sum_ref):
        first = pl.program_id(0) == 0
        incoming = m_ref[...] + o_ref[...].astype(f32)
        normed = (x_ref[...].astype(f32) - stat_ref[0:1, :]) * stat_ref[1:2, :]
        scaled = incoming * gain_ref[:, 0:1]
        row_ref[...] = jnp.zeros_like(row_ref)
        row_ref[0:1, :] = jnp.sum(scaled, axis=0, keepdims=True)
        row_ref[1:2, :] = jnp.sum(scaled * normed, axis=0, keepdims=True)
        lanes_summed(sum_ref, 0, incoming * normed, first)
        lanes_summed(sum_ref, 1, incoming, first)

    return call(
        body, "norm_one_sums", (count // TOKENS,),
        [tile_of(half, lambda s: s[ROW]), tile_of(half), tile_of(half), tile_of(8), pl.BlockSpec((half, columns.shape[1]), lambda i, s: (s[ROW], 0))],
        (mine, other, x_own, stats, columns),
        [tile_of(8), pl.BlockSpec((2, half, 128), lambda i, s: (0, 0, 0))],
        [shape(8, count, dtype=f32), shape(2, half, 128, dtype=f32)],
    )


def norm_one_back(mine, other, x_own, stats, columns, mid_grad, sums, sums_peer):
    half, count = x_own.shape

    def body(_, m_ref, o_ref, x_ref, stat_ref, gain_ref, mid_ref, a_ref, b_ref, out_ref):
        inverse = stat_ref[1:2, :]
        normed = (x_ref[...].astype(f32) - stat_ref[0:1, :]) * inverse
        scaled = (m_ref[...] + o_ref[...].astype(f32)) * gain_ref[:, 0:1]
        means = (a_ref[...] + b_ref[...]) / (2 * half)
        out_ref[...] = mid_ref[...] + inverse * (scaled - means[0:1, :] - normed * means[1:2, :])

    mine_tile = tile_of(half, lambda s: s[ROW])
    return call(
        body, "norm_one_back", (count // TOKENS,),
        [mine_tile, tile_of(half), tile_of(half), tile_of(8), pl.BlockSpec((half, columns.shape[1]), lambda i, s: (s[ROW], 0)), mine_tile, tile_of(8), tile_of(8)],
        (mine, other, x_own, stats, columns, mid_grad, sums, sums_peer),
        tile_of(half), shape(half, count, dtype=f32),
    )


def block_result(x_mid, part, other, columns):
    half, count = other.shape

    def body(_, x_ref, p_ref, o_ref, b_ref, out_ref):
        out_ref[...] = (x_ref[...] + (p_ref[...].astype(f32) + o_ref[...].astype(f32)) + b_ref[:, 6:7]).astype(bf16)

    mine_tile = tile_of(half, lambda s: s[ROW])
    return call(
        body, "block_result", (count // TOKENS,),
        [mine_tile, mine_tile, tile_of(half), pl.BlockSpec((half, columns.shape[1]), lambda i, s: (s[ROW], 0))],
        (x_mid, part, other, columns),
        tile_of(half), shape(half, count),
    )


class Fetch:
    def __init__(self, sent):
        self.got = [row_swap(sent)]

    def more(self, *marks):
        first = after(self.got[0], *marks)
        self.got = [first, dp_xor(first, 1), dp_xor(first, 2)]

    def rest(self, first, *marks):
        self.got.append(dp_xor(after(self.got[first], *marks), 3 - first))
        return self.got


class Total:
    def __init__(self, sources, r, k, y_first, y_last, *marks):
        self.rows, self.width = sources[0][0].shape[0], sum(part[1] for _, _, _, part in sources)
        self.r, self.k, self.y_first, self.y_last = r, k, y_first, y_last
        self.fast = lax.axis_size("dp") == 8
        tied = lambda marks: [(own, other, after(right, *marks), part) for own, other, right, part in sources]
        if not self.fast:
            self.grad = weight_grad(tied(marks), lambda i, s: i, 4, 4)
            return
        if y_first:
            send, keep = (lambda i, s: 2 * (1 - s[LOW_Y]) + i), (lambda i, s: 2 * s[LOW_Y] + i)
            blocks, parts, mask = 2, 4, 1
        else:
            send, keep = (lambda i, s: 1 - s[LOW_Z] + 2 * i), (lambda i, s: s[LOW_Z] + 2 * i)
            blocks, parts, mask = 4, 8, 2
        shaped = lambda v: v.reshape(2, 2, self.rows // 8, self.width)
        sent = weight_grad(tied(marks), send, blocks, parts)
        self.got, self.sent = dp_xor(shaped(sent), mask), [sent]
        self.kept = lambda *marks: shaped(weight_grad(tied(marks), keep, blocks, parts))

    def hold(self, *marks):
        if self.fast:
            self.keep = self.kept(*marks)
        return self.marks()

    def marks(self):
        return [self.keep] if self.fast else []

    def sent_marks(self):
        return self.sent if self.fast else []

    def sum_one(self, *marks):
        if self.fast:
            axis, at, mask = (1, LOW_Z, 2) if self.y_first else (0, LOW_Y, 1)
            self.keep, send = halved(after(self.keep, *marks), self.got, axis, at)
            self.got = dp_xor(send, mask)
            return [self.keep]
        return []

    def sum_two(self, *marks):
        if self.fast:
            self.keep, send = halved(after(self.keep, *marks), self.got, 0, HIGH_Z)
            self.got = dp_xor(send, 4)
            return [self.keep]
        return []

    def sum_three(self, *marks):
        if self.fast:
            cross = [
                (2 * i + j, 2 * (i ^ 1) + (j ^ 1))
                for i in range(lax.axis_size("dp"))
                for j in range(2)
                if i % 2 != j
            ]
            self.keep = added(after(self.keep, *marks), self.got)
            self.got = lax.ppermute(self.keep, ("dp", "row"), cross)
            return [self.keep]
        return []

    def spread_one(self, *marks):
        if self.fast:
            self.keep = chosen(after(self.keep, *marks), self.got)
            self.got = dp_xor(self.keep, 4)
            return [self.keep]
        return []

    def spread_two(self, *marks):
        if self.fast:
            self.keep = paired(HIGH_Z, after(self.keep, *marks), self.got, 0)
            self.got = dp_xor(self.keep, 2 if self.y_last else 1)
            return [self.keep]
        return []

    def spread_three(self, *marks):
        if self.fast:
            if self.y_last:
                self.keep = paired(LOW_Z, after(self.keep, *marks), self.got, 1)
                self.got = dp_xor(self.keep, 1)
            else:
                self.keep = paired(LOW_Y, after(self.keep, *marks), self.got, 0)
                self.got = dp_xor(self.keep, 2)
            return [self.keep]
        return []

    def tail(self, most, spare, *marks):
        if not self.fast:
            return list(marks)
        less = most - HEAD_DIM
        at = LOW_Y if self.y_last else LOW_Z
        self.keep = after(self.keep, *marks)
        tails = tails_of(self.keep, self.got, at, self.y_last, most, less - spare, less)
        self.tails = col_swap(tails)
        return [tails]

    def slots(self, c, most, spare, *marks):
        less = most - HEAD_DIM
        size = 2 * less + spare
        if not self.fast:
            both = self.result()
            cut = lambda i: [v[:, i * most : (i + 1) * most] for v in both]
            return jnp.stack([from_slots(c, *cut(i), 1, spare).astype(f32) for i in range(self.width // most)])
        at = LOW_Y if self.y_last else LOW_Z
        keep = after(self.keep, *marks)
        return unslotted(keep, self.got, self.tails, at, self.y_last, most, size)

    def wide(self, *marks):
        if self.fast:
            return widened(after(self.keep, *marks), self.got, LOW_Y if self.y_last else LOW_Z, self.y_last)
        return jnp.concatenate(self.result(), axis=1).astype(f32)

    def result(self):
        halves = self.grad.reshape(2, self.rows // 2, self.width)
        keep, got = pick(halves, self.r, 0), row_swap(pick(halves, 1 - self.r, 0))
        both = lax.psum(ordered(self.r, keep[None], got[None], 0), "dp")
        return both[0], both[1]


def hop(value, mask):
    return dp_xor(value, mask) if lax.axis_size("dp") == 8 else None


def hop_added(value, peer, *marks):
    return value if peer is None else sums_added(after(value, *marks), peer, 16)


def per_device(
    block_in,
    out_grad,
    seq_lengths,
    ln1_gain,
    ln1_bias,
    qkv_weight,
    qv_bias,
    out_weight,
    out_bias,
    ln2_gain,
    ln2_bias,
    fc_weight,
    fc_bias,
    proj_weight,
    proj_bias,
):
    n_dp = lax.axis_size("dp")
    r, c, k = lax.axis_index("row"), lax.axis_index("col"), lax.axis_index("dp")
    x_own, grad_own = block_in.T, out_grad.T
    half, tokens = x_own.shape
    heads = 7
    most = heads * HEAD_DIM
    spare = 32
    column = lambda v: v.astype(f32)[:, None]

    y, z = k % 2, (k // 2) % 2
    at = jnp.arange(8)
    held = (r, c, y, z, (k // 4) % 2, 2 * z + y, 1 - r, (y == r).astype(r.dtype))
    Here.places = sum(jnp.where(at == i, value, 0) for i, value in enumerate(held)).astype(jnp.int32)
    qkv_tail = col_swap(qkv_weight[:, :, :spare])
    proj_turned = proj_weight.T
    qkv_sent = pack_heads(qkv_weight, qkv_tail, most)
    fc_sent, proj_sent = pack(after(fc_weight, qkv_sent), proj_turned)
    qkv_fetch = Fetch(qkv_sent)
    x_peer = row_swap(after(x_own, qkv_sent))
    vectors = after(jnp.stack([ln1_gain, ln1_bias, out_bias, ln2_gain, ln2_bias]), qkv_sent)
    vectors = ordered(r, vectors, row_swap(vectors), 1)
    both = jnp.stack([half_of(r, fc_bias, 0), jnp.concatenate([proj_bias, proj_bias])])
    columns = jnp.concatenate([vectors, both, jnp.zeros_like(both[:1])]).astype(f32).T
    qv_bias = after(qv_bias, qkv_sent)
    bias_first, bias_second = head_slots(c, qv_bias, col_swap(qv_bias[:, :spare]), 1, most)
    bias_mine = jnp.where(r == 0, bias_first, bias_second).astype(f32)
    bias_mine = jnp.stack([bias_mine[0], jnp.zeros_like(bias_mine[0]), bias_mine[1]])[:, :, None]

    out_weight = after(out_weight, qkv_sent)
    out_first, out_second = head_slots(c, out_weight, col_swap(out_weight[:spare]), 0, most)
    out_mine = jnp.where(r == 0, out_first, out_second)
    out_sent = jnp.where(r == 0, out_second, out_first)
    ff_size = fc_weight.shape[1] // 2
    qkv_full = own_rows(after(qkv_weight, fc_sent, out_sent), qkv_tail, most)
    qkv_fetch.more(qkv_full)
    fc_full = own_rows(after(fc_weight, qkv_fetch.got[0]), None, ff_size)
    qkv_fetch.rest(2, fc_full)
    proj_full = own_rows(after(proj_turned, fc_full, *qkv_fetch.got[1:3]), None, ff_size)

    lengths = after(seq_lengths, qkv_sent)[0]
    group = 2 * tokens
    places = jnp.arange(group, dtype=jnp.int32)
    ends = jnp.cumsum(lengths, dtype=jnp.int32)
    first = jnp.sum(
        jnp.where(ends[None, :] <= places[:, None], lengths[None, :], 0), axis=1, dtype=jnp.int32
    ).reshape(group // BLK, BLK)
    info = jnp.concatenate([(c * (tokens // BLK))[None].astype(jnp.int32), first[:, 0] // BLK])

    h_one, stats_one = norm_one(after(x_own, proj_full, info, bias_mine), x_peer, columns)
    qkv_full = all_rows(after(qkv_full, h_one), qkv_fetch.got)
    h_one_peer = col_swap(after(h_one, qkv_full))
    out_got = row_swap(after(out_sent, qkv_full))
    fc_fetch = Fetch(after(fc_sent, qkv_full))
    proj_fetch = Fetch(after(proj_sent, qkv_full))
    projected = project(qkv_full, h_one, h_one_peer, bias_mine)
    out_full = ordered(r, after(out_mine, projected), out_got, 1)
    attended, log_totals = attend(info, after(projected, out_full), first, heads)
    fc_fetch.more(attended)
    proj_fetch.more(attended)
    other = mapped(out_full, after(attended, fc_fetch.got[0], proj_fetch.got[0]), 1, True)
    low = mapped(out_full, attended, 0, True, col_swap(other))
    branch_other = row_swap(low)
    grad_got = row_swap(after(grad_own, low))
    fc_fetch.rest(1, low)
    proj_fetch.rest(2, low)
    fc_full = all_rows(after(fc_full, low), fc_fetch.got)
    proj_full = all_rows(after(proj_full, fc_full), proj_fetch.got)
    x_mid, h_two, stats_two = norm_two(x_own, x_peer, after(low, proj_full), branch_other, columns)
    h_two_peer = col_swap(h_two)
    activated, slope = hidden(fc_full, h_two, h_two_peer, columns)
    grad_full = paired(ROW, after(grad_own, activated), grad_got, 0).reshape(2 * half, tokens)
    grad_peer = col_swap(grad_full)

    mark = [grad_peer]
    pre_grad, hidden_sums = hidden_back(proj_full, grad_full, grad_peer, slope)
    mark = [pre_grad]
    h_two_other = mapped(fc_full, after(pre_grad, *mark), 1, False)
    mark = [h_two_other]
    fc_total = Total([(h_two, h_two_peer, pre_grad, (0, ff_size))], r, k, False, True, *mark)
    mark = fc_total.sent_marks()
    low = mapped(fc_full, after(pre_grad, *mark), 0, False, col_swap(h_two_other))
    low_other, mark = row_swap(low), [low]
    proj_total = Total([(grad_full, grad_peer, activated, (0, ff_size))], r, k, True, False, *mark)
    mark = proj_total.sent_marks()
    part_other = mapped(proj_full, after(activated, *mark), 1, False)
    mark = [part_other]
    mark = proj_total.hold(*mark)
    mark = fc_total.hold(*mark)
    mark = fc_total.sum_one(*mark)
    mid_grad, branch_grad, sums_two = norm_two_back(
        after(low, *mark), low_other, grad_full, x_mid, stats_two, columns
    )
    branch_peer, mark = col_swap(branch_grad), [branch_grad]
    mark = proj_total.sum_one(*mark)
    attended_grad = attended_back(out_full, after(branch_grad, *mark), branch_peer)
    mark = [attended_grad]
    parts = attend_back(info, projected, attended, after(attended_grad, *mark), log_totals, first, heads)
    mark = [parts]
    three_other = mapped_three(qkv_full, after(parts, *mark), 1)
    mark = [three_other]
    oq_total = Total([(branch_grad, branch_peer, attended, (0, most)), (h_one, h_one_peer, parts, (2, most))], r, k, True, True, *mark)
    mark = oq_total.sent_marks()
    mark = fc_total.sum_two(*mark)
    mark = proj_total.sum_two(*mark)
    kv_total = Total([(h_one, h_one_peer, parts, (0, 2 * most))], r, k, True, False, *mark)
    mark = kv_total.sent_marks()
    proj_part = mapped(proj_full, after(activated, *mark), 0, False, col_swap(part_other))
    mark = [proj_part]
    mark = oq_total.hold(*mark)
    mark = oq_total.sum_one(*mark)
    mine = mapped_three(qkv_full, after(parts, *mark), 0, col_swap(three_other))
    mark = [mine]
    send = half_rows(after(mine, *mark), PEER)
    one_other, mark = row_swap(send), [send]
    mark = kv_total.hold(*mark)
    mark = kv_total.sum_one(*mark)
    mark = proj_total.sum_three(*mark)
    mark = fc_total.sum_three(*mark)
    mark = oq_total.sum_two(*mark)
    mark = kv_total.sum_two(*mark)
    mark = oq_total.sum_three(*mark)
    mark = proj_total.spread_one(*mark)
    mark = fc_total.spread_one(*mark)
    sums, sums_one = norm_one_sums(after(mine, *mark), one_other, x_own, stats_one, columns)
    sums_peer, mark = row_swap(sums), [sums]
    mark = kv_total.sum_three(*mark)
    mark = oq_total.spread_one(*mark)
    packed = packed_sums(sums_two, after(sums_one, *mark), grad_own, hidden_sums, parts, most)
    packed_peer, mark = col_swap(packed), [packed]
    packed = sums_added(after(packed, *mark), packed_peer, 8)
    packed_peer, mark = hop(packed, 2), [packed]
    mark = proj_total.spread_two(*mark)
    mark = kv_total.spread_one(*mark)
    packed = hop_added(packed, packed_peer, *mark)
    packed_peer, mark = hop(packed, 1), [packed]
    x_grad = norm_one_back(after(mine, *mark), one_other, x_own, stats_one, columns, mid_grad, sums, sums_peer)
    mark = [x_grad]
    mark = fc_total.spread_two(*mark)
    mark = kv_total.spread_two(*mark)
    mark = oq_total.spread_two(*mark)
    mark = kv_total.spread_three(*mark)
    packed = hop_added(packed, packed_peer, *mark)
    packed_peer, mark = hop(packed, 4), [packed]
    mark = oq_total.spread_three(*mark)
    packed = hop_added(packed, packed_peer, *mark)
    if n_dp != 8:
        for i in range(n_dp.bit_length() - 1):
            packed = sums_added(packed, dp_xor(packed, 1 << i), 16)
    packed_peer, mark = row_swap(packed), [packed]
    mark = proj_total.spread_three(*mark)
    packed_peer = after(packed_peer, *mark)
    mark = [packed_peer]
    mark = fc_total.spread_three(*mark)
    mark = kv_total.tail(most, spare, *mark)
    mark = oq_total.tail(most, spare, *mark)
    send = half_rows(after(proj_part, *mark), PEER)
    block_other, mark = row_swap(send), [send]
    whole = oq_total.slots(c, most, spare, *mark)
    out_weight_grad = whole[0]
    q_weight_grad = whole[1]
    mark = [whole]
    whole = kv_total.slots(c, most, spare, *mark)
    k_weight_grad = whole[0]
    v_weight_grad = whole[1]
    mark = [whole]
    block_out = block_result(after(x_mid, *mark), proj_part, block_other, columns)
    mark = [block_out]
    proj_weight_grad = proj_total.wide(*mark).T
    mark = [proj_weight_grad]
    fc_weight_grad = fc_total.wide(*mark)
    mark = [fc_weight_grad]

    own = half_of(r, packed, 1)
    fc_bias_grad = ordered(r, packed[8], packed_peer[8], 0)
    qv_mine, qv_peer = packed[9:11, :most], packed_peer[9:11, :most]
    qv_bias_grad = from_slots(
        c, jnp.where(r == 0, qv_mine, qv_peer), jnp.where(r == 0, qv_peer, qv_mine), 1, spare
    )
    qkv_weight_grad = jnp.stack([q_weight_grad, k_weight_grad, v_weight_grad])
    out_weight_grad = out_weight_grad.T
    return (
        block_out.T,
        x_grad.T,
        packed[3, :half],
        packed[3, half:],
        qkv_weight_grad,
        qv_bias_grad,
        out_weight_grad,
        own[2],
        own[0],
        own[1],
        fc_weight_grad,
        fc_bias_grad,
        proj_weight_grad,
        packed[4, :half],
    )


def solution(mesh):
    placed = (
        P(("dp", "col"), "row"),
        P(("dp", "col"), "row"),
        P("dp", None),
        P("row"),
        P("row"),
        P(None, "row", "col"),
        P(None, "col"),
        P("col", "row"),
        P("row"),
        P("row"),
        P("row"),
        P("row", "col"),
        P("col"),
        P("col", "row"),
        P("row"),
    )
    return jax.shard_map(
        per_device,
        mesh=mesh,
        in_specs=placed,
        out_specs=(
            P(("dp", "col"), "row"),
            P(("dp", "col"), "row"),
            P("row"),
            P("row"),
            P(None, "row", "col"),
            P(None, "col"),
            P("col", "row"),
            P("row"),
            P("row"),
            P("row"),
            P("row", "col"),
            P("col"),
            P("col", "row"),
            P("row"),
        ),
        check_vma=False,
    )
```
